32 devices in a mesh: dp: 8 (over z, y), head: 4 (over x, core).
Axes of the slice: x: 2, y: 2, z: 4, core: 2. Of those that a mesh axis runs over, the one named last changes fastest.
Arguments:
- inputs: bfloat16 [16384, 1024], P(('dp', 'head')), may hold values from -6 to 6
- memory: bfloat16 [32, 512, 1024], P('dp'), may hold values from -6 to 6
- compressed: bfloat16 [32, 512, 1024], P('dp'), may hold values from -6 to 6
- slot_valid: int32 [32, 512], P('dp'), may hold values 0 or 1
- slot_age: int32 [32, 512], P('dp'), may hold values from 513 to 3584
- w_query: bfloat16 [1024, 1024], P('dp', 'head'), may hold values from -0.1875 to 0.1875
- w_key: bfloat16 [1024, 1024], P('dp', 'head'), may hold values from -0.1875 to 0.1875
- w_value: bfloat16 [1024, 1024], P('dp', 'head'), may hold values from -0.1875 to 0.1875
- content_bias: bfloat16 [1024], P(('dp', 'head')), may hold values from -3 to 3
- w_out: bfloat16 [1024, 1024], P(('dp', 'head')), may hold values from -2 to 2
- ln_gain: bfloat16 [1024], P(('dp', 'head')), may hold values from 0.5 to 1.5
- ln_bias: bfloat16 [1024], P(('dp', 'head')), may hold values from -2 to 2
- w_up: bfloat16 [1024, 4096], P('dp', 'head'), may hold values from -0.1875 to 0.1875
- up_bias: bfloat16 [4096], P(('dp', 'head')), may hold values from -3 to 3
- w_down: bfloat16 [4096, 1024], P('head', 'dp'), may hold values from -0.09375 to 0.09375
- down_bias: bfloat16 [1024], P(('dp', 'head')), may hold values from -3 to 3
- w_comp: bfloat16 [3, 1024, 1024], P(None, 'dp', 'head'), may hold values from -0.109375 to 0.109375
- comp_bias: bfloat16 [1024], P('head'), may hold values from -3 to 3
- cotangent: bfloat16 [16384, 1024], P(('dp', 'head')), may hold values from -6 to 6
Outputs:
- output: bfloat16 [16384, 1024], P(('dp', 'head'))
- grad_input: float32 [16384, 1024], P(('dp', 'head'))
- grad_query: float32 [1024, 1024], P('dp', 'head')
- grad_key: float32 [1024, 1024], P('dp', 'head')
- grad_value: float32 [1024, 1024], P('dp', 'head')
- grad_content_bias: float32 [1024], P(('dp', 'head'))
- grad_out: float32 [1024, 1024], P(('dp', 'head'))
- grad_ln_gain: float32 [1024], P(('dp', 'head'))
- grad_ln_bias: float32 [1024], P(('dp', 'head'))
- grad_up: float32 [1024, 4096], P('dp', 'head')
- grad_up_bias: float32 [4096], P(('dp', 'head'))
- grad_down: float32 [4096, 1024], P('head', 'dp')
- grad_down_bias: float32 [1024], P(('dp', 'head'))
- new_memory: bfloat16 [32, 512, 1024], P('dp')
- new_compressed: bfloat16 [32, 512, 1024], P('dp', None, 'head')
The draws below stay inside these ranges and needn't reach their ends.
All inputs are finite; a program needn't handle non-finite values. No bound on the sum of `slot_valid` on one device may be relied on, other than what follows from the above.
Results may differ from the reference program's by a relative error of at most 0.017.
Values may be sent and summed in bfloat16 or wider, within the bound.
No kernel may reach another device: no remote copies, remote signals or barrier semaphores. Data moves between devices by JAX's collectives and lax.ppermute only.
A program may use at most 192 MiB of HBM per device.

```python
import jax
import jax.numpy as jnp
from jax import lax

D = 1024
H = 8
HD = 128
FF = 4096
SEG = 512
CM = 512
RATE = 3
SEQ_DEV = 4
CC = 171
SEQS = 32
TOKENS = 16384
N_DP = 8


def with_ends(array, rng, low, high):
    spot = [jax.random.randint(jax.random.fold_in(rng, axis), (), 0, length) for axis, length in enumerate(array.shape)]
    main_axis = array.shape.index(max(array.shape))
    next_to = spot[:main_axis] + [(spot[main_axis] + 1) % array.shape[main_axis]] + spot[main_axis + 1:]
    return array.at[tuple(spot)].set(low).at[tuple(next_to)].set(high)


def raised(entries, own_key, source, target, shards_of, factor):
    def block_of(position):
        return (jnp.arange(entries.shape[position]) // (entries.shape[position] // shards_of)).reshape((-1,) + (1,) * (entries.ndim - 1 - position))

    one_side = jax.random.permutation(own_key, shards_of)[block_of(target)]
    second = (block_of(target) + shards_of // 2) % shards_of
    return jnp.where((block_of(source) == one_side) | (block_of(source) == second), factor * entries, entries)


def block_scale(key, extent, shards, smallest, high):
    level, own = 1.0, jax.random.fold_in(key, 6)
    for dim, blocks in shards:
        heights = jnp.exp(jax.random.uniform(jax.random.fold_in(own, dim), (blocks,), jnp.float32, smallest / len(shards), high / len(shards)))
        level = level * jnp.repeat(heights, extent[dim] // blocks).reshape([-1 if axis == dim else 1 for axis in range(len(extent))])
    return level


def centred(rng, dims, deviation, reach, cuts=(), kind=jnp.bfloat16):
    values = deviation * jax.random.normal(rng, dims, jnp.float32)
    if cuts:
        values = values * block_scale(rng, dims, cuts, -0.22, 0.18)
    return jnp.clip(values, -reach, reach).astype(kind)


def bell_draw_with(rng, dims, deviation, bound, split, heavy, kind=jnp.bfloat16):
    values = deviation * jax.random.normal(rng, dims, jnp.float32)
    if split:
        values = values * block_scale(rng, dims, split, -0.22, 0.18)
    return jnp.clip(raised(values, jax.random.fold_in(rng, 3), *heavy), -bound, bound).astype(kind)


def setup_inputs(seed: int = 0) -> dict:
    streams_of = jax.random.split(jax.random.key(seed), 20)
    inputs = bell_draw_with(streams_of[0], (TOKENS, D), 1.0, 6.0, ((0, 32),), (0, 1, 32, 2.75))
    memory = centred(streams_of[1], (SEQS, SEG, D), 1.0, 6.0, ((0, 8),))
    compressed = centred(streams_of[2], (SEQS, CM, D), 1.0, 6.0, ((0, 8),))
    slot_valid = with_ends((jax.random.randint(streams_of[3], (SEQS, CM), 0, 4) < 3).astype(jnp.int32), jax.random.fold_in(streams_of[3], 1), 0, 1)
    slot_age = with_ends(jax.random.randint(streams_of[4], (SEQS, CM), SEG + 1, SEG + 2 * RATE * CM + 1), jax.random.fold_in(streams_of[4], 1), SEG + 1, SEG + 2 * RATE * CM).astype(jnp.int32)
    w_query = centred(streams_of[5], (D, D), D ** -0.5, 0.1875, ((0, 8), (1, 4)))
    w_key = centred(streams_of[6], (D, D), D ** -0.5, 0.1875, ((0, 8), (1, 4)))
    w_value = centred(streams_of[7], (D, D), D ** -0.5, 0.1875, ((0, 8), (1, 4)))
    content_bias = centred(streams_of[8], (D,), 0.5, 3.0, ((0, 32),))
    w_out = centred(streams_of[9], (D, D), (D // 128) ** -0.5, 2.0, ((0, 32),))
    ln_gain = jnp.clip(1.0 + 0.1 * jax.random.normal(streams_of[10], (D,), jnp.float32), 0.5, 1.5).astype(jnp.bfloat16)
    ln_bias = centred(streams_of[11], (D,), 0.3, 2.0, ((0, 32),))
    w_up = centred(streams_of[12], (D, FF), D ** -0.5, 0.1875, ((0, 8), (1, 4)))
    up_bias = centred(streams_of[13], (FF,), 0.5, 3.0, ((0, 32),))
    w_down = centred(streams_of[14], (FF, D), FF ** -0.5, 0.09375, ((0, 4), (1, 8)))
    down_bias = centred(streams_of[15], (D,), 0.5, 3.0, ((0, 32),))
    w_comp = centred(streams_of[16], (RATE, D, D), (RATE * D) ** -0.5, 0.109375, ((1, 8), (2, 4)))
    comp_bias = centred(streams_of[17], (D,), 0.5, 3.0, ((0, 4),))
    cotangent = bell_draw_with(streams_of[18], (TOKENS, D), 1.0, 6.0, ((0, 32),), (0, 1, 32, 2.75))
    return dict(inputs=inputs, memory=memory, compressed=compressed, slot_valid=slot_valid, slot_age=slot_age, w_query=w_query, w_key=w_key, w_value=w_value, content_bias=content_bias, w_out=w_out, ln_gain=ln_gain, ln_bias=ln_bias, w_up=w_up, up_bias=up_bias, w_down=w_down, down_bias=down_bias, w_comp=w_comp, comp_bias=comp_bias, cotangent=cotangent)


@jax.custom_vjp
def low(v):
    return lax.optimization_barrier(v.astype(jnp.bfloat16)).astype(jnp.float32)

@jax.custom_vjp
def low_back(v):
    return v

def low_keep(v):
    return (low(v), None)

def low_pass(kept, grad):
    return (grad,)

def back_keep(v):
    return (v, None)

def back_low(kept, grad):
    return (low(grad),)
low.defvjp(low_keep, low_pass)
low_back.defvjp(back_keep, back_low)
highest = lax.Precision.HIGHEST
layer_eps = 1e-05

def head_slopes(first, number):
    return 0.6 * jnp.power(0.7, (first + jnp.arange(number)).astype(jnp.float32))

def score_terms(slopes, slot_mask, slot_dist):
    row_index = jnp.arange(SEG, dtype=jnp.int32)[:, None]
    col_index = jnp.arange(SEG, dtype=jnp.int32)[None, :]
    distance = jnp.concatenate([jnp.broadcast_to(row_index + slot_dist[None, :], (SEG, CM)), jnp.broadcast_to(row_index + SEG - col_index, (SEG, SEG)), jnp.broadcast_to(row_index - col_index, (SEG, SEG))], axis=1)
    allowed = jnp.concatenate([jnp.broadcast_to(slot_mask[None, :] > 0, (SEG, CM)), jnp.ones((SEG, SEG), dtype=jnp.bool_), row_index >= col_index], axis=1)
    log_decay = jnp.log1p(jnp.maximum(distance, 0).astype(jnp.float32))
    return (-slopes[:, None, None] * log_decay[None], allowed)

def attend(queries, key_part, value_part, slot_mask, slot_dist):
    pos_bias, allowed = score_terms(head_slopes(0, H), slot_mask, slot_dist)
    content = jnp.einsum('ihd,jhd->hij', queries, key_part, precision=highest)
    scores = low_back(content * HD ** (-0.5) + pos_bias)
    scores = jnp.where(allowed[None], scores, -1e+30)
    row_max = lax.optimization_barrier(jnp.max(scores, axis=-1, keepdims=True))
    weights = jnp.exp(scores - row_max)
    attn_probs = low(weights / lax.optimization_barrier(jnp.sum(weights, axis=-1, keepdims=True)))
    return jnp.einsum('hij,jhd->ihd', attn_probs, value_part, precision=highest)

def one_seq(pieces):
    return attend(*pieces)

def forward(params, tokens, memory_in, compressed_in, slot_mask, slot_dist):
    w_query, w_key, w_value, content_bias, w_out, ln_gain, ln_bias, w_up, up_bias, w_down, down_bias = params
    seq_count = tokens.shape[0]
    queries = low(low_back(jnp.dot(tokens, w_query, precision=highest) + content_bias))
    sources = jnp.concatenate([compressed_in, memory_in, tokens], axis=1)
    key_rows = low(low_back(jnp.dot(sources, w_key, precision=highest)))
    value_rows = low(low_back(jnp.dot(sources, w_value, precision=highest)))
    query_shape = (seq_count, SEG, H, HD)
    key_shape = (seq_count, CM + 2 * SEG, H, HD)
    mixed_out = lax.map(jax.checkpoint(one_seq), (queries.reshape(query_shape), key_rows.reshape(key_shape), value_rows.reshape(key_shape), slot_mask, slot_dist))
    mixed_out = low(low_back(mixed_out.reshape(seq_count, SEG, D)))
    attn_out = low_back(jnp.dot(mixed_out, w_out, precision=highest))
    residual = tokens + attn_out
    center = residual - lax.optimization_barrier(jnp.mean(residual, axis=-1, keepdims=True))
    normed = low(center * lax.rsqrt(lax.optimization_barrier(jnp.mean(center * center, axis=-1, keepdims=True)) + layer_eps) * ln_gain + ln_bias)
    before = low_back(jnp.dot(normed, w_up, precision=highest) + up_bias)
    hidden = low(jax.nn.gelu(before))
    return residual + jnp.dot(hidden, w_down, precision=highest) + down_bias

def compress(memory_in, comp_matrix, comp_shift):
    pad_rows = CC * RATE - SEG
    padded = jnp.pad(memory_in, ((0, 0), (0, pad_rows), (0, 0))).reshape(memory_in.shape[0], CC, RATE * D)
    return jnp.dot(padded, comp_matrix, precision=highest) + comp_shift

def widen(array_in):
    return array_in.astype(jnp.float32)

def reference(inputs, memory, compressed, slot_valid, slot_age, w_query, w_key, w_value, content_bias, w_out, ln_gain, ln_bias, w_up, up_bias, w_down, down_bias, w_comp, comp_bias, cotangent):
    params = jax.tree.map(widen, (w_query, w_key, w_value, content_bias, w_out, ln_gain, ln_bias, w_up, up_bias, w_down, down_bias))
    comp_matrix = w_comp.astype(jnp.float32).reshape(RATE * D, D)
    comp_shift = comp_bias.astype(jnp.float32)
    shaped = (N_DP, SEQ_DEV, SEG, D)
    token_blocks = inputs.astype(jnp.float32).reshape(shaped)
    memory_blocks = memory.astype(jnp.float32).reshape(shaped)
    compressed_blocks = compressed.astype(jnp.float32).reshape(N_DP, SEQ_DEV, CM, D)
    mask_blocks = slot_valid.reshape(N_DP, SEQ_DEV, CM)
    dist_blocks = slot_age.reshape(N_DP, SEQ_DEV, CM)
    upstream_blocks = cotangent.astype(jnp.float32).reshape(shaped)

    def one_block(totals, pieces):
        tokens, memory_in, compressed_in, slot_mask, slot_dist, upstream = pieces

        def layer_fn(weight_set, token_in):
            layer_out = forward(weight_set, token_in, memory_in, compressed_in, slot_mask, slot_dist)
            return (layer_out, compress(memory_in, comp_matrix, comp_shift))
        (result, squeezed), pullback = jax.vjp(layer_fn, params, tokens)
        weight_grads, token_grads = pullback((upstream, jnp.zeros_like(squeezed)))
        return (jax.tree.map(jnp.add, totals, weight_grads), (result.astype(jnp.bfloat16), token_grads, squeezed.astype(jnp.bfloat16)))
    zeros_init = jax.tree.map(jnp.zeros_like, params)
    totals, (results, token_grads, squeezed_all) = lax.scan(one_block, zeros_init, (token_blocks, memory_blocks, compressed_blocks, mask_blocks, dist_blocks, upstream_blocks))
    new_compressed = jnp.concatenate([compressed[:, CC:, :], squeezed_all.reshape(SEQS, CC, D)], axis=1)
    return (results.reshape(TOKENS, D), token_grads.reshape(TOKENS, D), totals[0], totals[1], totals[2], totals[3], totals[4], totals[5], totals[6], totals[7], totals[8], totals[9], totals[10], inputs.reshape(SEQS, SEG, D), new_compressed)
```

```python
import functools

import jax
import jax.numpy as jnp
from jax import lax
from jax.experimental import pallas as pl
from jax.experimental.pallas import tpu as pltpu
from jax.sharding import PartitionSpec as P

D = 1024
HD = 128
SEG = 512
CM = 512
RATE = 3
CC = 171
LN_EPS = 1e-05
LOG2E = 1.4426950408889634
SCALE2 = LOG2E * HD ** (-0.5)
FAR = 1e32
VMEM = 56 * 1024 * 1024
BF = jnp.bfloat16
F32 = jnp.float32


def nt(a, b):
    return lax.dot_general(a, b, (((1,), (1,)), ((), ())), preferred_element_type=F32)


def tn(a, b):
    return lax.dot_general(a, b, (((0,), (0,)), ((), ())), preferred_element_type=F32)


def nn(a, b):
    return jnp.dot(a, b, preferred_element_type=F32)


def x_swap(a):
    return lax.ppermute(a, "head", [(i, i ^ 2) for i in range(4)])


def c_swap(a):
    return lax.ppermute(a, "head", [(i, i ^ 1) for i in range(4)])


def fwd_kernel(slope_ref, q_ref, kv_ref, near_ref, far_ref, mixed_ref, lse_ref):
    a = pl.program_id(0)
    slope2 = slope_ref[a] * LOG2E
    q = q_ref[...]
    parts = []
    for n in range(3):
        k = kv_ref[n * SEG:(n + 1) * SEG, :HD]
        table = far_ref[...] if n == 0 else near_ref[(n - 1) * SEG:n * SEG, :]
        parts.append(nt(k, q) * SCALE2 - slope2 * table)
    top = jnp.maximum(jnp.maximum(jnp.max(parts[0], axis=0, keepdims=True), jnp.max(parts[1], axis=0, keepdims=True)),
                      jnp.max(parts[2], axis=0, keepdims=True))
    total = jnp.zeros((1, SEG), F32)
    acc = jnp.zeros((HD, SEG), F32)
    for n in range(3):
        p = jnp.exp2(parts[n] - top)
        total = total + jnp.sum(p, axis=0, keepdims=True)
        acc = acc + tn(kv_ref[n * SEG:(n + 1) * SEG, HD:], p.astype(BF))
    mixed_ref[...] = (acc / total).T.astype(BF)
    lse_ref[...] = (top + jnp.log2(total)).reshape(1, 1, SEG)


def bwd_kernel(slope_ref, q_ref, kv_ref, near_ref, far_ref, mixed_ref, lse_ref, do_ref, dq_ref, dkv_ref):
    a = pl.program_id(0)
    slope2 = slope_ref[a] * LOG2E
    q = q_ref[...]
    do = do_ref[...]
    lse = lse_ref[...].reshape(1, SEG)
    row_dot = jnp.sum((do.astype(F32) * mixed_ref[...].astype(F32)).T, axis=0, keepdims=True)
    inv_root = HD ** (-0.5)
    dq = jnp.zeros((HD, SEG), F32)
    for n in range(3):
        rows = slice(n * SEG, (n + 1) * SEG)
        k = kv_ref[rows, :HD]
        v = kv_ref[rows, HD:]
        table = far_ref[...] if n == 0 else near_ref[(n - 1) * SEG:n * SEG, :]
        p = jnp.exp2(nt(k, q) * SCALE2 - slope2 * table - lse)
        ds = (p * (nt(v, do) - row_dot)).astype(BF)
        dkv_ref[rows, HD:] = nn(p.astype(BF), do).astype(BF)
        dkv_ref[rows, :HD] = (nn(ds, q) * inv_root).astype(BF)
        dq = dq + tn(k, ds)
    dq_ref[...] = (dq.T * inv_root).astype(BF)


ROWS = 3 * SEG
PARAMS = pltpu.CompilerParams(vmem_limit_bytes=VMEM)
smem_spec = pl.BlockSpec(memory_space=pltpu.SMEM)
q_spec = pl.BlockSpec((SEG, HD), lambda a: (0, a))
kv_spec = pl.BlockSpec((ROWS, 2 * HD), lambda a: (0, a))
near_spec = pl.BlockSpec((2 * SEG, SEG), lambda a: (0, 0))
far_spec = pl.BlockSpec((SEG, SEG), lambda a: (0, 0))
lse_spec = pl.BlockSpec((1, 1, SEG), lambda a: (a, 0, 0))


def attend(slopes, q, kv, near, far):
    return pl.pallas_call(
        fwd_kernel,
        grid=(2,),
        in_specs=[smem_spec, q_spec, kv_spec, near_spec, far_spec],
        out_specs=[q_spec, lse_spec],
        out_shape=[jax.ShapeDtypeStruct((SEG, 2 * HD), BF), jax.ShapeDtypeStruct((2, 1, SEG), F32)],
        compiler_params=PARAMS,
        cost_estimate=pl.CostEstimate(flops=2 * 4 * SEG * ROWS * HD, bytes_accessed=6 << 20, transcendentals=2 * SEG * ROWS),
    )(slopes, q, kv, near, far)


def attend_back(slopes, q, kv, near, far, mixed, lse, do):
    return pl.pallas_call(
        bwd_kernel,
        grid=(2,),
        in_specs=[smem_spec, q_spec, kv_spec, near_spec, far_spec, q_spec, lse_spec, q_spec],
        out_specs=[q_spec, kv_spec],
        out_shape=[jax.ShapeDtypeStruct((SEG, 2 * HD), BF), jax.ShapeDtypeStruct((ROWS, 4 * HD), BF)],
        compiler_params=PARAMS,
        cost_estimate=pl.CostEstimate(flops=2 * 10 * SEG * ROWS * HD, bytes_accessed=8 << 20, transcendentals=2 * SEG * ROWS),
    )(slopes, q, kv, near, far, mixed, lse, do)


def gelu_pair(before):
    c0, c1 = 0.7978845608028654, 0.044715
    sq = before * before
    t = jnp.tanh(c0 * before * (1.0 + c1 * sq))
    half = 0.5 * (1.0 + t)
    return before * half, half + 0.5 * before * (1.0 - t * t) * (c0 * (1.0 + 3.0 * c1 * sq))


def butterfly(a, n_dp):
    a = a + c_swap(a)
    a = a + x_swap(a)
    step = 1
    while step < n_dp:
        a = a + lax.ppermute(a, "dp", [(i, i ^ step) for i in range(n_dp)])
        step *= 2
    return a


def per_device(
    inputs,
    memory,
    compressed,
    slot_valid,
    slot_age,
    w_query,
    w_key,
    w_value,
    content_bias,
    w_out,
    ln_gain,
    ln_bias,
    w_up,
    up_bias,
    w_down,
    down_bias,
    w_comp,
    comp_bias,
    cotangent,
):
    n_dp = lax.axis_size("dp")
    d = lax.axis_index("dp")
    h = lax.axis_index("head")
    seqs = memory.shape[0]
    kw = w_key.shape[0]

    pack = jnp.concatenate(
        [w_key[:, :HD], w_value[:, :HD], w_key[:, HD:], w_value[:, HD:], w_query], axis=1
    )
    w_own = lax.all_gather(pack, "dp", axis=0, tiled=True)
    inputs_x = x_swap(inputs)
    w_par = c_swap(w_own)
    small = jnp.concatenate([content_bias, ln_gain, ln_bias, down_bias, up_bias]).reshape(1, -1)
    small = lax.all_gather(small, ("dp", "head"), axis=0, tiled=True).astype(F32)
    out_rows = w_out.shape[0]
    wo = lax.all_gather(w_out, "dp", axis=0, tiled=True)
    wo2 = jnp.stack([wo, c_swap(wo)])
    wo4 = jnp.concatenate([wo2, x_swap(wo2)]).reshape(4, n_dp, out_rows, D)
    w_o = jnp.take(wo4, h ^ jnp.arange(4), axis=0).transpose(1, 0, 2, 3).reshape(4, D // 4, D)
    w_o = jnp.take(w_o, h ^ jnp.arange(4), axis=0).reshape(D, D)
    cot_x = x_swap(cotangent)
    up_own = lax.all_gather(w_up, "dp", axis=0, tiled=True)
    down_own = lax.all_gather(w_down.T, "dp", axis=0, tiled=True)
    up_par = c_swap(up_own)
    down_par = c_swap(down_own)
    comp_w = lax.all_gather(w_comp, "dp", axis=1, tiled=True)

    other = c_swap(jnp.stack([inputs, inputs_x]))
    four = jnp.concatenate([jnp.stack([inputs, inputs_x]), other])
    rank = jnp.arange(4)
    new_memory = jnp.take(four, ((rank ^ h) >> 1) | (((rank ^ h) & 1) << 1), axis=0)

    share = content_bias.shape[0]
    bias_all = small[:, :share].reshape(4, 2 * HD)
    gain = small[:, share:2 * share].reshape(1, D)
    shift = small[:, 2 * share:3 * share].reshape(1, D)
    down_shift = small[:, 3 * share:4 * share].reshape(1, D)
    up_shift = small[:, 4 * share:].reshape(4, D)

    i = jnp.arange(SEG, dtype=jnp.int32)[None, :]
    j = jnp.arange(2 * SEG, dtype=jnp.int32)[:, None]
    gap = i + SEG - j
    near = jnp.where(gap >= 0, jnp.log1p(jnp.maximum(gap, 0).astype(F32)), FAR)

    def far_of(s):
        age = lax.dynamic_index_in_dim(slot_age, s, 0, keepdims=False)[:, None]
        valid = lax.dynamic_index_in_dim(slot_valid, s, 0, keepdims=False)[:, None]
        return jnp.where(valid > 0, jnp.log1p(jnp.maximum(i + age, 0).astype(F32)), FAR)

    groups = (h, h ^ 1)
    slopes = [0.6 * jnp.power(0.7, (2 * g + jnp.arange(2)).astype(F32)) for g in groups]
    weights = (w_own, w_par)
    seq_ids = (h, h ^ 2)
    tokens = (inputs, inputs_x)
    far = [far_of(s) for s in seq_ids]
    sources = [
        jnp.concatenate(
            [lax.dynamic_index_in_dim(compressed, s, 0, keepdims=False),
             lax.dynamic_index_in_dim(memory, s, 0, keepdims=False), t], axis=0)
        for s, t in zip(seq_ids, tokens)
    ]

    q, kv, mixed, lse = {}, {}, {}, {}
    for t in (1, 0):
        for g in (0, 1):
            bias = lax.dynamic_index_in_dim(bias_all, groups[g], 0, keepdims=True)
            q[t, g] = (nn(tokens[t], weights[g][:, 4 * HD:]) + bias).astype(BF)
            kv[t, g] = nn(sources[t], weights[g][:, :4 * HD]).astype(BF)
            mixed[t, g], lse[t, g] = attend(slopes[g], q[t, g], kv[t, g], near, far[t])
    sent = x_swap(jnp.concatenate([mixed[1, 0], mixed[1, 1]], axis=1))
    mixed_rows = jnp.concatenate([mixed[0, 0], mixed[0, 1], sent], axis=1)
    residual = inputs.astype(F32) + nn(mixed_rows, w_o)
    center = residual - jnp.mean(residual, axis=-1, keepdims=True)
    rstd = lax.rsqrt(jnp.mean(center * center, axis=-1, keepdims=True) + LN_EPS)
    normed = (center * rstd * gain + shift).astype(BF)
    normed_x = x_swap(normed)

    ups, downs = (up_own, up_par), (down_own, down_par)
    norm2, cot2 = (normed, normed_x), (cotangent, cot_x)
    hidden, grad_b, branch, grad_n = {}, {}, {}, {}
    for t in (0, 1):
        for g in (0, 1):
            shift_g = lax.dynamic_index_in_dim(up_shift, groups[g], 0, keepdims=True)
            before = nn(norm2[t], ups[g]) + shift_g
            act, slope = gelu_pair(before)
            hidden[t, g] = act.astype(BF)
            grad_b[t, g] = (nn(cot2[t], downs[g]) * slope).astype(BF)
        grad_n[t] = nt(grad_b[t, 0], ups[0]) + nt(grad_b[t, 1], ups[1])
        branch[t] = nt(hidden[t, 0], downs[0]) + nt(hidden[t, 1], downs[1])
    grad_n_x = x_swap(grad_n[1].astype(BF))
    branch_x = x_swap(branch[1].astype(BF))
    grad_normed = grad_n[0] + grad_n_x.astype(F32)
    output = (residual + branch[0] + branch_x.astype(F32) + down_shift).astype(BF)

    g_up = [tn(normed, grad_b[0, g]) + tn(normed_x, grad_b[1, g]) for g in (0, 1)]
    g_down = [tn(cotangent, hidden[0, g]) + tn(cot_x, hidden[1, g]) for g in (0, 1)]
    g_up_sum = (g_up[0] + c_swap(g_up[1].astype(BF)).astype(F32)).astype(BF)
    g_down_sum = (g_down[0] + c_swap(g_down[1].astype(BF)).astype(F32)).astype(BF)
    grad_up = lax.psum_scatter(g_up_sum, "dp", scatter_dimension=0, tiled=True).astype(F32)
    grad_down = lax.psum_scatter(g_down_sum, "dp", scatter_dimension=0, tiled=True).astype(F32).T
    up_cols = [jnp.sum(grad_b[0, g].astype(F32), axis=0) + jnp.sum(grad_b[1, g].astype(F32), axis=0) for g in (0, 1)]

    xhat = center * rstd
    g = grad_normed * gain
    upstream = cotangent.astype(F32)
    grad_residual = upstream + rstd * (
        g - jnp.mean(g, axis=-1, keepdims=True) - xhat * jnp.mean(g * xhat, axis=-1, keepdims=True)
    )
    attn_grad = grad_residual.astype(BF)
    grad_mixed = nt(attn_grad, w_o).astype(BF)
    half = D // 2
    got = x_swap(grad_mixed[:, half:])
    g_out = tn(mixed_rows, attn_grad).astype(BF).reshape(4, D // 4, D)
    g_out = jnp.take(g_out, h ^ jnp.arange(4), axis=0).reshape(n_dp, 2, 2, out_rows, D)
    cc, xx = h % 2, h // 2
    pick = lambda a, n, axis: lax.dynamic_index_in_dim(a, n, axis, keepdims=False)
    g_out = (pick(g_out, cc, 2).astype(F32) + c_swap(pick(g_out, 1 - cc, 2)).astype(F32)).astype(BF)
    g_out = (pick(g_out, xx, 1).astype(F32) + x_swap(pick(g_out, 1 - xx, 1)).astype(F32)).astype(BF)
    grad_out = lax.psum_scatter(g_out.reshape(n_dp * out_rows, D), "dp", scatter_dimension=0, tiled=True).astype(F32)

    do = {(0, 0): grad_mixed[:, :2 * HD], (0, 1): grad_mixed[:, 2 * HD:half],
          (1, 0): got[:, :2 * HD], (1, 1): got[:, 2 * HD:]}
    dq, dkv = {}, {}
    term = {}
    for t in (0, 1):
        for g in (0, 1):
            dq[t, g], dkv[t, g] = attend_back(
                slopes[g], q[t, g], kv[t, g], near, far[t], mixed[t, g], lse[t, g], do[t, g])
        term[t] = sum(nt(dkv[t, g][2 * SEG:], weights[g][:, :4 * HD]) + nt(dq[t, g], weights[g][:, 4 * HD:]) for g in (0, 1))
    term_x = x_swap(term[1].astype(BF))
    grad_input = grad_residual + term[0] + term_x.astype(F32)
    g_w = []
    for g in (0, 1):
        g_kv = tn(sources[0], dkv[0, g]) + tn(sources[1], dkv[1, g])
        g_q = tn(inputs, dq[0, g]) + tn(inputs_x, dq[1, g])
        g_w.append((g_kv, g_q))
    from_par = c_swap(jnp.concatenate([g_w[1][0].astype(BF), g_w[1][1].astype(BF)], axis=1))
    g_sum = jnp.concatenate(
        [(g_w[0][0] + from_par[:, :4 * HD].astype(F32)).astype(BF),
         (g_w[0][1] + from_par[:, 4 * HD:].astype(F32)).astype(BF)], axis=1)
    g_sum = lax.psum_scatter(g_sum, "dp", scatter_dimension=0, tiled=True).astype(F32)
    grad_key = jnp.concatenate([g_sum[:, :HD], g_sum[:, 2 * HD:3 * HD]], axis=1)
    grad_value = jnp.concatenate([g_sum[:, HD:2 * HD], g_sum[:, 3 * HD:4 * HD]], axis=1)
    grad_query = g_sum[:, 4 * HD:]

    lane = jnp.arange(4)[:, None]
    place = lambda parts: jnp.where(lane == groups[0], parts[0][None], 0.0) + jnp.where(lane == groups[1], parts[1][None], 0.0)
    bias_cols = [jnp.sum(dq[0, g].astype(F32), axis=0) + jnp.sum(dq[1, g].astype(F32), axis=0) for g in (0, 1)]
    early = jnp.concatenate([
        jnp.sum(grad_normed * xhat, axis=0).reshape(-1, share),
        jnp.sum(grad_normed, axis=0).reshape(-1, share),
        jnp.sum(upstream, axis=0).reshape(-1, share),
        place(up_cols).reshape(-1, up_bias.shape[0]),
    ], axis=1)
    early = pick(butterfly(early, n_dp), d * 4 + h, 0)
    late = pick(butterfly(place(bias_cols).reshape(-1, share), n_dp), d * 4 + h, 0)

    width = comp_w.shape[2]
    padded = jnp.pad(memory, ((0, 0), (0, CC * RATE - SEG), (0, 0))).reshape(seqs, CC, RATE * D)
    squeezed = nn(padded, comp_w.reshape(RATE * D, width)) + comp_bias.astype(F32)
    kept = lax.dynamic_slice_in_dim(compressed[:, CC:, :], h * width, width, 2)
    new_compressed = jnp.concatenate([kept, squeezed.astype(BF)], axis=1)

    return (
        output,
        grad_input,
        grad_query,
        grad_key,
        grad_value,
        late,
        grad_out,
        early[:share],
        early[share:2 * share],
        grad_up,
        early[3 * share:],
        grad_down,
        early[2 * share:3 * share],
        new_memory,
        new_compressed,
    )


def solution(mesh):
    both = ("dp", "head")
    in_specs = (
        P(both, None),
        P("dp", None, None),
        P("dp", None, None),
        P("dp", None),
        P("dp", None),
        P("dp", "head"),
        P("dp", "head"),
        P("dp", "head"),
        P(both),
        P(both, None),
        P(both),
        P(both),
        P("dp", "head"),
        P(both),
        P("head", "dp"),
        P(both),
        P(None, "dp", "head"),
        P("head"),
        P(both, None),
    )
    out_specs = (
        P(both, None),
        P(both, None),
        P("dp", "head"),
        P("dp", "head"),
        P("dp", "head"),
        P(both),
        P(both, None),
        P(both),
        P(both),
        P("dp", "head"),
        P(both),
        P("head", "dp"),
        P(both),
        P("dp", None, None),
        P("dp", None, "head"),
    )
    return jax.shard_map(per_device, mesh=mesh, in_specs=in_specs, out_specs=out_specs, check_vma=False)
```

```python
import jax
import jax.numpy as jnp
from jax import lax
from jax.experimental import pallas as pl
from jax.experimental.pallas import tpu as pltpu
from jax.sharding import PartitionSpec as P

D = 1024
HD = 128
SEG = 512
CM = 512
RATE = 3
CC = 171
LN_EPS = 1e-05
LOG2E = 1.4426950408889634
SCALE2 = LOG2E * HD ** (-0.5)
FAR = 1e32
VMEM = 56 * 1024 * 1024
BF = jnp.bfloat16
F32 = jnp.float32


def nt(a, b):
    return lax.dot_general(a, b, (((1,), (1,)), ((), ())), preferred_element_type=F32)


def tn(a, b):
    return lax.dot_general(a, b, (((0,), (0,)), ((), ())), preferred_element_type=F32)


def nn(a, b):
    return jnp.dot(a, b, preferred_element_type=F32)


def x_swap(a):
    return lax.ppermute(a, "head", [(i, i ^ 2) for i in range(4)])


def c_swap(a):
    return lax.ppermute(a, "head", [(i, i ^ 1) for i in range(4)])


def fwd_kernel(slope_ref, q_ref, kv_ref, near_ref, far_ref, mixed_ref, lse_ref):
    a = pl.program_id(0)
    slope2 = slope_ref[a] * LOG2E
    q = q_ref[0]
    parts = []
    for n in range(3):
        k = kv_ref[0, n * SEG:(n + 1) * SEG, :HD]
        table = far_ref[...] if n == 0 else near_ref[(n - 1) * SEG:n * SEG, :]
        parts.append(nt(k, q) * SCALE2 - slope2 * table)
    top = jnp.maximum(jnp.maximum(jnp.max(parts[0], axis=0, keepdims=True), jnp.max(parts[1], axis=0, keepdims=True)),
                      jnp.max(parts[2], axis=0, keepdims=True))
    total = jnp.zeros((1, SEG), F32)
    acc = jnp.zeros((HD, SEG), F32)
    for n in range(3):
        p = jnp.exp2(parts[n] - top)
        total = total + jnp.sum(p, axis=0, keepdims=True)
        acc = acc + tn(kv_ref[0, n * SEG:(n + 1) * SEG, HD:], p.astype(BF))
    mixed_ref[...] = (acc / total).T.astype(BF)
    lse_ref[...] = (top + jnp.log2(total)).reshape(1, 1, SEG)


def bwd_kernel(slope_ref, q_ref, kv_ref, near_ref, far_ref, mixed_ref, lse_ref, do_ref, dq_ref, dkv_ref, sum_ref):
    a = pl.program_id(0)
    slope2 = slope_ref[a] * LOG2E
    q = q_ref[0]
    do = do_ref[...]
    lse = lse_ref[...].reshape(1, SEG)
    row_dot = jnp.sum((do.astype(F32) * mixed_ref[...].astype(F32)).T, axis=0, keepdims=True)
    inv_root = HD ** (-0.5)
    dq = jnp.zeros((HD, SEG), F32)
    for n in range(3):
        rows = slice(n * SEG, (n + 1) * SEG)
        k = kv_ref[0, rows, :HD]
        v = kv_ref[0, rows, HD:]
        table = far_ref[...] if n == 0 else near_ref[(n - 1) * SEG:n * SEG, :]
        p = jnp.exp2(nt(k, q) * SCALE2 - slope2 * table - lse)
        ds = (p * (nt(v, do) - row_dot)).astype(BF)
        dkv_ref[rows, HD:] = nn(p.astype(BF), do).astype(BF)
        dkv_ref[rows, :HD] = (nn(ds, q) * inv_root).astype(BF)
        dq = dq + tn(k, ds)
    dq = (dq.T * inv_root).astype(BF)
    dq_ref[...] = dq
    sum_ref[...] = jnp.sum(dq.astype(F32), axis=0, keepdims=True)


def ring_order(n):
    up = list(range(0, n, 2))
    return up + [p + 1 for p in reversed(up)]


def ring_perms(n):
    order = ring_order(n)
    ahead = [(order[p], order[(p + 1) % n]) for p in range(n)]
    return ahead, [(b, a) for a, b in ahead]


def ring_place(d, n):
    return jnp.where(d % 2 == 0, d // 2, n - 1 - d // 2)


def ring_member(p, n):
    p = p % n
    return jnp.where(p < n // 2, 2 * p, 2 * (n - 1 - p) + 1)


def ring_gather(chunk, n):
    ahead, back = ring_perms(n)
    out, f, b = [chunk], chunk, chunk
    for k in range(1, n // 2 + 1):
        f = lax.ppermute(f, "dp", ahead)
        out.append(f)
        if k < n - n // 2:
            b = lax.ppermute(b, "dp", back)
            out.append(b)
    return out


def ring_sources(d, n):
    place = ring_place(d, n)
    steps = [0]
    for k in range(1, n // 2 + 1):
        steps.append(-k)
        if k < n - n // 2:
            steps.append(k)
    return ring_member(place + jnp.array(steps, jnp.int32), n).astype(jnp.int32)


def ring_scatter(array, d, n):
    ahead, back = ring_perms(n)
    place = ring_place(d, n)

    def block(p):
        return lax.dynamic_index_in_dim(array, ring_member(p, n), 0, keepdims=False).astype(F32)

    up, down = n // 2, n - n // 2 - 1
    f, b = block(place + up).astype(BF), block(place - down).astype(BF)
    for k in range(1, up + 1):
        f = lax.ppermute(f, "dp", ahead)
        if k < up:
            f = (f.astype(F32) + block(place + up - k)).astype(BF)
        if k <= down:
            b = lax.ppermute(b, "dp", back)
            if k < down:
                b = (b.astype(F32) + block(place - down + k)).astype(BF)
    return f.astype(F32) + b.astype(F32) + block(place)


ROWS = 3 * SEG
HALF = D // 2
smem_spec = pl.BlockSpec(memory_space=pltpu.SMEM)
vmem_spec = pl.BlockSpec(memory_space=pltpu.VMEM)
any_spec = pl.BlockSpec(memory_space=pl.ANY)


def params():
    return pltpu.CompilerParams(vmem_limit_bytes=VMEM)


def cost(us):
    return pl.CostEstimate(flops=int(us * 1.1e9), bytes_accessed=1 << 20, transcendentals=0)


def shape(*dims, kind=BF):
    return jax.ShapeDtypeStruct(dims, kind)


def whole(*dims):
    return pl.BlockSpec(dims, lambda *i: (0,) * len(dims))


def attend(t, slopes, q, kv, near, far):
    return pl.pallas_call(
        fwd_kernel,
        grid=(4,),
        in_specs=[
            smem_spec,
            pl.BlockSpec((1, SEG, HD), lambda a: (t, 0, a)),
            pl.BlockSpec((1, ROWS, 2 * HD), lambda a: (t, 0, a)),
            whole(2 * SEG, SEG),
            whole(SEG, SEG),
        ],
        out_specs=[pl.BlockSpec((SEG, HD), lambda a: (0, a)), pl.BlockSpec((1, 1, SEG), lambda a: (a, 0, 0))],
        out_shape=[shape(SEG, HALF), shape(4, 1, SEG, kind=F32)],
        compiler_params=params(),
        cost_estimate=cost(12),
    )(slopes, q, kv, near, far)


def attend_back(t, slopes, q, kv, near, far, mixed, lse, do):
    column = pl.BlockSpec((SEG, HD), lambda a: (0, a))
    return pl.pallas_call(
        bwd_kernel,
        grid=(4,),
        in_specs=[
            smem_spec,
            pl.BlockSpec((1, SEG, HD), lambda a: (t, 0, a)),
            pl.BlockSpec((1, ROWS, 2 * HD), lambda a: (t, 0, a)),
            whole(2 * SEG, SEG),
            whole(SEG, SEG),
            column,
            pl.BlockSpec((1, 1, SEG), lambda a: (a, 0, 0)),
            column,
        ],
        out_specs=[column, pl.BlockSpec((ROWS, 2 * HD), lambda a: (0, a)), pl.BlockSpec((1, HD), lambda a: (0, a))],
        out_shape=[shape(SEG, HALF), shape(ROWS, D), shape(1, HALF, kind=F32)],
        compiler_params=params(),
        cost_estimate=cost(16),
    )(slopes, q, kv, near, far, mixed, lse, do)


def project_kernel(ids_ref, comp_ref, mem_ref, own_ref, other_ref, w_own_ref, w_par_ref, bias_ref, kv_ref, q_ref):
    t, n = pl.program_id(0), pl.program_id(1)

    def put(source):
        kv_ref[0, :, :HALF] = nn(source, w_own_ref[:, :HALF]).astype(BF)
        kv_ref[0, :, HALF:] = nn(source, w_par_ref[:, :HALF]).astype(BF)

    def ask(source):
        put(source)
        q_ref[0, :, :2 * HD] = (nn(source, w_own_ref[:, HALF:]) + bias_ref[:, :2 * HD]).astype(BF)
        q_ref[0, :, 2 * HD:] = (nn(source, w_par_ref[:, HALF:]) + bias_ref[:, 2 * HD:]).astype(BF)

    pl.when(n == 0)(lambda: put(comp_ref[0]))
    pl.when(n == 1)(lambda: put(mem_ref[0]))
    pl.when((n == 2) & (t == 0))(lambda: ask(own_ref[...]))
    pl.when((n == 2) & (t == 1))(lambda: ask(other_ref[...]))


def project(ids, compressed, memory, own, other, w_own, w_par, bias):
    return pl.pallas_call(
        project_kernel,
        grid_spec=pltpu.PrefetchScalarGridSpec(
            num_scalar_prefetch=1,
            grid=(2, 3),
            in_specs=[
                pl.BlockSpec((1, CM, D), lambda t, n, ids: (ids[t], 0, 0)),
                pl.BlockSpec((1, SEG, D), lambda t, n, ids: (ids[t], 0, 0)),
                whole(SEG, D),
                whole(SEG, D),
                whole(D, 3 * 2 * HD),
                whole(D, 3 * 2 * HD),
                whole(1, HALF),
            ],
            out_specs=[
                pl.BlockSpec((1, SEG, D), lambda t, n, ids: (t, n, 0)),
                pl.BlockSpec((1, SEG, HALF), lambda t, n, ids: (t, 0, 0)),
            ],
        ),
        out_shape=[shape(2, ROWS, D), shape(2, SEG, HALF)],
        compiler_params=params(),
        cost_estimate=cost(12),
    )(ids, compressed, memory, own, other, w_own, w_par, bias)


def norm_kernel(mixed_ref, sent_ref, w_ref, in_ref, gain_ref, shift_ref, residual_ref, normed_ref):
    out = nn(mixed_ref[...], w_ref[:HALF]) + nn(sent_ref[...], w_ref[HALF:])
    residual = in_ref[...].astype(F32) + out
    residual_ref[...] = residual
    center = residual - jnp.mean(residual, axis=-1, keepdims=True)
    rstd = lax.rsqrt(jnp.mean(center * center, axis=-1, keepdims=True) + LN_EPS)
    normed_ref[...] = (center * rstd * gain_ref[...] + shift_ref[...]).astype(BF)


def attention_out(mixed, sent, w_o, inputs, gain, shift):
    rows = SEG // 2
    half = pl.BlockSpec((rows, HALF), lambda i: (i, 0))
    full = pl.BlockSpec((rows, D), lambda i: (i, 0))
    return pl.pallas_call(
        norm_kernel,
        grid=(2,),
        in_specs=[half, half, whole(D, D), full, whole(1, D), whole(1, D)],
        out_specs=[full, full],
        out_shape=[shape(SEG, D, kind=F32), shape(SEG, D)],
        compiler_params=params(),
        cost_estimate=cost(4),
    )(mixed, sent, w_o, inputs, gain, shift)


def gelu_pair(before):
    c0, c1 = 0.7978845608028654, 0.044715
    sq = before * before
    t = jnp.tanh(c0 * before * (1.0 + c1 * sq))
    half = 0.5 * (1.0 + t)
    return before * half, half + 0.5 * before * (1.0 - t * t) * (c0 * (1.0 + 3.0 * c1 * sq))


def ffn_kernel(norm_ref, cot_ref, bias_ref, up0, down0, up1, down1, hid_ref, gb_ref, sum_ref, branch_ref, gn_ref, branch, gn):
    i, n = pl.program_id(0), pl.num_programs(0)

    def body(up, down, first):
        before = nn(norm_ref[...], up[...]) + bias_ref[...]
        act, slope = gelu_pair(before)
        act = act.astype(BF)
        gb = (nn(cot_ref[...], down[...]) * slope).astype(BF)
        hid_ref[...] = act
        gb_ref[...] = gb
        sum_ref[...] = jnp.sum(gb.astype(F32), axis=0, keepdims=True)
        if first:
            branch[...] = nt(act, down[...])
            gn[...] = nt(gb, up[...])
        else:
            branch[...] += nt(act, down[...])
            gn[...] += nt(gb, up[...])

    pl.when(i == 0)(lambda: body(up0, down0, True))
    pl.when((i > 0) & (i < n // 2))(lambda: body(up0, down0, False))
    pl.when(i >= n // 2)(lambda: body(up1, down1, False))

    @pl.when(i == n - 1)
    def _():
        branch_ref[...] = branch[...].astype(branch_ref.dtype)
        gn_ref[...] = gn[...].astype(gn_ref.dtype)


def feed_forward(norm, cot, bias, w_own, w_par, kind, tile=512):
    n = D // tile
    low = lambda i: jnp.minimum(i, n - 1)
    high = lambda i: jnp.maximum(i - n, 0)
    part = pl.BlockSpec((SEG, tile), lambda i: (0, i))
    return pl.pallas_call(
        ffn_kernel,
        grid=(2 * n,),
        in_specs=[
            whole(SEG, D),
            whole(SEG, D),
            pl.BlockSpec((1, tile), lambda i: (0, i)),
            pl.BlockSpec((D, tile), lambda i: (0, low(i))),
            pl.BlockSpec((D, tile), lambda i: (1, low(i))),
            pl.BlockSpec((D, tile), lambda i: (0, high(i))),
            pl.BlockSpec((D, tile), lambda i: (1, high(i))),
        ],
        out_specs=[part, part, pl.BlockSpec((1, tile), lambda i: (0, i)), whole(SEG, D), whole(SEG, D)],
        out_shape=[shape(SEG, 2 * D), shape(SEG, 2 * D), shape(1, 2 * D, kind=F32), shape(SEG, D, kind=kind), shape(SEG, D, kind=kind)],
        scratch_shapes=[pltpu.VMEM((SEG, D), F32)] * 2,
        compiler_params=params(),
        cost_estimate=cost(16),
    )(norm, cot, bias, w_own, w_own, w_par, w_par)


def ffn_grad_kernel(n0, n1, c0, c1, gb0, gb1, hid0, hid1, *rest):
    out_ref = rest[-1]

    def put(total):
        total = total.reshape(out_ref.shape[0], out_ref.shape[2], -1)
        if len(rest) > 1:
            total = total + rest[0][:, 0].astype(F32)
        out_ref[:, 0] = total.astype(BF)

    m = pl.program_id(0)
    pl.when(m == 0)(lambda: put(tn(n0[...], gb0[...]) + tn(n1[...], gb1[...])))
    pl.when(m == 1)(lambda: put(tn(c0[...], hid0[...]) + tn(c1[...], hid1[...])))


def ffn_grads(g, n_dp, norms, cots, gbs, hids, *received, tile=512):
    n = D // tile
    tokens = whole(SEG, D)
    early = pl.BlockSpec((SEG, tile), lambda m, i: (0, g * n + jnp.where(m == 0, i, n - 1)))
    late = pl.BlockSpec((SEG, tile), lambda m, i: (0, g * n + jnp.where(m == 0, 0, i)))
    block = pl.BlockSpec((n_dp, 1, D // n_dp, tile), lambda m, i: (0, m, 0, i))
    return pl.pallas_call(
        ffn_grad_kernel,
        grid=(2, n),
        in_specs=[tokens] * 4 + [early] * 2 + [late] * 2 + [block] * len(received),
        out_specs=block,
        out_shape=shape(n_dp, 2, D // n_dp, D),
        compiler_params=params(),
        cost_estimate=cost(7),
    )(*norms, *cots, *gbs, *hids, *received)


def norm_back_kernel(h_ref, residual_ref, gn_ref, gnx_ref, cot_ref, gain_ref, mixed_ref, sent_ref, w_ref,
                     grad_ref, keep_ref, send_ref, sums_ref, out_ref, acc):
    i = pl.program_id(0)
    residual = residual_ref[...]
    center = residual - jnp.mean(residual, axis=-1, keepdims=True)
    rstd = lax.rsqrt(jnp.mean(center * center, axis=-1, keepdims=True) + LN_EPS)
    xhat = center * rstd
    gn = gn_ref[...] + gnx_ref[...].astype(F32)
    g = gn * gain_ref[...]
    cot = cot_ref[...].astype(F32)
    grad = cot + rstd * (g - jnp.mean(g, axis=-1, keepdims=True) - xhat * jnp.mean(g * xhat, axis=-1, keepdims=True))
    grad_ref[...] = grad
    low = grad.astype(BF)
    keep_ref[...] = nt(low, w_ref[:HALF]).astype(BF)
    send_ref[...] = nt(low, w_ref[HALF:]).astype(BF)
    total = lambda a: jnp.sum(a, axis=0, keepdims=True)
    sums = jnp.concatenate([total(gn * xhat), total(gn), total(cot)], axis=0)

    @pl.when(i == 0)
    def _():
        sums_ref[...] = sums
        acc[:HALF] = tn(mixed_ref[...], low)
        acc[HALF:] = tn(sent_ref[...], low)

    @pl.when(i > 0)
    def _():
        sums_ref[...] += sums
        acc[:HALF] += tn(mixed_ref[...], low)
        acc[HALF:] += tn(sent_ref[...], low)

    @pl.when(i == pl.num_programs(0) - 1)
    def _():
        for b in range(4):
            out_ref[h_ref[0] ^ b] = acc[b * 2 * HD:(b + 1) * 2 * HD].astype(BF)


def norm_back(h, residual, gn, gnx, cot, gain, mixed, sent, w_o):
    rows = SEG // 2
    half = pl.BlockSpec((rows, HALF), lambda i: (i, 0))
    full = pl.BlockSpec((rows, D), lambda i: (i, 0))
    return pl.pallas_call(
        norm_back_kernel,
        grid=(2,),
        in_specs=[smem_spec, full, full, full, full, whole(1, D), half, half, whole(D, D)],
        out_specs=[full, half, half, whole(3, D), whole(4, 2 * HD, D)],
        out_shape=[shape(SEG, D, kind=F32), shape(SEG, HALF), shape(SEG, HALF), shape(3, D, kind=F32), shape(4, 2 * HD, D)],
        scratch_shapes=[pltpu.VMEM((D, D), F32)],
        compiler_params=params(),
        cost_estimate=cost(7),
    )(h, residual, gn, gnx, cot, gain, mixed, sent, w_o)


def term_kernel(dq_ref, dkv_ref, w_own_ref, w_par_ref, *rest):
    out = nt(dkv_ref[:, :HALF], w_own_ref[:, :HALF]) + nt(dkv_ref[:, HALF:], w_par_ref[:, :HALF])
    out = out + nt(dq_ref[:, :2 * HD], w_own_ref[:, HALF:]) + nt(dq_ref[:, 2 * HD:], w_par_ref[:, HALF:])
    if len(rest) > 1:
        out = out + rest[0][...]
    rest[-1][...] = out.astype(rest[-1].dtype)


def token_term(dq, dkv, w_own, w_par, *residual):
    rows = SEG // 2
    full = pl.BlockSpec((rows, D), lambda i: (i, 0))
    weight = whole(D, 3 * 2 * HD)
    return pl.pallas_call(
        term_kernel,
        grid=(2,),
        in_specs=[
            pl.BlockSpec((rows, HALF), lambda i: (i, 0)),
            pl.BlockSpec((rows, D), lambda i: (4 + i, 0)),
            weight,
            weight,
        ] + [full] * len(residual),
        out_specs=full,
        out_shape=shape(SEG, D, kind=F32 if residual else BF),
        compiler_params=params(),
        cost_estimate=cost(4),
    )(dq, dkv, w_own, w_par, *residual)


def weight_grad_kernel(ids_ref, comp_ref, mem_ref, own_ref, other_ref, dkv0, dkv1, dq0, dq1, *rest):
    t, n = pl.program_id(0), pl.program_id(1)
    out_ref, acc = rest[-2:]
    rows = D // out_ref.shape[0]

    def add(source, dkv):
        acc[:, :HALF] += tn(source, dkv[...])

    @pl.when((t == 0) & (n == 0))
    def _():
        acc[:, :HALF] = tn(comp_ref[0], dkv0[...])

    pl.when((t == 0) & (n == 1))(lambda: add(mem_ref[0], dkv0))

    @pl.when((t == 0) & (n == 2))
    def _():
        add(own_ref[...], dkv0)
        acc[:, HALF:] = tn(own_ref[...], dq0[...])

    pl.when((t == 1) & (n == 0))(lambda: add(comp_ref[0], dkv1))
    pl.when((t == 1) & (n == 1))(lambda: add(mem_ref[0], dkv1))

    @pl.when((t == 1) & (n == 2))
    def _():
        add(other_ref[...], dkv1)
        acc[:, HALF:] += tn(other_ref[...], dq1[...])
        total = acc[...].reshape(out_ref.shape[0], rows, 6 * HD)
        if len(rest) > 2:
            total = total + rest[0][...].astype(F32)
            out_ref[:, rows:] = rest[1][...]
        out_ref[:, :rows] = total.astype(BF)


def weight_grads(g, n_dp, ids, compressed, memory, own, other, dkvs, dqs, *received):
    rows = D // n_dp
    outer = rows + (16 if received else 0)
    return pl.pallas_call(
        weight_grad_kernel,
        grid_spec=pltpu.PrefetchScalarGridSpec(
            num_scalar_prefetch=1,
            grid=(2, 3),
            in_specs=[
                pl.BlockSpec((1, CM, D), lambda t, n, ids: (ids[t], 0, 0)),
                pl.BlockSpec((1, SEG, D), lambda t, n, ids: (ids[t], 0, 0)),
                whole(SEG, D),
                whole(SEG, D),
                pl.BlockSpec((SEG, HALF), lambda t, n, ids: (jnp.where(t == 0, n, 2), g)),
                pl.BlockSpec((SEG, HALF), lambda t, n, ids: (jnp.where(t == 0, 0, n), g)),
                pl.BlockSpec((SEG, 2 * HD), lambda t, n, ids: (0, g)),
                pl.BlockSpec((SEG, 2 * HD), lambda t, n, ids: (0, g)),
            ] + [whole(*a.shape) for a in received],
            out_specs=whole(n_dp, outer, 6 * HD),
            scratch_shapes=[pltpu.VMEM((D, 6 * HD), F32)],
        ),
        out_shape=shape(n_dp, outer, 6 * HD),
        compiler_params=params(),
        cost_estimate=cost(7),
    )(ids, compressed, memory, own, other, *dkvs, *dqs, *received)


def copies(moves, out_shapes, index, *arrays):
    count = len(arrays)

    def kernel(index_ref, *refs):
        ins, outs, sems = refs[:count], refs[count:-1], refs[-1]
        started = []
        for n, (source, target) in enumerate(moves(index_ref, ins, outs)):
            copy = pltpu.make_async_copy(source, target, sems.at[n])
            copy.start()
            started.append(copy)
        for copy in started:
            copy.wait()

    return pl.pallas_call(
        kernel,
        in_specs=[smem_spec] + [any_spec] * count,
        out_specs=[vmem_spec] * len(out_shapes),
        out_shape=[shape(*dims) for dims in out_shapes],
        scratch_shapes=[pltpu.SemaphoreType.DMA((64,))],
        compiler_params=pltpu.CompilerParams(vmem_limit_bytes=16 << 20),
        cost_estimate=cost(3),
    )(index, *arrays)


def assemble(chunks, sources, parts):
    n, cols = len(chunks), chunks[0].shape[1]

    def moves(index, ins, outs):
        for k in range(n):
            row = 0
            for out, rows in zip(outs, parts):
                yield ins[k].at[pl.ds(row, rows)], out.at[pl.ds(pl.multiple_of(index[k] * rows, rows), rows)]
                row += rows

    return copies(moves, [(n * rows, cols) for rows in parts], sources, *chunks)


def compress_kernel(h_ref, memory_ref, compressed_ref, w_ref, bias_ref, out_ref, weight):
    n_dp, _, rows, width = w_ref.shape

    @pl.when(pl.program_id(0) == 0)
    def _():
        for r in range(RATE):
            for k in range(n_dp):
                weight[r, k * rows:(k + 1) * rows] = w_ref[k, r]

    row = lax.broadcasted_iota(jnp.int32, (176, SEG), 0)
    col = lax.broadcasted_iota(jnp.int32, (176, SEG), 1)
    total = jnp.zeros((176, width), F32)
    for r in range(RATE):
        pick = jnp.where((col == RATE * row + r) & (row < CC), 1.0, 0.0).astype(BF)
        taken = nn(pick, memory_ref[0]).astype(BF)
        total = total + nn(taken, weight[r])
    made = (total + bias_ref[...].astype(F32)).astype(BF)
    to = lax.broadcasted_iota(jnp.int32, (SEG, SEG), 0)
    of = lax.broadcasted_iota(jnp.int32, (SEG, SEG), 1)
    keep = jnp.where(of == to + CC, 1.0, 0.0).astype(BF)
    to = lax.broadcasted_iota(jnp.int32, (SEG, 176), 0)
    of = lax.broadcasted_iota(jnp.int32, (SEG, 176), 1)
    put = jnp.where((of == to - (CM - CC)) & (of < CC), 1.0, 0.0).astype(BF)
    out_ref[0] = (nn(keep, compressed_ref[0]) + nn(put, made)).astype(BF)


def compress(h, memory, compressed, w, bias):
    seqs, width = memory.shape[0], w.shape[3]
    return pl.pallas_call(
        compress_kernel,
        grid_spec=pltpu.PrefetchScalarGridSpec(
            num_scalar_prefetch=1,
            grid=(seqs,),
            in_specs=[
                pl.BlockSpec((1, SEG, D), lambda s, h: (s, 0, 0)),
                pl.BlockSpec((1, CM, width), lambda s, h: (s, 0, h[0])),
                whole(*w.shape),
                whole(1, width),
            ],
            out_specs=pl.BlockSpec((1, CM, width), lambda s, h: (s, 0, 0)),
            scratch_shapes=[pltpu.VMEM((RATE, D, width), BF)],
        ),
        out_shape=shape(seqs, CM, width),
        compiler_params=params(),
        cost_estimate=cost(8),
    )(h, memory, compressed, w, bias.reshape(1, -1))


def per_device(
    inputs,
    memory,
    compressed,
    slot_valid,
    slot_age,
    w_query,
    w_key,
    w_value,
    content_bias,
    w_out,
    ln_gain,
    ln_bias,
    w_up,
    up_bias,
    w_down,
    down_bias,
    w_comp,
    comp_bias,
    cotangent,
):
    n_dp = lax.axis_size("dp")
    d = lax.axis_index("dp")
    h = lax.axis_index("head")
    h1 = h.reshape(1)
    ids = jnp.stack([h, h ^ 2]).astype(jnp.int32)
    seqs = memory.shape[0]
    rows = w_key.shape[0]
    out_rows = w_out.shape[0]
    share, up_share = content_bias.shape[0], up_bias.shape[0]
    values = 4 * share + up_share
    sources = ring_sources(d, n_dp)
    pick = lambda a, n, axis: lax.dynamic_index_in_dim(a, n, axis, keepdims=False)

    pack = jnp.concatenate(
        [w_key[:, :HD], w_value[:, :HD], w_key[:, HD:], w_value[:, HD:], w_query], axis=1
    )
    small = jnp.concatenate([content_bias, ln_gain, ln_bias, down_bias, up_bias]).reshape(1, -1)
    small = jnp.concatenate([small, c_swap(small)])
    small = jnp.concatenate([small, x_swap(small)])
    small = jnp.take(small, h ^ jnp.arange(4), axis=0, mode="clip")
    small = jnp.pad(small, ((0, 12), (0, 6 * HD - values)))
    pack_ring = ring_gather(jnp.concatenate([pack, small]), n_dp)
    inputs_x = x_swap(inputs)
    last = jnp.concatenate(
        [w_comp.reshape(RATE * rows, 2 * HD)] + [w_out[:, k * 2 * HD:(k + 1) * 2 * HD] for k in range(4)]
    )
    last = lax.all_gather(last, "dp", axis=0, tiled=True).reshape(n_dp, -1, 2 * HD)
    cot_x = x_swap(cotangent)
    ffn_ring = ring_gather(jnp.concatenate([w_up, w_down.T]), n_dp)

    w_own, small = assemble(pack_ring, sources, (rows, 16))
    w_par = c_swap(w_own)
    small = small.reshape(n_dp, 16, 6 * HD)[:, :4, :values].reshape(4 * n_dp, values).astype(F32)
    bias_all = small[:, :share].reshape(4, 2 * HD)
    gain = small[:, share:2 * share].reshape(1, D)
    shift = small[:, 2 * share:3 * share].reshape(1, D)
    down_shift = small[:, 3 * share:4 * share].reshape(1, D)
    up_shift = small[:, 4 * share:].reshape(4, D)
    two = lambda a: jnp.concatenate([pick(a, h, 0), pick(a, h ^ 1, 0)]).reshape(1, -1)
    bias, up_shift = two(bias_all), two(up_shift)

    i = jnp.arange(SEG, dtype=jnp.int32)[None, :]
    j = jnp.arange(2 * SEG, dtype=jnp.int32)[:, None]
    gap = i + SEG - j
    near = jnp.where(gap >= 0, jnp.log1p(jnp.maximum(gap, 0).astype(F32)), FAR)

    def far_of(s):
        age, valid = pick(slot_age, s, 0)[:, None], pick(slot_valid, s, 0)[:, None]
        return jnp.where(valid > 0, jnp.log1p(jnp.maximum(i + age, 0).astype(F32)), FAR)

    far = [far_of(h), far_of(h ^ 2)]
    heads = jnp.concatenate([2 * h + jnp.arange(2), 2 * (h ^ 1) + jnp.arange(2)])
    slopes = 0.6 * jnp.power(0.7, heads.astype(F32))

    kv_q = project(ids, compressed, memory, inputs, inputs_x, w_own, w_par, bias)
    kv, q = kv_q
    mixed_x, lse_x = attend(1, slopes, q, kv, near, far[1])
    sent = x_swap(mixed_x)
    mixed, lse = attend(0, slopes, q, kv, near, far[0])

    def ffn_moves(index, ins, outs):
        for k in range(n_dp):
            at = pl.multiple_of(index[k] * rows, rows)
            yield ins[k].at[pl.ds(0, rows)], outs[0].at[pl.ds(at, rows)]
            yield ins[k].at[pl.ds(rows, rows)], outs[0].at[pl.ds(D + at, rows)]

    (ffn_own,) = copies(ffn_moves, [(2 * D, D)], sources, *ffn_ring)
    ffn_par = c_swap(ffn_own)

    comp_w = last[:, :RATE * rows].reshape(n_dp, RATE, rows, 2 * HD)
    wo = last[:, RATE * rows:].reshape(n_dp, 4, out_rows, 2 * HD).transpose(0, 2, 1, 3).reshape(n_dp, out_rows, D)
    wo2 = jnp.stack([wo, c_swap(wo)])
    wo2x = x_swap(wo2)
    per = n_dp // 4

    def wo_moves(index, ins, outs):
        me = index[0]
        for e in range(4):
            for b in range(4):
                source = ins[e // 2].at[e % 2, pl.ds(b * per, per)]
                yield source, outs[0].at[me ^ b, :, me ^ e]

    (w_o,) = copies(wo_moves, [(4, per, 4, out_rows, D)], h1, wo2, wo2x)
    w_o = w_o.reshape(D, D)

    residual, normed = attention_out(mixed, sent, w_o, inputs, gain, shift)
    normed_x = x_swap(normed)
    hid, gb, up_cols, branch, gn = feed_forward(normed, cotangent, up_shift, ffn_own, ffn_par, F32)

    other = c_swap(jnp.stack([inputs, inputs_x]))

    def memory_moves(index, ins, outs):
        me = index[0]
        yield ins[0], outs[0].at[me]
        yield ins[1], outs[0].at[me ^ 2]
        yield ins[2].at[0], outs[0].at[me ^ 1]
        yield ins[2].at[1], outs[0].at[me ^ 3]

    (new_memory,) = copies(memory_moves, [(seqs, SEG, D)], h1, inputs, inputs_x, other)
    new_compressed = compress(h1, memory, compressed, comp_w, comp_bias)

    hid_x, gb_x, up_cols_x, branch_x, gn_x = feed_forward(normed_x, cot_x, up_shift, ffn_own, ffn_par, BF)
    gn_x = x_swap(gn_x)
    branch_x = x_swap(branch_x)
    output = (residual + branch + branch_x.astype(F32) + down_shift).astype(BF)

    acts = ((normed, normed_x), (cotangent, cot_x), (gb, gb_x), (hid, hid_x))
    from_par = c_swap(ffn_grads(1, n_dp, *acts))
    ffn_sum = ring_scatter(ffn_grads(0, n_dp, *acts, from_par), d, n_dp)
    grad_up, grad_down = ffn_sum[0], ffn_sum[1].T

    grad_residual, do, do_x, sums, g_out = norm_back(h1, residual, gn, gn_x, cotangent, gain, mixed, sent, w_o)
    do_x = x_swap(do_x)
    g_out = g_out.reshape(n_dp, 2, 2, out_rows, D)
    cc, xx = h % 2, h // 2
    g_out = (pick(g_out, cc, 2).astype(F32) + c_swap(pick(g_out, 1 - cc, 2)).astype(F32)).astype(BF)
    g_out = (pick(g_out, xx, 1).astype(F32) + x_swap(pick(g_out, 1 - xx, 1)).astype(F32)).astype(BF)
    grad_out = lax.psum_scatter(g_out.reshape(n_dp * out_rows, D), "dp", scatter_dimension=0, tiled=True).astype(F32)

    dq, dkv, q_cols = attend_back(0, slopes, q, kv, near, far[0], mixed, lse, do)
    term = token_term(dq, dkv, w_own, w_par, grad_residual)
    dq_x, dkv_x, q_cols_x = attend_back(1, slopes, q, kv, near, far[1], mixed_x, lse_x, do_x)
    term_x = x_swap(token_term(dq_x, dkv_x, w_own, w_par))
    grad_input = term + term_x.astype(F32)

    lane = jnp.arange(4)[:, None]

    def place(a):
        a = a.reshape(2, 1, -1)
        return jnp.where(lane == h, a[0], 0.0) + jnp.where(lane == h ^ 1, a[1], 0.0)

    tiny = jnp.concatenate([
        place(q_cols + q_cols_x).reshape(-1, share),
        sums[0].reshape(-1, share),
        sums[1].reshape(-1, share),
        sums[2].reshape(-1, share),
        place(up_cols + up_cols_x).reshape(-1, up_share),
    ], axis=1)
    tiny = tiny + x_swap(tiny)
    tiny = tiny + c_swap(tiny)
    tiny = jnp.pad(tiny.astype(BF).reshape(n_dp, 4, values), ((0, 0), (0, 12), (0, 6 * HD - values)))

    work = (ids, compressed, memory, inputs, inputs_x, (dkv, dkv_x), (dq, dq_x))
    from_par = c_swap(weight_grads(1, n_dp, *work))
    g_sum = ring_scatter(weight_grads(0, n_dp, *work, from_par, tiny), d, n_dp)
    tiny = pick(g_sum[rows:], h, 0)
    g_sum = g_sum[:rows]
    grad_key = jnp.concatenate([g_sum[:, :HD], g_sum[:, 2 * HD:3 * HD]], axis=1)
    grad_value = jnp.concatenate([g_sum[:, HD:2 * HD], g_sum[:, 3 * HD:4 * HD]], axis=1)
    grad_query = g_sum[:, 4 * HD:]

    return (
        output,
        grad_input,
        grad_query,
        grad_key,
        grad_value,
        tiny[:share],
        grad_out,
        tiny[share:2 * share],
        tiny[2 * share:3 * share],
        grad_up,
        tiny[4 * share:values],
        grad_down,
        tiny[3 * share:4 * share],
        new_memory,
        new_compressed,
    )


def solution(mesh):
    both = ("dp", "head")
    in_specs = (
        P(both, None),
        P("dp", None, None),
        P("dp", None, None),
        P("dp", None),
        P("dp", None),
        P("dp", "head"),
        P("dp", "head"),
        P("dp", "head"),
        P(both),
        P(both, None),
        P(both),
        P(both),
        P("dp", "head"),
        P(both),
        P("head", "dp"),
        P(both),
        P(None, "dp", "head"),
        P("head"),
        P(both, None),
    )
    out_specs = (
        P(both, None),
        P(both, None),
        P("dp", "head"),
        P("dp", "head"),
        P("dp", "head"),
        P(both),
        P(both, None),
        P(both),
        P(both),
        P("dp", "head"),
        P(both),
        P("head", "dp"),
        P(both),
        P("dp", None, None),
        P("dp", None, "head"),
    )
    return jax.shard_map(per_device, mesh=mesh, in_specs=in_specs, out_specs=out_specs, check_vma=False)
```

```python
import functools

import jax
import jax.numpy as jnp
from jax import lax
from jax.experimental import pallas as pl
from jax.experimental.pallas import tpu as pltpu
from jax.sharding import PartitionSpec as P

D = 1024
HD = 128
SEG = 512
CM = 512
RATE = 3
CC = 171
LN_EPS = 1e-05
LOG2E = 1.4426950408889634
SCALE2 = LOG2E * HD ** (-0.5)
FAR = 1e32
VMEM = 56 * 1024 * 1024
BF = jnp.bfloat16
F32 = jnp.float32


def nt(a, b):
    return lax.dot_general(a, b, (((1,), (1,)), ((), ())), preferred_element_type=F32)


def tn(a, b):
    return lax.dot_general(a, b, (((0,), (0,)), ((), ())), preferred_element_type=F32)


def nn(a, b):
    return jnp.dot(a, b, preferred_element_type=F32)


def x_swap(a):
    return lax.ppermute(a, "head", [(i, i ^ 2) for i in range(4)])


def c_swap(a):
    return lax.ppermute(a, "head", [(i, i ^ 1) for i in range(4)])


def fwd_kernel(slope_ref, q_ref, bias_ref, kv_ref, near_ref, far_ref, mixed_ref, lse_ref):
    a = pl.program_id(0)
    slope2 = slope_ref[a] * LOG2E
    q = (q_ref[0] + bias_ref[...]).astype(BF)
    parts = []
    for n in range(3):
        k = kv_ref[0, n * SEG:(n + 1) * SEG, :HD]
        table = far_ref[...] if n == 0 else near_ref[(n - 1) * SEG:n * SEG, :]
        parts.append(nt(k, q) * SCALE2 - slope2 * table)
    top = jnp.maximum(jnp.maximum(jnp.max(parts[0], axis=0, keepdims=True), jnp.max(parts[1], axis=0, keepdims=True)),
                      jnp.max(parts[2], axis=0, keepdims=True))
    total = jnp.zeros((1, SEG), F32)
    acc = jnp.zeros((HD, SEG), F32)
    for n in range(3):
        p = jnp.exp2(parts[n] - top)
        total = total + jnp.sum(p, axis=0, keepdims=True)
        acc = acc + tn(kv_ref[0, n * SEG:(n + 1) * SEG, HD:], p.astype(BF))
    mixed_ref[...] = (acc / total).T.astype(BF)
    lse_ref[...] = (top + jnp.log2(total)).reshape(1, 1, SEG)


def bwd_kernel(slope_ref, q_ref, bias_ref, kv_ref, near_ref, far_ref, mixed_ref, lse_ref, do_ref, dq_ref, dkv_ref, sum_ref):
    a = pl.program_id(0)
    slope2 = slope_ref[a] * LOG2E
    q = (q_ref[0] + bias_ref[...]).astype(BF)
    do = do_ref[...]
    lse = lse_ref[...].reshape(1, SEG)
    row_dot = jnp.sum((do.astype(F32) * mixed_ref[...].astype(F32)).T, axis=0, keepdims=True)
    inv_root = HD ** (-0.5)
    dq = jnp.zeros((HD, SEG), F32)
    for n in range(3):
        rows = slice(n * SEG, (n + 1) * SEG)
        k = kv_ref[0, rows, :HD]
        v = kv_ref[0, rows, HD:]
        table = far_ref[...] if n == 0 else near_ref[(n - 1) * SEG:n * SEG, :]
        p = jnp.exp2(nt(k, q) * SCALE2 - slope2 * table - lse)
        ds = (p * (nt(v, do) - row_dot)).astype(BF)
        dkv_ref[rows, HD:] = nn(p.astype(BF), do).astype(BF)
        dkv_ref[rows, :HD] = (nn(ds, q) * inv_root).astype(BF)
        dq = dq + tn(k, ds)
    dq = (dq.T * inv_root).astype(BF)
    dq_ref[...] = dq
    sum_ref[...] = jnp.sum(dq.astype(F32), axis=0, keepdims=True)


def ring_order(n):
    up = list(range(0, n, 2))
    return up + [p + 1 for p in reversed(up)]


def ring_perms(n):
    order = ring_order(n)
    ahead = [(order[p], order[(p + 1) % n]) for p in range(n)]
    return ahead, [(b, a) for a, b in ahead]


def ring_place(d, n):
    return jnp.where(d % 2 == 0, d // 2, n - 1 - d // 2)


def ring_member(p, n):
    p = p % n
    return jnp.where(p < n // 2, 2 * p, 2 * (n - 1 - p) + 1)


def after(first, *then):
    out = lax.optimization_barrier((first,) + then)[1:]
    return out if len(then) > 1 else out[0]


class RingGather:
    def __init__(self, chunk, n):
        self.n, self.k = n, 0
        self.ahead, self.back = ring_perms(n)
        self.f = self.b = chunk
        self.chunks = [chunk]

    def step(self, first=None):
        self.k += 1
        if self.k > self.n // 2:
            return
        if first is not None:
            self.f, self.b = after(first, self.f, self.b)
        self.f = lax.ppermute(self.f, "dp", self.ahead)
        self.chunks.append(self.f)
        if self.k < self.n - self.n // 2:
            self.b = lax.ppermute(self.b, "dp", self.back)
            self.chunks.append(self.b)

    def finish(self):
        while self.k < self.n // 2:
            self.step()
        return self.chunks


def ring_sources(d, n):
    place = ring_place(d, n)
    steps = [0]
    for k in range(1, n // 2 + 1):
        steps.append(-k)
        if k < n - n // 2:
            steps.append(k)
    return ring_member(place + jnp.array(steps, jnp.int32), n).astype(jnp.int32)


ROWS = 3 * SEG
HALF = D // 2
smem_spec = pl.BlockSpec(memory_space=pltpu.SMEM)
vmem_spec = pl.BlockSpec(memory_space=pltpu.VMEM)
any_spec = pl.BlockSpec(memory_space=pl.ANY)


def params():
    return pltpu.CompilerParams(vmem_limit_bytes=VMEM)


def cost(us):
    return pl.CostEstimate(flops=int(us * 0.18e9), bytes_accessed=1, transcendentals=0)


def shape(*dims, kind=BF):
    return jax.ShapeDtypeStruct(dims, kind)


def whole(*dims):
    return pl.BlockSpec(dims, lambda *i: (0,) * len(dims))


def attend(t, slopes, q, bias, kv, near, far):
    return pl.pallas_call(
        fwd_kernel,
        grid=(4,),
        in_specs=[
            smem_spec,
            pl.BlockSpec((1, SEG, HD), lambda a: (t, 0, a)),
            pl.BlockSpec((1, HD), lambda a: (0, a)),
            pl.BlockSpec((1, ROWS, 2 * HD), lambda a: (t, 0, a)),
            whole(2 * SEG, SEG),
            whole(SEG, SEG),
        ],
        out_specs=[pl.BlockSpec((SEG, HD), lambda a: (0, a)), pl.BlockSpec((1, 1, SEG), lambda a: (a, 0, 0))],
        out_shape=[shape(SEG, HALF), shape(4, 1, SEG, kind=F32)],
        compiler_params=params(),
        cost_estimate=cost(12),
    )(slopes, q, bias, kv, near, far)


def attend_back(t, slopes, q, bias, kv, near, far, mixed, lse, do):
    column = pl.BlockSpec((SEG, HD), lambda a: (0, a))
    return pl.pallas_call(
        bwd_kernel,
        grid=(4,),
        in_specs=[
            smem_spec,
            pl.BlockSpec((1, SEG, HD), lambda a: (t, 0, a)),
            pl.BlockSpec((1, HD), lambda a: (0, a)),
            pl.BlockSpec((1, ROWS, 2 * HD), lambda a: (t, 0, a)),
            whole(2 * SEG, SEG),
            whole(SEG, SEG),
            column,
            pl.BlockSpec((1, 1, SEG), lambda a: (a, 0, 0)),
            column,
        ],
        out_specs=[column, pl.BlockSpec((ROWS, 2 * HD), lambda a: (0, a)), pl.BlockSpec((1, HD), lambda a: (0, a))],
        out_shape=[shape(SEG, HALF), shape(ROWS, D), shape(1, HALF, kind=F32)],
        compiler_params=params(),
        cost_estimate=cost(16),
    )(slopes, q, bias, kv, near, far, mixed, lse, do)


def pack_kernel(key_ref, value_ref, query_ref, out_ref, *rest):
    smalls, pack_ref = rest[:-1], rest[-1]
    rows = key_ref.shape[0]
    piece = out_ref.shape[0]
    pack_ref[:rows, :HD] = key_ref[:, :HD]
    pack_ref[:rows, HD:2 * HD] = value_ref[:, :HD]
    pack_ref[:rows, 2 * HD:3 * HD] = key_ref[:, HD:]
    pack_ref[:rows, 3 * HD:4 * HD] = value_ref[:, HD:]
    pack_ref[:rows, 4 * HD:6 * HD] = query_ref[...]
    for k in range(4):
        pack_ref[k * piece:(k + 1) * piece, 6 * HD:] = out_ref[:, k * 2 * HD:(k + 1) * 2 * HD]
    line = jnp.concatenate([a[...].astype(F32) for a in smalls], axis=1)
    line = jnp.concatenate([line, jnp.zeros((1, D - line.shape[1]), F32)], axis=1)
    row = lax.broadcasted_iota(jnp.int32, (16, D), 0)
    pack_ref[rows:] = jnp.where(row == 0, jnp.broadcast_to(line, (16, D)), 0.0).astype(BF)


def pack(w_key, w_value, w_query, w_out, smalls):
    return pl.pallas_call(
        pack_kernel,
        in_specs=[vmem_spec] * (4 + len(smalls)),
        out_specs=vmem_spec,
        out_shape=shape(w_key.shape[0] + 16, D),
        compiler_params=params(),
        cost_estimate=cost(1),
    )(w_key, w_value, w_query, w_out, *[a.reshape(1, -1) for a in smalls])


def project_kernel(ids_ref, comp_ref, mem_ref, own_ref, other_ref, w_own_ref, w_par_ref, kv_ref, q_ref):
    t, n = pl.program_id(0), pl.program_id(1)

    def put(source):
        kv_ref[0, :, :HALF] = nn(source, w_own_ref[:, :HALF]).astype(BF)
        kv_ref[0, :, HALF:] = nn(source, w_par_ref[:, :HALF]).astype(BF)

    def ask(source):
        put(source)
        q_ref[0, :, :2 * HD] = nn(source, w_own_ref[:, HALF:])
        q_ref[0, :, 2 * HD:] = nn(source, w_par_ref[:, HALF:])

    pl.when(n == 0)(lambda: put(comp_ref[0]))
    pl.when(n == 1)(lambda: put(mem_ref[0]))
    pl.when((n == 2) & (t == 0))(lambda: ask(own_ref[...]))
    pl.when((n == 2) & (t == 1))(lambda: ask(other_ref[...]))


def project(ids, compressed, memory, own, other, w_own, w_par):
    return pl.pallas_call(
        project_kernel,
        grid_spec=pltpu.PrefetchScalarGridSpec(
            num_scalar_prefetch=1,
            grid=(2, 3),
            in_specs=[
                pl.BlockSpec((1, CM, D), lambda t, n, ids: (ids[t], 0, 0)),
                pl.BlockSpec((1, SEG, D), lambda t, n, ids: (ids[t], 0, 0)),
                whole(SEG, D),
                whole(SEG, D),
                whole(D, 3 * 2 * HD),
                whole(D, 3 * 2 * HD),
            ],
            out_specs=[
                pl.BlockSpec((1, SEG, D), lambda t, n, ids: (t, n, 0)),
                pl.BlockSpec((1, SEG, HALF), lambda t, n, ids: (t, 0, 0)),
            ],
        ),
        out_shape=[shape(2, ROWS, D), shape(2, SEG, HALF, kind=F32)],
        compiler_params=params(),
        cost_estimate=cost(12),
    )(ids, compressed, memory, own, other, w_own, w_par)


def norm_kernel(mixed_ref, sent_ref, w_ref, in_ref, gain_ref, shift_ref, residual_ref, normed_ref):
    out = nn(mixed_ref[...], w_ref[:HALF]) + nn(sent_ref[...], w_ref[HALF:])
    residual = in_ref[...].astype(F32) + out
    residual_ref[...] = residual
    center = residual - jnp.mean(residual, axis=-1, keepdims=True)
    rstd = lax.rsqrt(jnp.mean(center * center, axis=-1, keepdims=True) + LN_EPS)
    normed_ref[...] = (center * rstd * gain_ref[...] + shift_ref[...]).astype(BF)


def attention_out(mixed, sent, w_o, inputs, gain, shift):
    rows = SEG // 2
    half = pl.BlockSpec((rows, HALF), lambda i: (i, 0))
    full = pl.BlockSpec((rows, D), lambda i: (i, 0))
    return pl.pallas_call(
        norm_kernel,
        grid=(2,),
        in_specs=[half, half, whole(D, D), full, whole(1, D), whole(1, D)],
        out_specs=[full, full],
        out_shape=[shape(SEG, D, kind=F32), shape(SEG, D)],
        compiler_params=params(),
        cost_estimate=cost(4),
    )(mixed, sent, w_o, inputs, gain, shift)


def gelu_pair(before):
    c0, c1 = 0.7978845608028654, 0.044715
    sq = before * before
    t = jnp.tanh(c0 * before * (1.0 + c1 * sq))
    half = 0.5 * (1.0 + t)
    return before * half, half + 0.5 * before * (1.0 - t * t) * (c0 * (1.0 + 3.0 * c1 * sq))


def ffn_kernel(n_dp, index_ref, norm_ref, cot_ref, bias_ref, *refs):
    chunks = refs[:2 * n_dp]
    hid_ref, gb_ref, sum_ref, branch_ref, gn_ref, up_ref, down_ref, branch, gn, sems = refs[2 * n_dp:]
    i, tiles = pl.program_id(0), up_ref.shape[0]
    tile, rows = up_ref.shape[2], D // n_dp

    def moves(step):
        group, column = divmod(step, tiles // 2)
        for k in range(n_dp):
            source = chunks[group * n_dp + k]
            at = pl.ds(pl.multiple_of(index_ref[k] * rows, rows), rows)
            for m, target in enumerate((up_ref, down_ref)):
                yield pltpu.make_async_copy(
                    source.at[pl.ds(m * rows, rows), pl.ds(column * tile, tile)],
                    target.at[step, at],
                    sems.at[(step * n_dp + k) * 2 + m],
                )

    @pl.when(i == 0)
    def _():
        for step in range(tiles):
            for move in moves(step):
                move.start()

    for step in range(tiles):
        @pl.when(i == step)
        def _(step=step):
            for move in moves(step):
                move.wait()

    up, down = up_ref.at[i], down_ref.at[i]
    before = nn(norm_ref[...], up[...]) + bias_ref[...]
    act, slope = gelu_pair(before)
    act = act.astype(BF)
    gb = (nn(cot_ref[...], down[...]) * slope).astype(BF)
    hid_ref[...] = act
    gb_ref[...] = gb
    sum_ref[...] = jnp.sum(gb.astype(F32), axis=0, keepdims=True)

    @pl.when(i == 0)
    def _():
        branch[...] = nt(act, down[...])
        gn[...] = nt(gb, up[...])

    @pl.when(i > 0)
    def _():
        branch[...] += nt(act, down[...])
        gn[...] += nt(gb, up[...])

    @pl.when(i == tiles - 1)
    def _():
        branch_ref[...] = branch[...].astype(branch_ref.dtype)
        gn_ref[...] = gn[...].astype(gn_ref.dtype)


def feed_forward(n_dp, sources, norm, cot, bias, own, par, kind, tile=512):
    tiles = 2 * D // tile
    part = pl.BlockSpec((SEG, tile), lambda i, index: (0, i))
    line = pl.BlockSpec((1, tile), lambda i, index: (0, i))
    return pl.pallas_call(
        functools.partial(ffn_kernel, n_dp),
        grid_spec=pltpu.PrefetchScalarGridSpec(
            num_scalar_prefetch=1,
            grid=(tiles,),
            in_specs=[whole(SEG, D), whole(SEG, D), line] + [any_spec] * (2 * n_dp),
            out_specs=[part, part, line, whole(SEG, D), whole(SEG, D)],
            scratch_shapes=[pltpu.VMEM((tiles, D, tile), BF)] * 2
            + [pltpu.VMEM((SEG, D), F32)] * 2
            + [pltpu.SemaphoreType.DMA((2 * tiles * n_dp,))],
        ),
        out_shape=[shape(SEG, 2 * D), shape(SEG, 2 * D), shape(1, 2 * D, kind=F32), shape(SEG, D, kind=kind), shape(SEG, D, kind=kind)],
        compiler_params=params(),
        cost_estimate=cost(16),
    )(sources, norm, cot, bias, *own, *par)


def ffn_grad_kernel(tiles, n0, n1, c0, c1, gb0, gb1, hid0, hid1, *rest):
    parts, outs = (rest[:-1], rest[-1:]) if len(rest) > 2 * tiles else ((), rest)
    step = pl.program_id(0) * tiles + pl.program_id(1)
    for m in range(2):
        for i in range(tiles):
            k = m * tiles + i

            @pl.when(step == k)
            def _(m=m, k=k):
                if m == 0:
                    total = tn(n0[...], gb0[...]) + tn(n1[...], gb1[...])
                else:
                    total = tn(c0[...], hid0[...]) + tn(c1[...], hid1[...])
                if parts:
                    out = outs[0]
                    total = total.reshape(out.shape[0], out.shape[2], -1)
                    out[:, 0] = (total + parts[k][...].astype(F32)).astype(BF)
                else:
                    outs[k][...] = total.reshape(outs[k].shape).astype(BF)


def ffn_grads(g, n_dp, norms, cots, gbs, hids, *received, tile=512):
    n = D // tile
    rows = D // n_dp
    tokens = whole(SEG, D)
    early = pl.BlockSpec((SEG, tile), lambda m, i: (0, g * n + jnp.where(m == 0, i, n - 1)))
    late = pl.BlockSpec((SEG, tile), lambda m, i: (0, g * n + jnp.where(m == 0, 0, i)))
    part = whole(n_dp, rows, tile)
    if received:
        out_specs = pl.BlockSpec((n_dp, 1, rows, tile), lambda m, i: (0, m, 0, i))
        out_shape = shape(n_dp, 2, rows, D)
    else:
        out_specs, out_shape = [part] * (2 * n), [shape(n_dp, rows, tile)] * (2 * n)
    return pl.pallas_call(
        functools.partial(ffn_grad_kernel, n),
        grid=(2, n),
        in_specs=[tokens] * 4 + [early] * 2 + [late] * 2 + [part] * len(received),
        out_specs=out_specs,
        out_shape=out_shape,
        compiler_params=params(),
        cost_estimate=cost(10),
    )(*norms, *cots, *gbs, *hids, *received)


def norm_back_kernel(h_ref, residual_ref, gn_ref, gnx_ref, cot_ref, gain_ref, mixed_ref, sent_ref, w_ref,
                     grad_ref, keep_ref, send_ref, sums_ref, out_ref, acc):
    i = pl.program_id(0)
    residual = residual_ref[...]
    center = residual - jnp.mean(residual, axis=-1, keepdims=True)
    rstd = lax.rsqrt(jnp.mean(center * center, axis=-1, keepdims=True) + LN_EPS)
    xhat = center * rstd
    gn = gn_ref[...] + gnx_ref[...].astype(F32)
    g = gn * gain_ref[...]
    cot = cot_ref[...].astype(F32)
    grad = cot + rstd * (g - jnp.mean(g, axis=-1, keepdims=True) - xhat * jnp.mean(g * xhat, axis=-1, keepdims=True))
    grad_ref[...] = grad
    low = grad.astype(BF)
    keep_ref[...] = nt(low, w_ref[:HALF]).astype(BF)
    send_ref[...] = nt(low, w_ref[HALF:]).astype(BF)
    total = lambda a: jnp.sum(a, axis=0, keepdims=True)
    sums = jnp.concatenate([total(gn * xhat), total(gn), total(cot)], axis=0)

    @pl.when(i == 0)
    def _():
        sums_ref[...] = sums
        acc[:HALF] = tn(mixed_ref[...], low)
        acc[HALF:] = tn(sent_ref[...], low)

    @pl.when(i > 0)
    def _():
        sums_ref[...] += sums
        acc[:HALF] += tn(mixed_ref[...], low)
        acc[HALF:] += tn(sent_ref[...], low)

    @pl.when(i == pl.num_programs(0) - 1)
    def _():
        for b in range(4):
            out_ref[h_ref[0] ^ b] = acc[b * 2 * HD:(b + 1) * 2 * HD].astype(BF)


def norm_back(h, residual, gn, gnx, cot, gain, mixed, sent, w_o):
    rows = SEG // 2
    half = pl.BlockSpec((rows, HALF), lambda i: (i, 0))
    full = pl.BlockSpec((rows, D), lambda i: (i, 0))
    return pl.pallas_call(
        norm_back_kernel,
        grid=(2,),
        in_specs=[smem_spec, full, full, full, full, whole(1, D), half, half, whole(D, D)],
        out_specs=[full, half, half, whole(3, D), whole(4, 2 * HD, D)],
        out_shape=[shape(SEG, D, kind=F32), shape(SEG, HALF), shape(SEG, HALF), shape(3, D, kind=F32), shape(4, 2 * HD, D)],
        scratch_shapes=[pltpu.VMEM((D, D), F32)],
        compiler_params=params(),
        cost_estimate=cost(7),
    )(h, residual, gn, gnx, cot, gain, mixed, sent, w_o)


def term_kernel(dq_ref, dkv_ref, w_own_ref, w_par_ref, *rest):
    out = nt(dkv_ref[:, :HALF], w_own_ref[:, :HALF]) + nt(dkv_ref[:, HALF:], w_par_ref[:, :HALF])
    out = out + nt(dq_ref[:, :2 * HD], w_own_ref[:, HALF:]) + nt(dq_ref[:, 2 * HD:], w_par_ref[:, HALF:])
    if len(rest) > 1:
        out = out + rest[0][...]
    rest[-1][...] = out.astype(rest[-1].dtype)


def token_term(dq, dkv, w_own, w_par, *residual):
    rows = SEG // 2
    full = pl.BlockSpec((rows, D), lambda i: (i, 0))
    weight = whole(D, 3 * 2 * HD)
    return pl.pallas_call(
        term_kernel,
        grid=(2,),
        in_specs=[
            pl.BlockSpec((rows, HALF), lambda i: (i, 0)),
            pl.BlockSpec((rows, D), lambda i: (4 + i, 0)),
            weight,
            weight,
        ] + [full] * len(residual),
        out_specs=full,
        out_shape=shape(SEG, D, kind=F32 if residual else BF),
        compiler_params=params(),
        cost_estimate=cost(4),
    )(dq, dkv, w_own, w_par, *residual)


def weight_grad_kernel(ids_ref, comp_ref, mem_ref, own_ref, other_ref, dkv0, dkv1, dq0, dq1, *rest):
    t, n = pl.program_id(0), pl.program_id(1)
    acc = rest[-1]
    parts, outs = (rest[:2], rest[3:4]) if len(rest) > 4 else ((), rest[:2])
    half = rest[0].shape[0]
    rows = D // (2 * half)

    def add(source, dkv):
        acc[:, :HALF] += tn(source, dkv[...])

    @pl.when((t == 0) & (n == 0))
    def _():
        acc[:, :HALF] = tn(comp_ref[0], dkv0[...])

    pl.when((t == 0) & (n == 1))(lambda: add(mem_ref[0], dkv0))

    @pl.when((t == 0) & (n == 2))
    def _():
        add(own_ref[...], dkv0)
        acc[:, HALF:] = tn(own_ref[...], dq0[...])

    pl.when((t == 1) & (n == 0))(lambda: add(comp_ref[0], dkv1))
    pl.when((t == 1) & (n == 1))(lambda: add(mem_ref[0], dkv1))

    @pl.when((t == 1) & (n == 2))
    def _():
        add(other_ref[...], dkv1)
        acc[:, HALF:] += tn(other_ref[...], dq1[...])
        total = acc[...].reshape(2 * half, rows, 6 * HD)
        for k in range(2):
            block = slice(k * half, (k + 1) * half)
            if parts:
                outs[0][block, :rows] = (total[block] + parts[k][...].astype(F32)).astype(BF)
            else:
                outs[k][...] = total[block].astype(BF)
        if parts:
            outs[0][:, rows:] = rest[2][...]


def weight_grads(g, n_dp, ids, compressed, memory, own, other, dkvs, dqs, *received):
    rows = D // n_dp
    if received:
        out_specs, out_shape = whole(n_dp, rows + 16, 6 * HD), shape(n_dp, rows + 16, 6 * HD)
    else:
        out_specs, out_shape = [whole(n_dp // 2, rows, 6 * HD)] * 2, [shape(n_dp // 2, rows, 6 * HD)] * 2
    return pl.pallas_call(
        weight_grad_kernel,
        grid_spec=pltpu.PrefetchScalarGridSpec(
            num_scalar_prefetch=1,
            grid=(2, 3),
            in_specs=[
                pl.BlockSpec((1, CM, D), lambda t, n, ids: (ids[t], 0, 0)),
                pl.BlockSpec((1, SEG, D), lambda t, n, ids: (ids[t], 0, 0)),
                whole(SEG, D),
                whole(SEG, D),
                pl.BlockSpec((SEG, HALF), lambda t, n, ids: (jnp.where(t == 0, n, 2), g)),
                pl.BlockSpec((SEG, HALF), lambda t, n, ids: (jnp.where(t == 0, 0, n), g)),
                pl.BlockSpec((SEG, 2 * HD), lambda t, n, ids: (0, g)),
                pl.BlockSpec((SEG, 2 * HD), lambda t, n, ids: (0, g)),
            ] + [whole(*a.shape) for a in received],
            out_specs=out_specs,
            scratch_shapes=[pltpu.VMEM((D, 6 * HD), F32)],
        ),
        out_shape=out_shape,
        compiler_params=params(),
        cost_estimate=cost(7),
    )(ids, compressed, memory, own, other, *dkvs, *dqs, *received)


def copies(moves, out_shapes, index, *arrays):
    count = len(arrays)

    def kernel(index_ref, *refs):
        ins, outs, sems = refs[:count], refs[count:-1], refs[-1]
        started = []
        for n, (source, target) in enumerate(moves(index_ref, ins, outs)):
            copy = pltpu.make_async_copy(source, target, sems.at[n])
            copy.start()
            started.append(copy)
        for copy in started:
            copy.wait()

    return pl.pallas_call(
        kernel,
        in_specs=[smem_spec] + [any_spec] * count,
        out_specs=[vmem_spec] * len(out_shapes),
        out_shape=[shape(*dims) for dims in out_shapes],
        scratch_shapes=[pltpu.SemaphoreType.DMA((96,))],
        compiler_params=pltpu.CompilerParams(vmem_limit_bytes=16 << 20),
        cost_estimate=cost(3),
    )(index, *arrays)


def assemble(chunks, sources, parts):
    n, cols = len(chunks), chunks[0].shape[1]

    def moves(index, ins, outs):
        for k in range(n):
            row = 0
            for out, rows in zip(outs, parts):
                yield ins[k].at[pl.ds(row, rows)], out.at[pl.ds(pl.multiple_of(index[k] * rows, rows), rows)]
                row += rows

    return copies(moves, [(n * rows, cols) for rows in parts], sources, *chunks)


def pick_kernel(index_ref, ahead_ref, back_ref, f_ref, b_ref):
    f_ref[...] = ahead_ref[0]
    b_ref[...] = back_ref[0]


def add_kernel(index_ref, f_in, b_in, ahead_ref, back_ref, f_ref, b_ref):
    f_ref[...] = (f_in[...].astype(F32) + ahead_ref[0].astype(F32)).astype(BF)
    b_ref[...] = (b_in[...].astype(F32) + back_ref[0].astype(F32)).astype(BF)


def add_one_kernel(index_ref, f_in, ahead_ref, back_ref, f_ref):
    f_ref[...] = (f_in[...].astype(F32) + ahead_ref[0].astype(F32)).astype(BF)


def close_kernel(index_ref, f_in, b_in, own_ref, _, out_ref):
    out_ref[...] = f_in[...].astype(F32) + b_in[...].astype(F32) + own_ref[0].astype(F32)


def ring_kernel(kernel, array, places, given, outs, kind=BF):
    _, rows, cols = array.shape
    flat = pl.BlockSpec((rows, cols), lambda i, index: (0, 0))
    block = lambda k: pl.BlockSpec((1, rows, cols), lambda i, index: (index[k], 0, 0))
    return pl.pallas_call(
        kernel,
        grid_spec=pltpu.PrefetchScalarGridSpec(
            num_scalar_prefetch=1,
            grid=(1,),
            in_specs=[flat] * len(given) + [block(0), block(1)],
            out_specs=[flat] * outs,
        ),
        out_shape=[shape(rows, cols, kind=kind)] * outs,
        compiler_params=pltpu.CompilerParams(vmem_limit_bytes=16 << 20),
        cost_estimate=cost(2),
    )(places, *given, array, array)


class RingScatter:
    def __init__(self, array, d, n):
        self.array, self.n, self.k = array, n, 0
        self.ahead, self.back = ring_perms(n)
        self.place = ring_place(d, n)
        self.up, self.down = n // 2, n - n // 2 - 1
        self.f, self.b = ring_kernel(pick_kernel, array, self.at(self.up, -self.down), (), 2)

    def at(self, p, q):
        return ring_member(self.place + jnp.array([p, q], jnp.int32), self.n).astype(jnp.int32)

    def step(self, first=None):
        self.k += 1
        k = self.k
        if k > self.up:
            return
        if first is not None:
            self.f, self.b = after(first, self.f, self.b)
        self.f = lax.ppermute(self.f, "dp", self.ahead)
        if k <= self.down:
            self.b = lax.ppermute(self.b, "dp", self.back)
        at = self.at(self.up - k, k - self.down)
        if k < self.down:
            self.f, self.b = ring_kernel(add_kernel, self.array, at, (self.f, self.b), 2)
        elif k < self.up:
            (self.f,) = ring_kernel(add_one_kernel, self.array, at, (self.f,), 1)

    def finish(self):
        while self.k < self.up:
            self.step()
        return ring_kernel(close_kernel, self.array, self.at(0, 0), (self.f, self.b), 1, F32)[0]


def sum_kernel(*refs):
    total = refs[0][...].astype(F32)
    for ref in refs[1:-1]:
        total = total + ref[...].astype(F32)
    refs[-1][...] = total.astype(refs[-1].dtype)


def add_up(kind, *arrays):
    rows, cols = arrays[0].shape
    specs = [
        pl.BlockSpec((rows // 2, cols), lambda i: (i, 0)) if a.shape[0] == rows else whole(*a.shape) for a in arrays
    ]
    return pl.pallas_call(
        sum_kernel,
        grid=(2,),
        in_specs=specs,
        out_specs=specs[0],
        out_shape=shape(rows, cols, kind=kind),
        compiler_params=params(),
        cost_estimate=cost(3),
    )(*arrays)


def compress_kernel(h_ref, memory_ref, compressed_ref, w_ref, bias_ref, out_ref, weight):
    n_dp, _, rows, width = w_ref.shape

    @pl.when(pl.program_id(0) == 0)
    def _():
        for r in range(RATE):
            for k in range(n_dp):
                weight[r, k * rows:(k + 1) * rows] = w_ref[k, r]

    row = lax.broadcasted_iota(jnp.int32, (176, SEG), 0)
    col = lax.broadcasted_iota(jnp.int32, (176, SEG), 1)
    total = jnp.zeros((176, width), F32)
    for r in range(RATE):
        pick = jnp.where((col == RATE * row + r) & (row < CC), 1.0, 0.0).astype(BF)
        taken = nn(pick, memory_ref[0]).astype(BF)
        total = total + nn(taken, weight[r])
    made = (total + bias_ref[...].astype(F32)).astype(BF)
    to = lax.broadcasted_iota(jnp.int32, (SEG, SEG), 0)
    of = lax.broadcasted_iota(jnp.int32, (SEG, SEG), 1)
    keep = jnp.where(of == to + CC, 1.0, 0.0).astype(BF)
    to = lax.broadcasted_iota(jnp.int32, (SEG, 176), 0)
    of = lax.broadcasted_iota(jnp.int32, (SEG, 176), 1)
    put = jnp.where((of == to - (CM - CC)) & (of < CC), 1.0, 0.0).astype(BF)
    out_ref[0] = (nn(keep, compressed_ref[0]) + nn(put, made)).astype(BF)


def compress(h, memory, compressed, w, bias):
    seqs, width = memory.shape[0], w.shape[3]
    return pl.pallas_call(
        compress_kernel,
        grid_spec=pltpu.PrefetchScalarGridSpec(
            num_scalar_prefetch=1,
            grid=(seqs,),
            in_specs=[
                pl.BlockSpec((1, SEG, D), lambda s, h: (s, 0, 0)),
                pl.BlockSpec((1, CM, width), lambda s, h: (s, 0, h[0])),
                whole(*w.shape),
                whole(1, width),
            ],
            out_specs=pl.BlockSpec((1, CM, width), lambda s, h: (s, 0, 0)),
            scratch_shapes=[pltpu.VMEM((RATE, D, width), BF)],
        ),
        out_shape=shape(seqs, CM, width),
        compiler_params=params(),
        cost_estimate=cost(8),
    )(h, memory, compressed, w, bias.reshape(1, -1))


def per_device(
    inputs,
    memory,
    compressed,
    slot_valid,
    slot_age,
    w_query,
    w_key,
    w_value,
    content_bias,
    w_out,
    ln_gain,
    ln_bias,
    w_up,
    up_bias,
    w_down,
    down_bias,
    w_comp,
    comp_bias,
    cotangent,
):
    n_dp = lax.axis_size("dp")
    d = lax.axis_index("dp")
    h = lax.axis_index("head")
    h1 = h.reshape(1)
    ids = jnp.stack([h, h ^ 2]).astype(jnp.int32)
    seqs = memory.shape[0]
    rows = w_key.shape[0]
    out_rows = w_out.shape[0]
    share, up_share = content_bias.shape[0], up_bias.shape[0]
    values = 4 * share + up_share
    sources = ring_sources(d, n_dp)
    pick = lambda a, n, axis: lax.dynamic_index_in_dim(a, n, axis, keepdims=False)

    ring = RingGather(
        pack(w_key, w_value, w_query, w_out, (content_bias, ln_gain, ln_bias, down_bias, up_bias)), n_dp)
    i = jnp.arange(SEG, dtype=jnp.int32)[None, :]
    j = jnp.arange(2 * SEG, dtype=jnp.int32)[:, None]
    gap = i + SEG - j
    near = jnp.where(gap >= 0, jnp.log1p(jnp.maximum(gap, 0).astype(F32)), FAR)

    def far_of(s):
        age, valid = pick(slot_age, s, 0)[:, None], pick(slot_valid, s, 0)[:, None]
        return jnp.where(valid > 0, jnp.log1p(jnp.maximum(i + age, 0).astype(F32)), FAR)

    far = [far_of(h), far_of(h ^ 2)]
    heads = jnp.concatenate([2 * h + jnp.arange(2), 2 * (h ^ 1) + jnp.arange(2)])
    slopes = 0.6 * jnp.power(0.7, heads.astype(F32))
    ffn_chunk = jnp.concatenate([w_up, w_down.T])

    inputs_x = x_swap(inputs)
    ring.step()
    ring.step(near)
    ring.step((far, slopes, ffn_chunk, sources))
    ring.step(inputs_x)
    chunks = ring.finish()

    def first_moves(index, ins, outs):
        for k in range(n_dp):
            at = pl.multiple_of(index[k] * rows, rows)
            yield ins[k].at[pl.ds(0, rows), pl.ds(0, 6 * HD)], outs[0].at[pl.ds(at, rows)]
            yield ins[k].at[pl.ds(0, rows), pl.ds(6 * HD, 2 * HD)], outs[1].at[index[k]]
            yield ins[k].at[pl.ds(rows, 16), pl.ds(0, 2 * HD)], outs[2].at[index[k]]

    w_own, wo, small = copies(first_moves, [(D, 6 * HD), (n_dp, rows, 2 * HD), (n_dp, 16, 2 * HD)], sources, *chunks)
    small = small[:, :1, :values]
    cc, xx = h % 2, h // 2
    small_c = c_swap(small)
    small = jnp.where(cc == 0, jnp.concatenate([small, small_c], axis=1), jnp.concatenate([small_c, small], axis=1))
    small_x = x_swap(small)
    small = jnp.where(xx == 0, jnp.concatenate([small, small_x], axis=1), jnp.concatenate([small_x, small], axis=1))
    small = small.reshape(4 * n_dp, values).astype(F32)
    w_par = c_swap(w_own)
    cot_x = x_swap(after(small_x, cotangent))
    wo = wo.reshape(n_dp, 4, out_rows, 2 * HD)
    wo_x = x_swap(wo)
    wo4 = (wo, c_swap(wo), wo_x, c_swap(wo_x))
    ffn = RingGather(ffn_chunk, n_dp)
    ffn.step(w_own)

    bias_all = small[:, :share].reshape(4, 2 * HD)
    gain = small[:, share:2 * share].reshape(1, D)
    shift = small[:, 2 * share:3 * share].reshape(1, D)
    down_shift = small[:, 3 * share:4 * share].reshape(1, D)
    up_shift = small[:, 4 * share:].reshape(4, D)
    two = lambda a: jnp.concatenate([pick(a, h, 0), pick(a, h ^ 1, 0)]).reshape(1, -1)
    bias, up_shift = two(bias_all), two(up_shift)

    kv, q = project(ids, compressed, memory, inputs, inputs_x, w_own, w_par)
    ffn.step(kv)
    bias = after((gain, shift, down_shift, up_shift), bias)
    mixed_x, lse_x = attend(1, slopes, q, bias, kv, near, far[1])
    ffn.step(mixed_x)
    sent = x_swap(mixed_x)
    q0 = after(cot_x, q)
    mixed, lse = attend(0, slopes, q0, bias, kv, near, far[0])
    ffn.step(mixed)
    chunks = ffn.finish()

    ffn_par = [c_swap(chunk) for chunk in chunks]
    per = n_dp // 4

    def wo_moves(index, ins, outs):
        me = index[0]
        for e in range(4):
            for b in range(4):
                for p in range(4):
                    target = outs[0].at[me ^ b, :, me ^ e, :, pl.ds(p * 2 * HD, 2 * HD)]
                    yield ins[e].at[pl.ds(b * per, per), p], target

    (w_o,) = copies(wo_moves, [(4, per, 4, out_rows, D)], h1, *wo4)
    w_o = w_o.reshape(D, D)

    residual, normed = attention_out(mixed, sent, w_o, inputs, gain, shift)
    normed_x = x_swap(normed)
    hid, gb, up_cols, branch, gn = feed_forward(n_dp, sources, normed, cotangent, up_shift, chunks, ffn_par, F32)

    other = (c_swap(inputs), c_swap(inputs_x))

    def memory_moves(index, ins, outs):
        me = index[0]
        yield ins[0], outs[0].at[me]
        yield ins[1], outs[0].at[me ^ 2]
        yield ins[2], outs[0].at[me ^ 1]
        yield ins[3], outs[0].at[me ^ 3]

    (new_memory,) = copies(memory_moves, [(seqs, SEG, D)], h1, inputs, inputs_x, *other)
    comp_w = lax.all_gather(after(mixed, w_comp), "dp", axis=0).reshape(n_dp, RATE, rows, 2 * HD)
    new_compressed = compress(h1, memory, compressed, comp_w, comp_bias)

    hid_x, gb_x, up_cols_x, branch_x, gn_x = feed_forward(n_dp, sources, normed_x, cot_x, up_shift, chunks, ffn_par, BF)
    gn_x = x_swap(gn_x)
    branch_x = x_swap(after(gn_x, branch_x))
    acts = ((normed, normed_x), (cotangent, cot_x), (gb, gb_x), (hid, hid_x))
    from_par = [c_swap(a) for a in ffn_grads(1, n_dp, *acts)]
    from_par = after((new_compressed, new_memory), *from_par)
    ffn_sum = RingScatter(ffn_grads(0, n_dp, *acts, *from_par).reshape(n_dp, 2 * rows, D), d, n_dp)
    gn_x = after(ffn_sum.f, gn_x)
    ffn_sum.step()
    grad_residual, do, do_x, sums, g_out = norm_back(h1, residual, gn, gn_x, cotangent, gain, mixed, sent, w_o)
    do = after((ffn_sum.f, ffn_sum.b), do)
    ffn_sum.step(do)
    do_x = x_swap(do_x)
    g_out = g_out.reshape(n_dp, 2, 2, out_rows, D)
    g_out = (pick(g_out, cc, 2).astype(F32) + c_swap(pick(g_out, 1 - cc, 2)).astype(F32)).astype(BF)
    g_out = (pick(g_out, xx, 1).astype(F32) + x_swap(pick(g_out, 1 - xx, 1)).astype(F32)).astype(BF)
    dq, dkv, q_cols = attend_back(0, slopes, q, bias, kv, near, far[0], mixed, lse, do)
    do_x = after((ffn_sum.f, ffn_sum.b), do_x)
    ffn_sum.step(dq)
    branch_x = after(dq, branch_x)
    output = add_up(BF, residual, branch, branch_x, down_shift)
    term = token_term(dq, dkv, w_own, w_par, grad_residual)
    dq_x, dkv_x, q_cols_x = attend_back(1, slopes, q, bias, kv, near, far[1], mixed_x, lse_x, do_x)
    dkv = after((ffn_sum.f, ffn_sum.b), dkv)
    ffn_sum.step(dq_x)
    out_sum = RingScatter(g_out, d, n_dp)
    out_sum.step(dq_x)
    term_x = x_swap(token_term(dq_x, dkv_x, w_own, w_par))
    grad_input = add_up(F32, term, term_x)

    lane = jnp.arange(4)[:, None]

    def place(a):
        a = a.reshape(2, 1, -1)
        return jnp.where(lane == h, a[0], 0.0) + jnp.where(lane == h ^ 1, a[1], 0.0)

    tiny = jnp.concatenate([
        place(q_cols + q_cols_x).reshape(-1, share),
        sums[0].reshape(-1, share),
        sums[1].reshape(-1, share),
        sums[2].reshape(-1, share),
        place(up_cols + up_cols_x).reshape(-1, up_share),
    ], axis=1)
    tiny = tiny + x_swap(tiny)
    tiny = tiny + c_swap(tiny)
    tiny = jnp.pad(tiny.astype(BF).reshape(n_dp, 4, values), ((0, 0), (0, 12), (0, 6 * HD - values)))

    work = (ids, compressed, memory, inputs, inputs_x, (dkv, dkv_x), (dq, dq_x))
    from_par = weight_grads(1, n_dp, *work)
    out_sum.step(from_par)
    from_par = after(ffn_sum.f, *[c_swap(a) for a in from_par])
    ffn_sum = ffn_sum.finish()
    grad_up, grad_down = ffn_sum[:rows], ffn_sum[rows:].T
    g_sum = RingScatter(weight_grads(0, n_dp, *work, *from_par, tiny), d, n_dp)
    g_sum.step()
    out_sum.step(g_sum.f)
    g_sum.step(out_sum.f)
    grad_out = out_sum.finish()
    g_sum = g_sum.finish()
    tiny = pick(g_sum[rows:], h, 0)
    g_sum = g_sum[:rows]
    grad_key = jnp.concatenate([g_sum[:, :HD], g_sum[:, 2 * HD:3 * HD]], axis=1)
    grad_value = jnp.concatenate([g_sum[:, HD:2 * HD], g_sum[:, 3 * HD:4 * HD]], axis=1)
    grad_query = g_sum[:, 4 * HD:]

    return (
        output,
        grad_input,
        grad_query,
        grad_key,
        grad_value,
        tiny[:share],
        grad_out,
        tiny[share:2 * share],
        tiny[2 * share:3 * share],
        grad_up,
        tiny[4 * share:values],
        grad_down,
        tiny[3 * share:4 * share],
        new_memory,
        new_compressed,
    )


def solution(mesh):
    both = ("dp", "head")
    in_specs = (
        P(both, None),
        P("dp", None, None),
        P("dp", None, None),
        P("dp", None),
        P("dp", None),
        P("dp", "head"),
        P("dp", "head"),
        P("dp", "head"),
        P(both),
        P(both, None),
        P(both),
        P(both),
        P("dp", "head"),
        P(both),
        P("head", "dp"),
        P(both),
        P(None, "dp", "head"),
        P("head"),
        P(both, None),
    )
    out_specs = (
        P(both, None),
        P(both, None),
        P("dp", "head"),
        P("dp", "head"),
        P("dp", "head"),
        P(both),
        P(both, None),
        P(both),
        P(both),
        P("dp", "head"),
        P(both),
        P("head", "dp"),
        P(both),
        P("dp", None, None),
        P("dp", None, "head"),
    )
    return jax.shard_map(per_device, mesh=mesh, in_specs=in_specs, out_specs=out_specs, check_vma=False)
```

```python
import functools

import jax
import jax.numpy as jnp
from jax import lax
from jax.experimental import pallas as pl
from jax.experimental.pallas import tpu as pltpu
from jax.sharding import PartitionSpec as P

D = 1024
HD = 128
SEG = 512
CM = 512
RATE = 3
CC = 171
LN_EPS = 1e-05
LOG2E = 1.4426950408889634
SCALE2 = LOG2E * HD ** (-0.5)
FAR = 1e32
VMEM = 56 * 1024 * 1024
BF = jnp.bfloat16
F32 = jnp.float32


def nt(a, b):
    return lax.dot_general(a, b, (((1,), (1,)), ((), ())), preferred_element_type=F32)


def tn(a, b):
    return lax.dot_general(a, b, (((0,), (0,)), ((), ())), preferred_element_type=F32)


def nn(a, b):
    return jnp.dot(a, b, preferred_element_type=F32)


def x_swap(a):
    return lax.ppermute(a, "head", [(i, i ^ 2) for i in range(4)])


def c_swap(a):
    return lax.ppermute(a, "head", [(i, i ^ 1) for i in range(4)])


def fwd_kernel(slope_ref, q_ref, bias_ref, kv_ref, near_ref, far_ref, mixed_ref, lse_ref):
    a = pl.program_id(0)
    slope2 = slope_ref[a] * LOG2E
    q = (q_ref[0] + bias_ref[...]).astype(BF)
    parts = []
    for n in range(3):
        k = kv_ref[0, n * SEG:(n + 1) * SEG, :HD]
        table = far_ref[...] if n == 0 else near_ref[(n - 1) * SEG:n * SEG, :]
        parts.append(nt(k, q) * SCALE2 - slope2 * table)
    top = jnp.maximum(jnp.maximum(jnp.max(parts[0], axis=0, keepdims=True), jnp.max(parts[1], axis=0, keepdims=True)),
                      jnp.max(parts[2], axis=0, keepdims=True))
    total = jnp.zeros((1, SEG), F32)
    acc = jnp.zeros((HD, SEG), F32)
    for n in range(3):
        p = jnp.exp2(parts[n] - top)
        total = total + jnp.sum(p, axis=0, keepdims=True)
        acc = acc + tn(kv_ref[0, n * SEG:(n + 1) * SEG, HD:], p.astype(BF))
    mixed_ref[...] = (acc / total).T.astype(BF)
    lse_ref[...] = (top + jnp.log2(total)).reshape(1, 1, SEG)


def bwd_kernel(slope_ref, q_ref, bias_ref, kv_ref, near_ref, far_ref, mixed_ref, lse_ref, do_ref, dq_ref, dkv_ref, sum_ref):
    a = pl.program_id(0)
    slope2 = slope_ref[a] * LOG2E
    q = (q_ref[0] + bias_ref[...]).astype(BF)
    do = do_ref[...]
    lse = lse_ref[...].reshape(1, SEG)
    row_dot = jnp.sum((do.astype(F32) * mixed_ref[...].astype(F32)).T, axis=0, keepdims=True)
    inv_root = HD ** (-0.5)
    dq = jnp.zeros((HD, SEG), F32)
    for n in range(3):
        rows = slice(n * SEG, (n + 1) * SEG)
        k = kv_ref[0, rows, :HD]
        v = kv_ref[0, rows, HD:]
        table = far_ref[...] if n == 0 else near_ref[(n - 1) * SEG:n * SEG, :]
        p = jnp.exp2(nt(k, q) * SCALE2 - slope2 * table - lse)
        ds = (p * (nt(v, do) - row_dot)).astype(BF)
        dkv_ref[rows, HD:] = nn(p.astype(BF), do).astype(BF)
        dkv_ref[rows, :HD] = (nn(ds, q) * inv_root).astype(BF)
        dq = dq + tn(k, ds)
    dq = (dq.T * inv_root).astype(BF)
    dq_ref[...] = dq
    sum_ref[...] = jnp.sum(dq.astype(F32), axis=0, keepdims=True)


def ring_order(n):
    up = list(range(0, n, 2))
    return up + [p + 1 for p in reversed(up)]


def ring_perms(n):
    order = ring_order(n)
    ahead = [(order[p], order[(p + 1) % n]) for p in range(n)]
    return ahead, [(b, a) for a, b in ahead]


def ring_place(d, n):
    return jnp.where(d % 2 == 0, d // 2, n - 1 - d // 2)


def ring_member(p, n):
    p = p % n
    return jnp.where(p < n // 2, 2 * p, 2 * (n - 1 - p) + 1)


def after(first, *then):
    out = lax.optimization_barrier((first,) + then)[1:]
    return out if len(then) > 1 else out[0]


class RingGather:
    def __init__(self, chunk, n):
        self.n, self.k = n, 0
        self.ahead, self.back = ring_perms(n)
        self.f = self.b = chunk
        self.chunks = [chunk]

    def step(self, first=None):
        self.k += 1
        if self.k > self.n // 2:
            return
        if first is not None:
            self.f, self.b = after(first, self.f, self.b)
        self.f = lax.ppermute(self.f, "dp", self.ahead)
        self.chunks.append(self.f)
        if self.k < self.n - self.n // 2:
            self.b = lax.ppermute(self.b, "dp", self.back)
            self.chunks.append(self.b)

    def finish(self):
        while self.k < self.n // 2:
            self.step()
        return self.chunks


def ring_sources(d, n):
    place = ring_place(d, n)
    steps = [0]
    for k in range(1, n // 2 + 1):
        steps.append(-k)
        if k < n - n // 2:
            steps.append(k)
    return ring_member(place + jnp.array(steps, jnp.int32), n).astype(jnp.int32)


ROWS = 3 * SEG
HALF = D // 2
smem_spec = pl.BlockSpec(memory_space=pltpu.SMEM)
vmem_spec = pl.BlockSpec(memory_space=pltpu.VMEM)
any_spec = pl.BlockSpec(memory_space=pl.ANY)


def params():
    return pltpu.CompilerParams(vmem_limit_bytes=VMEM)


def cost(us):
    return pl.CostEstimate(flops=int(us * 0.18e9), bytes_accessed=1, transcendentals=0)


def shape(*dims, kind=BF):
    return jax.ShapeDtypeStruct(dims, kind)


def whole(*dims):
    return pl.BlockSpec(dims, lambda *i: (0,) * len(dims))


def attend(t, slopes, q, bias, kv, near, far):
    return pl.pallas_call(
        fwd_kernel,
        grid=(4,),
        in_specs=[
            smem_spec,
            pl.BlockSpec((1, SEG, HD), lambda a: (t, 0, a)),
            pl.BlockSpec((1, HD), lambda a: (0, a)),
            pl.BlockSpec((1, ROWS, 2 * HD), lambda a: (t, 0, a)),
            whole(2 * SEG, SEG),
            whole(SEG, SEG),
        ],
        out_specs=[pl.BlockSpec((SEG, HD), lambda a: (0, a)), pl.BlockSpec((1, 1, SEG), lambda a: (a, 0, 0))],
        out_shape=[shape(SEG, HALF), shape(4, 1, SEG, kind=F32)],
        compiler_params=params(),
        cost_estimate=cost(9),
    )(slopes, q, bias, kv, near, far)


def attend_back(t, slopes, q, bias, kv, near, far, mixed, lse, do):
    column = pl.BlockSpec((SEG, HD), lambda a: (0, a))
    return pl.pallas_call(
        bwd_kernel,
        grid=(4,),
        in_specs=[
            smem_spec,
            pl.BlockSpec((1, SEG, HD), lambda a: (t, 0, a)),
            pl.BlockSpec((1, HD), lambda a: (0, a)),
            pl.BlockSpec((1, ROWS, 2 * HD), lambda a: (t, 0, a)),
            whole(2 * SEG, SEG),
            whole(SEG, SEG),
            column,
            pl.BlockSpec((1, 1, SEG), lambda a: (a, 0, 0)),
            column,
        ],
        out_specs=[column, pl.BlockSpec((ROWS, 2 * HD), lambda a: (0, a)), pl.BlockSpec((1, HD), lambda a: (0, a))],
        out_shape=[shape(SEG, HALF), shape(ROWS, D), shape(1, HALF, kind=F32)],
        compiler_params=params(),
        cost_estimate=cost(12),
    )(slopes, q, bias, kv, near, far, mixed, lse, do)


def pack_kernel(key_ref, value_ref, query_ref, out_ref, *rest):
    smalls, pack_ref = rest[:-1], rest[-1]
    rows = key_ref.shape[0]
    piece = out_ref.shape[0]
    pack_ref[:rows, :HD] = key_ref[:, :HD]
    pack_ref[:rows, HD:2 * HD] = value_ref[:, :HD]
    pack_ref[:rows, 2 * HD:3 * HD] = key_ref[:, HD:]
    pack_ref[:rows, 3 * HD:4 * HD] = value_ref[:, HD:]
    pack_ref[:rows, 4 * HD:6 * HD] = query_ref[...]
    for k in range(4):
        pack_ref[k * piece:(k + 1) * piece, 6 * HD:] = out_ref[:, k * 2 * HD:(k + 1) * 2 * HD]
    line = jnp.concatenate([a[...].astype(F32) for a in smalls], axis=1)
    line = jnp.concatenate([line, jnp.zeros((1, D - line.shape[1]), F32)], axis=1)
    row = lax.broadcasted_iota(jnp.int32, (16, D), 0)
    pack_ref[rows:] = jnp.where(row == 0, jnp.broadcast_to(line, (16, D)), 0.0).astype(BF)


def pack(w_key, w_value, w_query, w_out, smalls):
    return pl.pallas_call(
        pack_kernel,
        in_specs=[vmem_spec] * (4 + len(smalls)),
        out_specs=vmem_spec,
        out_shape=shape(w_key.shape[0] + 16, D),
        compiler_params=params(),
        cost_estimate=cost(1),
    )(w_key, w_value, w_query, w_out, *[a.reshape(1, -1) for a in smalls])


def project_kernel(id_ref, comp_ref, mem_ref, token_ref, w_own_ref, w_par_ref, kv_ref, q_ref, source, own, par, sems):
    n = pl.program_id(0)
    blocks = (comp_ref.at[id_ref[0]], mem_ref.at[id_ref[0]], token_ref)
    moves = [pltpu.make_async_copy(a, source.at[k], sems.at[k]) for k, a in enumerate(blocks)]
    own_move = pltpu.make_async_copy(w_own_ref, own, sems.at[3])
    par_move = pltpu.make_async_copy(w_par_ref, par, sems.at[4])

    @pl.when(n == 0)
    def _():
        own_move.start()
        moves[0].start()
        par_move.start()
        moves[1].start()
        moves[2].start()
        own_move.wait()

    for k in range(3):
        pl.when(n == k)(moves[k].wait)
    a = source[n]
    kv_ref[0, :, :HALF] = nn(a, own[:, :HALF]).astype(BF)
    pl.when(n == 0)(par_move.wait)
    kv_ref[0, :, HALF:] = nn(a, par[:, :HALF]).astype(BF)

    @pl.when(n == 2)
    def _():
        q_ref[0, :, :2 * HD] = nn(a, own[:, HALF:])
        q_ref[0, :, 2 * HD:] = nn(a, par[:, HALF:])


def project(seq, compressed, memory, tokens, w_own, w_par):
    return pl.pallas_call(
        project_kernel,
        grid_spec=pltpu.PrefetchScalarGridSpec(
            num_scalar_prefetch=1,
            grid=(3,),
            in_specs=[any_spec] * 5,
            out_specs=[
                pl.BlockSpec((1, SEG, D), lambda n, seq: (0, n, 0)),
                pl.BlockSpec((1, SEG, HALF), lambda n, seq: (0, 0, 0)),
            ],
            scratch_shapes=[
                pltpu.VMEM((3, SEG, D), BF),
                pltpu.VMEM((D, 6 * HD), BF),
                pltpu.VMEM((D, 6 * HD), BF),
                pltpu.SemaphoreType.DMA((5,)),
            ],
        ),
        out_shape=[shape(1, ROWS, D), shape(1, SEG, HALF, kind=F32)],
        compiler_params=params(),
        cost_estimate=cost(8),
    )(seq.reshape(1), compressed, memory, tokens, w_own, w_par)


def norm_kernel(mixed_ref, sent_ref, w_ref, in_ref, lines_ref, residual_ref, normed_ref):
    out = nn(mixed_ref[...], w_ref[:HALF]) + nn(sent_ref[...], w_ref[HALF:])
    residual = in_ref[...].astype(F32) + out
    residual_ref[...] = residual
    center = residual - jnp.mean(residual, axis=-1, keepdims=True)
    rstd = lax.rsqrt(jnp.mean(center * center, axis=-1, keepdims=True) + LN_EPS)
    normed_ref[...] = (center * rstd * lines_ref[0:1] + lines_ref[1:2]).astype(BF)


def attention_out(mixed, sent, w_o, inputs, lines):
    rows = SEG // 2
    half = pl.BlockSpec((rows, HALF), lambda i: (i, 0))
    full = pl.BlockSpec((rows, D), lambda i: (i, 0))
    return pl.pallas_call(
        norm_kernel,
        grid=(2,),
        in_specs=[half, half, whole(D, D), full, whole(3, D)],
        out_specs=[full, full],
        out_shape=[shape(SEG, D, kind=F32), shape(SEG, D)],
        compiler_params=params(),
        cost_estimate=cost(4),
    )(mixed, sent, w_o, inputs, lines)


def gelu_pair(before):
    c0, c1 = 0.7978845608028654, 0.044715
    sq = before * before
    t = jnp.tanh(c0 * before * (1.0 + c1 * sq))
    half = 0.5 * (1.0 + t)
    return before * half, half + 0.5 * before * (1.0 - t * t) * (c0 * (1.0 + 3.0 * c1 * sq))


def ffn_kernel(n_dp, index_ref, norm_ref, low_ref, high_ref, bias_ref, *refs):
    chunks = refs[:2 * n_dp]
    hid_ref, gb_ref, sum_ref, branch_ref, gn_ref, up_ref, down_ref, branch, gn, sems = refs[2 * n_dp:]
    i, tiles = pl.program_id(0), up_ref.shape[0]
    tile, rows = up_ref.shape[2], D // n_dp

    def moves(step):
        group, column = divmod(step, tiles // 2)
        for k in range(n_dp):
            source = chunks[group * n_dp + k]
            at = pl.ds(pl.multiple_of(index_ref[k] * rows, rows), rows)
            for m, target in enumerate((up_ref, down_ref)):
                yield pltpu.make_async_copy(
                    source.at[pl.ds(m * rows, rows), pl.ds(column * tile, tile)],
                    target.at[step, at],
                    sems.at[(step * n_dp + k) * 2 + m],
                )

    @pl.when(i == 0)
    def _():
        for step in range(tiles):
            for move in moves(step):
                move.start()

    for step in range(tiles):
        @pl.when(i == step)
        def _(step=step):
            for move in moves(step):
                move.wait()

    up, down = up_ref.at[i], down_ref.at[i]
    before = nn(norm_ref[...], up[...]) + bias_ref[...]
    act, slope = gelu_pair(before)
    act = act.astype(BF)
    back = jnp.concatenate([nn(low_ref[...], down[...]), nn(high_ref[...], down[...])])
    gb = (back * slope).astype(BF)
    hid_ref[...] = act
    gb_ref[...] = gb
    sum_ref[...] = jnp.sum(gb.astype(F32), axis=0, keepdims=True)

    @pl.when(i == 0)
    def _():
        branch[...] = nt(act, down[...])
        gn[...] = nt(gb, up[...])

    @pl.when(i > 0)
    def _():
        branch[...] += nt(act, down[...])
        gn[...] += nt(gb, up[...])

    @pl.when(i == tiles - 1)
    def _():
        branch_ref[...] = branch[...].astype(branch_ref.dtype)
        gn_ref[...] = gn[...].astype(gn_ref.dtype)


def feed_forward(n_dp, sources, norm, cot, bias, own, par, kind, tile=512):
    tiles = 2 * D // tile
    part = pl.BlockSpec((SEG, tile), lambda i, index: (0, i))
    line = pl.BlockSpec((1, tile), lambda i, index: (0, i))
    return pl.pallas_call(
        functools.partial(ffn_kernel, n_dp),
        grid_spec=pltpu.PrefetchScalarGridSpec(
            num_scalar_prefetch=1,
            grid=(tiles,),
            in_specs=[whole(SEG, D), whole(SEG // 2, D), whole(SEG // 2, D), line] + [any_spec] * (2 * n_dp),
            out_specs=[part, part, line, whole(SEG, D), whole(SEG, D)],
            scratch_shapes=[pltpu.VMEM((tiles, D, tile), BF)] * 2
            + [pltpu.VMEM((SEG, D), F32)] * 2
            + [pltpu.SemaphoreType.DMA((2 * tiles * n_dp,))],
        ),
        out_shape=[shape(SEG, 2 * D), shape(SEG, 2 * D), shape(1, 2 * D, kind=F32), shape(SEG, D, kind=kind), shape(SEG, D, kind=kind)],
        compiler_params=params(),
        cost_estimate=cost(16),
    )(sources, norm, *cot, bias, *own, *par)


def ffn_grad_kernel(tiles, n0, n1, c0_low, c0_high, c1_low, c1_high, gb0, gb1, hid0, hid1, *rest):
    parts, outs = (rest[:-1], rest[-1:]) if len(rest) > 2 * tiles else ((), rest)
    step = pl.program_id(0) * tiles + pl.program_id(1)
    for m in range(2):
        for i in range(tiles):
            k = m * tiles + i

            @pl.when(step == k)
            def _(m=m, k=k):
                if m == 0:
                    total = tn(n0[...], gb0[...]) + tn(n1[...], gb1[...])
                else:
                    half = SEG // 2
                    total = tn(c0_low[...], hid0[:half]) + tn(c0_high[...], hid0[half:])
                    total = total + tn(c1_low[...], hid1[:half]) + tn(c1_high[...], hid1[half:])
                if parts:
                    out = outs[0]
                    total = total.reshape(out.shape[0], out.shape[2], -1)
                    out[:, 0] = (total + parts[k][...].astype(F32)).astype(BF)
                else:
                    outs[k][...] = total.reshape(outs[k].shape).astype(BF)


def ffn_grads(g, n_dp, norms, cots, gbs, hids, *received, tile=512):
    n = D // tile
    rows = D // n_dp
    tokens = whole(SEG, D)
    early = pl.BlockSpec((SEG, tile), lambda m, i: (0, g * n + jnp.where(m == 0, i, n - 1)))
    late = pl.BlockSpec((SEG, tile), lambda m, i: (0, g * n + jnp.where(m == 0, 0, i)))
    part = whole(n_dp, rows, tile)
    if received:
        out_specs = pl.BlockSpec((n_dp, 1, rows, tile), lambda m, i: (0, m, 0, i))
        out_shape = shape(n_dp, 2, rows, D)
    else:
        out_specs, out_shape = [part] * (2 * n), [shape(n_dp, rows, tile)] * (2 * n)
    return pl.pallas_call(
        functools.partial(ffn_grad_kernel, n),
        grid=(2, n),
        in_specs=[tokens] * 2 + [whole(SEG // 2, D)] * 4 + [early] * 2 + [late] * 2 + [part] * len(received),
        out_specs=out_specs,
        out_shape=out_shape,
        compiler_params=params(),
        cost_estimate=cost(10),
    )(*norms, *cots, *gbs, *hids, *received)


def norm_back_kernel(h_ref, residual_ref, gn_ref, gnx_ref, cot_ref, lines_ref, mixed_ref, sent_ref, w_ref,
                     grad_ref, keep_ref, send_ref, sums_ref, mine_ref, theirs_ref, acc):
    i = pl.program_id(0)
    residual = residual_ref[...]
    center = residual - jnp.mean(residual, axis=-1, keepdims=True)
    rstd = lax.rsqrt(jnp.mean(center * center, axis=-1, keepdims=True) + LN_EPS)
    xhat = center * rstd
    gn = gn_ref[...] + gnx_ref[...].astype(F32)
    g = gn * lines_ref[0:1]
    cot = cot_ref[...].astype(F32)
    grad = cot + rstd * (g - jnp.mean(g, axis=-1, keepdims=True) - xhat * jnp.mean(g * xhat, axis=-1, keepdims=True))
    grad_ref[...] = grad
    low = grad.astype(BF)
    keep_ref[...] = nt(low, w_ref[:HALF]).astype(BF)
    send_ref[...] = nt(low, w_ref[HALF:]).astype(BF)
    total = lambda a: jnp.sum(a, axis=0, keepdims=True)
    sums = jnp.concatenate([total(gn * xhat), total(gn), total(cot)], axis=0)

    @pl.when(i == 0)
    def _():
        sums_ref[...] = sums
        acc[:HALF] = tn(mixed_ref[...], low)
        acc[HALF:] = tn(sent_ref[...], low)

    @pl.when(i > 0)
    def _():
        sums_ref[...] += sums
        acc[:HALF] += tn(mixed_ref[...], low)
        acc[HALF:] += tn(sent_ref[...], low)

    @pl.when(i == pl.num_programs(0) - 1)
    def _():
        per = mine_ref.shape[0] // 4
        first = h_ref[0] % 2 == 0
        for b in range(4):
            block = acc[b * 2 * HD:(b + 1) * 2 * HD].reshape(per, 2, 2, mine_ref.shape[2], D)
            at = pl.ds((h_ref[0] ^ b) * per, per)
            mine_ref[at] = jnp.where(first, block[:, :, 0], block[:, :, 1]).astype(BF)
            theirs_ref[at] = jnp.where(first, block[:, :, 1], block[:, :, 0]).astype(BF)


def out_half_kernel(h_ref, mine_ref, got_ref, keep_ref, send_ref):
    total = mine_ref[...].astype(F32) + got_ref[...].astype(F32)
    first = h_ref[0] // 2 == 0
    keep_ref[...] = jnp.where(first, total[:, 0], total[:, 1]).astype(BF)
    send_ref[...] = jnp.where(first, total[:, 1], total[:, 0]).astype(BF)


def out_half(h, mine, got):
    n_dp, _, rows, _ = mine.shape
    return pl.pallas_call(
        out_half_kernel,
        in_specs=[smem_spec, vmem_spec, vmem_spec],
        out_specs=[vmem_spec, vmem_spec],
        out_shape=[shape(n_dp, rows, D)] * 2,
        compiler_params=pltpu.CompilerParams(vmem_limit_bytes=16 << 20),
        cost_estimate=cost(1),
    )(h, mine, got)


def norm_back(n_dp, h, residual, gn, gnx, cot, gain, mixed, sent, w_o):
    rows = SEG // 2
    half = pl.BlockSpec((rows, HALF), lambda i: (i, 0))
    full = pl.BlockSpec((rows, D), lambda i: (i, 0))
    return pl.pallas_call(
        norm_back_kernel,
        grid=(2,),
        in_specs=[smem_spec, full, full, full, full, whole(3, D), half, half, whole(D, D)],
        out_specs=[full, half, half, whole(3, D)] + [whole(n_dp, 2, D // n_dp // 4, D)] * 2,
        out_shape=[shape(SEG, D, kind=F32), shape(SEG, HALF), shape(SEG, HALF), shape(3, D, kind=F32)] + [shape(n_dp, 2, D // n_dp // 4, D)] * 2,
        scratch_shapes=[pltpu.VMEM((D, D), F32)],
        compiler_params=params(),
        cost_estimate=cost(10),
    )(h, residual, gn, gnx, cot, gain, mixed, sent, w_o)


def term_kernel(dq_ref, dkv_ref, w_own_ref, w_par_ref, *rest):
    out = nt(dkv_ref[:, :HALF], w_own_ref[:, :HALF]) + nt(dkv_ref[:, HALF:], w_par_ref[:, :HALF])
    out = out + nt(dq_ref[:, :2 * HD], w_own_ref[:, HALF:]) + nt(dq_ref[:, 2 * HD:], w_par_ref[:, HALF:])
    if len(rest) > 1:
        out = out + rest[0][...]
    rest[-1][...] = out.astype(rest[-1].dtype)


def token_term(dq, dkv, w_own, w_par, *residual):
    rows = SEG // 2
    full = pl.BlockSpec((rows, D), lambda i: (i, 0))
    weight = whole(D, 3 * 2 * HD)
    return pl.pallas_call(
        term_kernel,
        grid=(2,),
        in_specs=[
            pl.BlockSpec((rows, HALF), lambda i: (i, 0)),
            pl.BlockSpec((rows, D), lambda i: (4 + i, 0)),
            weight,
            weight,
        ] + [full] * len(residual),
        out_specs=full,
        out_shape=shape(SEG, D, kind=F32 if residual else BF),
        compiler_params=params(),
        cost_estimate=cost(4),
    )(dq, dkv, w_own, w_par, *residual)


def weight_grad_kernel(g, ids_ref, comp_ref, mem_ref, own_ref, other_ref, dkv0, dkv1, dq0, dq1, *rest):
    step = pl.program_id(0)
    source, grads, query_grads, acc, sems = rest[-5:]
    parts, outs = (rest[:2], rest[5:6]) if len(rest) > 8 else ((), rest[:2])
    half = rest[0].shape[0]
    rows = D // (2 * half)
    blocks = []
    for t, (tokens, dkv) in enumerate(((own_ref, dkv0), (other_ref, dkv1))):
        for n, a in enumerate((comp_ref.at[ids_ref[t]], mem_ref.at[ids_ref[t]], tokens)):
            blocks.append((a, dkv.at[pl.ds(n * SEG, SEG), pl.ds(g * HALF, HALF)]))
    moves = [
        (pltpu.make_async_copy(a, source.at[k], sems.at[2 * k]), pltpu.make_async_copy(b, grads.at[k], sems.at[2 * k + 1]))
        for k, (a, b) in enumerate(blocks)
    ]
    extra = [
        pltpu.make_async_copy(a.at[:, pl.ds(g * 2 * HD, 2 * HD)], query_grads.at[k], sems.at[12 + k])
        for k, a in enumerate((dq0, dq1))
    ]

    @pl.when(step == 0)
    def _():
        for pair in moves:
            pair[0].start()
            pair[1].start()
        extra[0].start()
        extra[1].start()

    for k in range(6):
        @pl.when(step == k)
        def _(k=k):
            moves[k][0].wait()
            moves[k][1].wait()
            if k == 0:
                acc[:, :HALF] = tn(source[k], grads[k])
            else:
                acc[:, :HALF] += tn(source[k], grads[k])
            if k == 2:
                extra[0].wait()
                acc[:, HALF:] = tn(source[k], query_grads[0])
            if k < 5:
                return
            extra[1].wait()
            acc[:, HALF:] += tn(source[k], query_grads[1])
            total = acc[...].reshape(2 * half, rows, 6 * HD)
            for p in range(2):
                block = slice(p * half, (p + 1) * half)
                if parts:
                    outs[0][block, :rows] = (total[block] + parts[p][...].astype(F32)).astype(BF)
                else:
                    outs[p][...] = total[block].astype(BF)
            if parts:
                tiny, mine, got = rest[2:5]
                out_rows = mine.shape[1]
                other = (mine[...].astype(F32) + got[...].astype(F32)).astype(BF)
                low = rows + (outs[0].shape[1] - rows) // 2
                outs[0][:, rows:] = jnp.zeros((2 * half, outs[0].shape[1] - rows, 6 * HD), BF)
                outs[0][:, rows:rows + out_rows] = other[:, :, :6 * HD]
                outs[0][:, low:low + out_rows, :2 * HD] = other[:, :, 6 * HD:]
                outs[0][:, low:low + 16, 2 * HD:4 * HD] = tiny[...]


def weight_grads(g, n_dp, ids, compressed, memory, own, other, dkvs, dqs, *received):
    rows = D // n_dp
    if received:
        extra = 2 * max(16, received[-1].shape[1])
        out_specs, out_shape = whole(n_dp, rows + extra, 6 * HD), shape(n_dp, rows + extra, 6 * HD)
    else:
        out_specs, out_shape = [whole(n_dp // 2, rows, 6 * HD)] * 2, [shape(n_dp // 2, rows, 6 * HD)] * 2
    return pl.pallas_call(
        functools.partial(weight_grad_kernel, g),
        grid_spec=pltpu.PrefetchScalarGridSpec(
            num_scalar_prefetch=1,
            grid=(6,),
            in_specs=[any_spec] * 8 + [whole(*a.shape) for a in received],
            out_specs=out_specs,
            scratch_shapes=[
                pltpu.VMEM((6, SEG, D), BF),
                pltpu.VMEM((6, SEG, HALF), BF),
                pltpu.VMEM((2, SEG, 2 * HD), BF),
                pltpu.VMEM((D, 6 * HD), F32),
                pltpu.SemaphoreType.DMA((14,)),
            ],
        ),
        out_shape=out_shape,
        compiler_params=params(),
        cost_estimate=cost(10),
    )(ids, compressed, memory, own, other, *dkvs, *dqs, *received)


def copies(moves, out_shapes, index, *arrays):
    count = len(arrays)

    def kernel(index_ref, *refs):
        ins, outs, sems = refs[:count], refs[count:-1], refs[-1]
        started = []
        for n, (source, target) in enumerate(moves(index_ref, ins, outs)):
            copy = pltpu.make_async_copy(source, target, sems.at[n])
            copy.start()
            started.append(copy)
        for copy in started:
            copy.wait()

    return pl.pallas_call(
        kernel,
        in_specs=[smem_spec] + [any_spec] * count,
        out_specs=[vmem_spec] * len(out_shapes),
        out_shape=[shape(*dims) for dims in out_shapes],
        scratch_shapes=[pltpu.SemaphoreType.DMA((192,))],
        compiler_params=pltpu.CompilerParams(vmem_limit_bytes=16 << 20),
        cost_estimate=cost(0),
    )(index, *arrays)


def assemble(chunks, sources, parts):
    n, cols = len(chunks), chunks[0].shape[1]

    def moves(index, ins, outs):
        for k in range(n):
            row = 0
            for out, rows in zip(outs, parts):
                yield ins[k].at[pl.ds(row, rows)], out.at[pl.ds(pl.multiple_of(index[k] * rows, rows), rows)]
                row += rows

    return copies(moves, [(n * rows, cols) for rows in parts], sources, *chunks)


def pick_kernel(index_ref, ahead_ref, back_ref, f_ref, b_ref):
    f_ref[...] = ahead_ref[0]
    b_ref[...] = back_ref[0]


def add_kernel(index_ref, f_in, b_in, ahead_ref, back_ref, f_ref, b_ref):
    f_ref[...] = (f_in[...].astype(F32) + ahead_ref[0].astype(F32)).astype(BF)
    b_ref[...] = (b_in[...].astype(F32) + back_ref[0].astype(F32)).astype(BF)


def add_one_kernel(index_ref, f_in, ahead_ref, back_ref, f_ref):
    f_ref[...] = (f_in[...].astype(F32) + ahead_ref[0].astype(F32)).astype(BF)


def close_kernel(index_ref, f_in, b_in, own_ref, _, out_ref):
    out_ref[...] = f_in[...].astype(F32) + b_in[...].astype(F32) + own_ref[0].astype(F32)


def close_ffn_kernel(index_ref, f_in, b_in, own_ref, _, up_ref, down_ref):
    total = f_in[...].astype(F32) + b_in[...].astype(F32) + own_ref[0].astype(F32)
    rows = up_ref.shape[0]
    up_ref[...] = total[:rows]
    down_ref[...] = total[rows:].T


def close_last_kernel(index_ref, f_in, b_in, own_ref, _, key_ref, value_ref, query_ref, out_ref, small_ref):
    total = f_in[...].astype(F32) + b_in[...].astype(F32) + own_ref[0].astype(F32)
    rows, out_rows = key_ref.shape[0], out_ref.shape[0]
    low = rows + (total.shape[0] - rows) // 2
    key_ref[:, :HD] = total[:rows, :HD]
    value_ref[:, :HD] = total[:rows, HD:2 * HD]
    key_ref[:, HD:] = total[:rows, 2 * HD:3 * HD]
    value_ref[:, HD:] = total[:rows, 3 * HD:4 * HD]
    query_ref[...] = total[:rows, 4 * HD:]
    out_ref[:, :6 * HD] = total[rows:rows + out_rows]
    out_ref[:, 6 * HD:] = total[low:low + out_rows, :2 * HD]
    small_ref[...] = total[low:low + 16, 2 * HD:4 * HD]


def ring_kernel(kernel, array, places, given, outs):
    _, rows, cols = array.shape
    shapes = [shape(rows, cols)] * outs if isinstance(outs, int) else [shape(*dims, kind=F32) for dims in outs]
    flat = pl.BlockSpec((rows, cols), lambda i, index: (0, 0))
    block = lambda k: pl.BlockSpec((1, rows, cols), lambda i, index: (index[k], 0, 0))
    return pl.pallas_call(
        kernel,
        grid_spec=pltpu.PrefetchScalarGridSpec(
            num_scalar_prefetch=1,
            grid=(1,),
            in_specs=[flat] * len(given) + [block(0), block(1)],
            out_specs=[pl.BlockSpec(a.shape, lambda i, index: (0, 0)) for a in shapes],
        ),
        out_shape=shapes,
        compiler_params=pltpu.CompilerParams(vmem_limit_bytes=16 << 20),
        cost_estimate=cost(2),
    )(places, *given, array, array)


class RingScatter:
    def __init__(self, array, d, n):
        self.array, self.n, self.k = array, n, 0
        self.ahead, self.back = ring_perms(n)
        self.place = ring_place(d, n)
        self.up, self.down = n // 2, n - n // 2 - 1
        self.f, self.b = ring_kernel(pick_kernel, array, self.at(self.up, -self.down), (), 2)

    def at(self, p, q):
        return ring_member(self.place + jnp.array([p, q], jnp.int32), self.n).astype(jnp.int32)

    def step(self, first=None):
        self.k += 1
        k = self.k
        if k > self.up:
            return
        if first is not None:
            self.f, self.b = after(first, self.f, self.b)
        self.f = lax.ppermute(self.f, "dp", self.ahead)
        if k <= self.down:
            self.b = lax.ppermute(self.b, "dp", self.back)
        at = self.at(self.up - k, k - self.down)
        if k < self.down:
            self.f, self.b = ring_kernel(add_kernel, self.array, at, (self.f, self.b), 2)
        elif k < self.up:
            (self.f,) = ring_kernel(add_one_kernel, self.array, at, (self.f,), 1)

    def finish(self, kernel=close_kernel, outs=None):
        while self.k < self.up:
            self.step()
        return ring_kernel(kernel, self.array, self.at(0, 0), (self.f, self.b), outs or [self.array.shape[1:]])


def sum_kernel(*refs):
    total = refs[0][...].astype(F32)
    for ref in refs[1:-1]:
        total = total + ref[...].astype(F32)
    refs[-1][...] = total.astype(refs[-1].dtype)


def add_up(kind, *arrays):
    rows, cols = arrays[0].shape
    specs = [
        pl.BlockSpec((rows // 2, cols), lambda i: (i, 0)) if a.shape[0] == rows else whole(*a.shape) for a in arrays
    ]
    return pl.pallas_call(
        sum_kernel,
        grid=(2,),
        in_specs=specs,
        out_specs=specs[0],
        out_shape=shape(rows, cols, kind=kind),
        compiler_params=params(),
        cost_estimate=cost(3),
    )(*arrays)


def compress_kernel(h_ref, memory_ref, compressed_ref, w_ref, bias_ref, out_ref, weight):
    n_dp, _, rows, width = w_ref.shape

    @pl.when(pl.program_id(0) == 0)
    def _():
        for r in range(RATE):
            for k in range(n_dp):
                weight[r, k * rows:(k + 1) * rows] = w_ref[k, r]

    row = lax.broadcasted_iota(jnp.int32, (176, SEG), 0)
    col = lax.broadcasted_iota(jnp.int32, (176, SEG), 1)
    total = jnp.zeros((176, width), F32)
    for r in range(RATE):
        pick = jnp.where((col == RATE * row + r) & (row < CC), 1.0, 0.0).astype(BF)
        taken = nn(pick, memory_ref[0]).astype(BF)
        total = total + nn(taken, weight[r])
    made = (total + bias_ref[...].astype(F32)).astype(BF)
    to = lax.broadcasted_iota(jnp.int32, (SEG, SEG), 0)
    of = lax.broadcasted_iota(jnp.int32, (SEG, SEG), 1)
    keep = jnp.where(of == to + CC, 1.0, 0.0).astype(BF)
    to = lax.broadcasted_iota(jnp.int32, (SEG, 176), 0)
    of = lax.broadcasted_iota(jnp.int32, (SEG, 176), 1)
    put = jnp.where((of == to - (CM - CC)) & (of < CC), 1.0, 0.0).astype(BF)
    out_ref[0] = (nn(keep, compressed_ref[0]) + nn(put, made)).astype(BF)


def compress(h, memory, compressed, w, bias):
    seqs, width = memory.shape[0], w.shape[3]
    return pl.pallas_call(
        compress_kernel,
        grid_spec=pltpu.PrefetchScalarGridSpec(
            num_scalar_prefetch=1,
            grid=(seqs,),
            in_specs=[
                pl.BlockSpec((1, SEG, D), lambda s, h: (s, 0, 0)),
                pl.BlockSpec((1, CM, width), lambda s, h: (s, 0, h[0])),
                whole(*w.shape),
                whole(1, width),
            ],
            out_specs=pl.BlockSpec((1, CM, width), lambda s, h: (s, 0, 0)),
            scratch_shapes=[pltpu.VMEM((RATE, D, width), BF)],
        ),
        out_shape=shape(seqs, CM, width),
        compiler_params=params(),
        cost_estimate=cost(8),
    )(h, memory, compressed, w, bias.reshape(1, -1))


def per_device(
    inputs,
    memory,
    compressed,
    slot_valid,
    slot_age,
    w_query,
    w_key,
    w_value,
    content_bias,
    w_out,
    ln_gain,
    ln_bias,
    w_up,
    up_bias,
    w_down,
    down_bias,
    w_comp,
    comp_bias,
    cotangent,
):
    n_dp = lax.axis_size("dp")
    d = lax.axis_index("dp")
    h = lax.axis_index("head")
    h1 = h.reshape(1)
    ids = jnp.stack([h, h ^ 2]).astype(jnp.int32)
    seqs = memory.shape[0]
    rows = w_key.shape[0]
    out_rows = w_out.shape[0]
    share, up_share = content_bias.shape[0], up_bias.shape[0]
    values = 4 * share + up_share
    sources = ring_sources(d, n_dp)
    pick = lambda a, n, axis: lax.dynamic_index_in_dim(a, n, axis, keepdims=False)

    ring = RingGather(
        pack(w_key, w_value, w_query, w_out, (content_bias, ln_gain, ln_bias, down_bias, up_bias)), n_dp)
    i = jnp.arange(SEG, dtype=jnp.int32)[None, :]
    j = jnp.arange(2 * SEG, dtype=jnp.int32)[:, None]
    gap = i + SEG - j
    near = jnp.where(gap >= 0, jnp.log1p(jnp.maximum(gap, 0).astype(F32)), FAR)

    def far_of(s):
        age, valid = pick(slot_age, s, 0)[:, None], pick(slot_valid, s, 0)[:, None]
        return jnp.where(valid > 0, jnp.log1p(jnp.maximum(i + age, 0).astype(F32)), FAR)

    far = [far_of(h), far_of(h ^ 2)]
    heads = jnp.concatenate([2 * h + jnp.arange(2), 2 * (h ^ 1) + jnp.arange(2)])
    slopes = 0.6 * jnp.power(0.7, heads.astype(F32))
    ffn_chunk = jnp.concatenate([w_up, w_down.T])

    inputs_x = x_swap(inputs)
    ring.step()
    ring.step(near)
    ring.step((far, slopes, ffn_chunk, sources))
    ring.step(inputs_x)
    cot_low = x_swap(after(inputs_x, cotangent[:SEG // 2]))
    chunks = ring.finish()
    pairs = [(chunk, c_swap(chunk)) for chunk in chunks]
    ffn = RingGather(ffn_chunk, n_dp)
    ffn.step((chunks[-1], chunks[-2]))

    def first_moves(index, ins, outs):
        for k in range(n_dp):
            at = pl.multiple_of(index[k] * rows, rows)
            for p in range(2):
                chunk = ins[2 * k + p]
                yield chunk.at[pl.ds(0, rows), pl.ds(0, 6 * HD)], outs[p].at[pl.ds(at, rows)]
                yield chunk.at[pl.ds(rows, 16), pl.ds(0, 2 * HD)], outs[2].at[p, index[k]]
            yield ins[2 * k].at[pl.ds(0, rows), pl.ds(6 * HD, 2 * HD)], outs[3].at[index[k]]

    w_own, w_par, small, wo = copies(
        first_moves, [(D, 6 * HD), (D, 6 * HD), (2, n_dp, 16, 2 * HD), (n_dp, rows, 2 * HD)], sources,
        *[chunk for pair in pairs for chunk in pair])
    small_x = x_swap(small)
    cot_high = x_swap(after(small_x, cotangent[SEG // 2:]))
    small = jnp.stack([small[0, :, 0, :values], small[1, :, 0, :values], small_x[0, :, 0, :values], small_x[1, :, 0, :values]])
    rank = jnp.arange(4) ^ h
    small = sum(jnp.where((rank == e)[None, :, None], small[e][:, None], 0) for e in range(4))
    small = small.reshape(4 * n_dp, values).astype(F32)
    wo = wo.reshape(n_dp, 4, out_rows, 2 * HD)
    wo_x = x_swap(wo)
    wo4 = (wo, c_swap(wo), wo_x, c_swap(wo_x))

    bias_all = small[:, :share].reshape(4, 2 * HD)
    lines = small[:, share:4 * share].reshape(4 * n_dp, 3, share).transpose(1, 0, 2).reshape(3, D)
    up_shift = small[:, 4 * share:].reshape(4, D)
    two = lambda a: jnp.concatenate([pick(a, h, 0), pick(a, h ^ 1, 0)]).reshape(1, -1)
    bias, up_shift = two(bias_all), two(up_shift)

    kv, q = project(h, compressed, memory, after(cot_low, inputs), w_own, w_par)
    ffn.step(kv)
    kv_x, q_x = project(h ^ 2, compressed, memory, after((kv, wo_x), inputs_x), w_own, w_par)
    bias = after((lines, up_shift), bias)
    mixed_x, lse_x = attend(0, slopes, q_x, bias, kv_x, near, far[1])
    ffn.step(mixed_x)
    sent = x_swap(mixed_x)
    mixed, lse = attend(0, slopes, after((mixed_x, cot_high), q), bias, kv, near, far[0])
    ffn.step(mixed)
    chunks = ffn.finish()

    ffn_par = [c_swap(chunk) for chunk in chunks]
    per = n_dp // 4

    def wo_moves(index, ins, outs):
        me = index[0]
        for e in range(4):
            for b in range(4):
                for p in range(4):
                    target = outs[0].at[me ^ b, :, me ^ e, :, pl.ds(p * 2 * HD, 2 * HD)]
                    yield ins[e].at[pl.ds(b * per, per), p], target

    (w_o,) = copies(wo_moves, [(4, per, 4, out_rows, D)], h1, *wo4)
    w_o = w_o.reshape(D, D)

    cot, cot_x = (cotangent[:SEG // 2], cotangent[SEG // 2:]), (cot_low, cot_high)
    residual, normed = attention_out(mixed, sent, w_o, inputs, lines)
    normed_x = x_swap(normed)
    hid, gb, up_cols, branch, gn = feed_forward(n_dp, sources, normed, cot, up_shift, chunks, ffn_par, F32)

    other = (c_swap(inputs), c_swap(inputs_x))

    def memory_moves(index, ins, outs):
        me = index[0]
        yield ins[0], outs[0].at[me]
        yield ins[1], outs[0].at[me ^ 2]
        yield ins[2], outs[0].at[me ^ 1]
        yield ins[3], outs[0].at[me ^ 3]

    (new_memory,) = copies(memory_moves, [(seqs, SEG, D)], h1, inputs, inputs_x, *other)
    comp_w = lax.all_gather(after((chunks[-1], normed), w_comp), "dp", axis=0).reshape(n_dp, RATE, rows, 2 * HD)
    new_compressed = compress(h1, memory, compressed, comp_w, comp_bias)

    hid_x, gb_x, up_cols_x, branch_x, gn_x = feed_forward(n_dp, sources, normed_x, cot_x, up_shift, chunks, ffn_par, BF)
    gn_x = x_swap(gn_x)
    acts = ((normed, normed_x), cot + cot_x, (gb, gb_x), (hid, hid_x))
    from_par = [c_swap(a) for a in ffn_grads(1, n_dp, *acts)]
    from_par = after((new_compressed, new_memory), *from_par)
    ffn_sum = RingScatter(ffn_grads(0, n_dp, *acts, *from_par).reshape(n_dp, 2 * rows, D), d, n_dp)
    gn_x = after(ffn_sum.f, gn_x)
    ffn_sum.step()
    grad_residual, do, do_x, sums, mine, theirs = norm_back(
        n_dp, h1, residual, gn, gn_x, cotangent, lines, mixed, sent, w_o)
    do_x = x_swap(do_x)
    keep, send = out_half(h1, mine, c_swap(theirs))
    do = after((ffn_sum.f, ffn_sum.b), do)
    ffn_sum.step(do)
    got = x_swap(send)
    branch_x = x_swap(after((gn_x, got), branch_x))
    dq, dkv, q_cols = attend_back(0, slopes, q, bias, kv, near, far[0], mixed, lse, do)
    do_x = after((ffn_sum.f, ffn_sum.b), do_x)
    ffn_sum.step(dq)
    branch_x = after(dq, branch_x)
    output = add_up(BF, residual, branch, branch_x, lines[2:])
    term = token_term(dq, dkv, w_own, w_par, grad_residual)
    dq_x, dkv_x, q_cols_x = attend_back(0, slopes, q_x, bias, kv_x, near, far[1], mixed_x, lse_x, do_x)
    ffn_sum.step(dq_x)
    dq_x = after(got, dq_x)
    term_x = token_term(dq_x, dkv_x, w_own, w_par)
    term_sent = x_swap(term_x)
    grad_input = add_up(F32, term, term_sent)

    lane = jnp.arange(4)[:, None]

    def place(a):
        a = a.reshape(2, 1, -1)
        return jnp.where(lane == h, a[0], 0.0) + jnp.where(lane == h ^ 1, a[1], 0.0)

    tiny = jnp.concatenate([
        place(q_cols + q_cols_x).reshape(-1, share),
        sums[0].reshape(-1, share),
        sums[1].reshape(-1, share),
        sums[2].reshape(-1, share),
        place(up_cols + up_cols_x).reshape(-1, up_share),
    ], axis=1)
    tiny = tiny + x_swap(tiny)
    dq, dkv = after((tiny, term_x), dq, dkv)
    tiny = tiny + c_swap(tiny)
    tiny = jnp.pad(tiny.astype(BF).reshape(n_dp, 4, values), ((0, 0), (0, 12), (0, 2 * HD - values)))

    work = (ids, compressed, memory, inputs, inputs_x, (dkv, dkv_x), (dq, dq_x))
    from_par = weight_grads(1, n_dp, *work)
    from_par = after(ffn_sum.f, *from_par)
    from_par = [c_swap(a) for a in from_par]
    grad_up, grad_down = ffn_sum.finish(close_ffn_kernel, [(rows, D), (D, rows)])
    g_sum = RingScatter(weight_grads(0, n_dp, *work, *from_par, tiny, keep, got), d, n_dp)
    g_sum.step()
    g_sum.step(output)
    g_sum.step((grad_up, grad_down))
    g_sum.step(term)
    grad_key, grad_value, grad_query, grad_out, tiny = g_sum.finish(
        close_last_kernel, [(rows, 2 * HD), (rows, 2 * HD), (rows, 2 * HD), (out_rows, D), (16, 2 * HD)])
    tiny = pick(tiny, h, 0)

    return (
        output,
        grad_input,
        grad_query,
        grad_key,
        grad_value,
        tiny[:share],
        grad_out,
        tiny[share:2 * share],
        tiny[2 * share:3 * share],
        grad_up,
        tiny[4 * share:values],
        grad_down,
        tiny[3 * share:4 * share],
        new_memory,
        new_compressed,
    )


def solution(mesh):
    both = ("dp", "head")
    in_specs = (
        P(both, None),
        P("dp", None, None),
        P("dp", None, None),
        P("dp", None),
        P("dp", None),
        P("dp", "head"),
        P("dp", "head"),
        P("dp", "head"),
        P(both),
        P(both, None),
        P(both),
        P(both),
        P("dp", "head"),
        P(both),
        P("head", "dp"),
        P(both),
        P(None, "dp", "head"),
        P("head"),
        P(both, None),
    )
    out_specs = (
        P(both, None),
        P(both, None),
        P("dp", "head"),
        P("dp", "head"),
        P("dp", "head"),
        P(both),
        P(both, None),
        P(both),
        P(both),
        P("dp", "head"),
        P(both),
        P("head", "dp"),
        P(both),
        P("dp", None, None),
        P("dp", None, "head"),
    )
    return jax.shard_map(per_device, mesh=mesh, in_specs=in_specs, out_specs=out_specs, check_vma=False)
```

```python
import functools

import jax
import jax.numpy as jnp
from jax import lax
from jax.experimental import pallas as pl
from jax.experimental.pallas import tpu as pltpu
from jax.sharding import PartitionSpec as P

D = 1024
HD = 128
SEG = 512
CM = 512
RATE = 3
CC = 171
LN_EPS = 1e-05
LOG2E = 1.4426950408889634
SCALE2 = LOG2E * HD ** (-0.5)
FAR = 1e32
VMEM = 56 * 1024 * 1024
BF = jnp.bfloat16
F32 = jnp.float32


def nt(a, b):
    return lax.dot_general(a, b, (((1,), (1,)), ((), ())), preferred_element_type=F32)


def tn(a, b):
    return lax.dot_general(a, b, (((0,), (0,)), ((), ())), preferred_element_type=F32)


def nn(a, b):
    return jnp.dot(a, b, preferred_element_type=F32)


def x_swap(a):
    return lax.ppermute(a, "head", [(i, i ^ 2) for i in range(4)])


def c_swap(a):
    return lax.ppermute(a, "head", [(i, i ^ 1) for i in range(4)])


def fwd_kernel(slope_ref, q_ref, bias_ref, kv_ref, near_ref, far_ref, mixed_ref, lse_ref):
    a = pl.program_id(0)
    slope2 = slope_ref[a] * LOG2E
    q = (q_ref[0] + bias_ref[...]).astype(BF)
    parts = []
    for n in range(3):
        k = kv_ref[0, n * SEG:(n + 1) * SEG, :HD]
        table = far_ref[...] if n == 0 else near_ref[(n - 1) * SEG:n * SEG, :]
        parts.append(nt(k, q) * SCALE2 - slope2 * table)
    top = jnp.maximum(jnp.maximum(jnp.max(parts[0], axis=0, keepdims=True), jnp.max(parts[1], axis=0, keepdims=True)),
                      jnp.max(parts[2], axis=0, keepdims=True))
    total = jnp.zeros((1, SEG), F32)
    acc = jnp.zeros((HD, SEG), F32)
    for n in range(3):
        p = jnp.exp2(parts[n] - top)
        total = total + jnp.sum(p, axis=0, keepdims=True)
        acc = acc + tn(kv_ref[0, n * SEG:(n + 1) * SEG, HD:], p.astype(BF))
    mixed_ref[...] = (acc / total).T.astype(BF)
    lse_ref[...] = (top + jnp.log2(total)).reshape(1, 1, SEG)


def bwd_kernel(slope_ref, q_ref, bias_ref, kv_ref, near_ref, far_ref, mixed_ref, lse_ref, do_ref, dq_ref, dkv_ref, sum_ref):
    a = pl.program_id(0)
    slope2 = slope_ref[a] * LOG2E
    q = (q_ref[0] + bias_ref[...]).astype(BF)
    do = do_ref[...]
    lse = lse_ref[...].reshape(1, SEG)
    row_dot = jnp.sum((do.astype(F32) * mixed_ref[...].astype(F32)).T, axis=0, keepdims=True)
    inv_root = HD ** (-0.5)
    dq = jnp.zeros((HD, SEG), F32)
    for n in range(3):
        rows = slice(n * SEG, (n + 1) * SEG)
        k = kv_ref[0, rows, :HD]
        v = kv_ref[0, rows, HD:]
        table = far_ref[...] if n == 0 else near_ref[(n - 1) * SEG:n * SEG, :]
        p = jnp.exp2(nt(k, q) * SCALE2 - slope2 * table - lse)
        ds = (p * (nt(v, do) - row_dot)).astype(BF)
        dkv_ref[rows, HD:] = nn(p.astype(BF), do).astype(BF)
        dkv_ref[rows, :HD] = (nn(ds, q) * inv_root).astype(BF)
        dq = dq + tn(k, ds)
    dq = (dq.T * inv_root).astype(BF)
    dq_ref[...] = dq
    sum_ref[...] = jnp.sum(dq.astype(F32), axis=0, keepdims=True)


def ring_order(n):
    up = list(range(0, n, 2))
    return up + [p + 1 for p in reversed(up)]


def ring_perms(n):
    order = ring_order(n)
    ahead = [(order[p], order[(p + 1) % n]) for p in range(n)]
    return ahead, [(b, a) for a, b in ahead]


def ring_place(d, n):
    return jnp.where(d % 2 == 0, d // 2, n - 1 - d // 2)


def ring_member(p, n):
    p = p % n
    return jnp.where(p < n // 2, 2 * p, 2 * (n - 1 - p) + 1)


def after(first, *then):
    out = lax.optimization_barrier((first,) + then)[1:]
    return out if len(then) > 1 else out[0]


class RingGather:
    def __init__(self, chunk, n):
        self.n, self.k = n, 0
        self.ahead, self.back = ring_perms(n)
        self.f = self.b = chunk
        self.chunks = [chunk]

    def step(self, first=None):
        self.k += 1
        if self.k > self.n // 2:
            return
        if first is not None:
            self.f, self.b = after(first, self.f, self.b)
        self.f = lax.ppermute(self.f, "dp", self.ahead)
        self.chunks.append(self.f)
        if self.k < self.n - self.n // 2:
            self.b = lax.ppermute(self.b, "dp", self.back)
            self.chunks.append(self.b)

    def finish(self):
        while self.k < self.n // 2:
            self.step()
        return self.chunks


def ring_sources(d, n):
    place = ring_place(d, n)
    steps = [0]
    for k in range(1, n // 2 + 1):
        steps.append(-k)
        if k < n - n // 2:
            steps.append(k)
    return ring_member(place + jnp.array(steps, jnp.int32), n).astype(jnp.int32)


ROWS = 3 * SEG
HALF = D // 2
smem_spec = pl.BlockSpec(memory_space=pltpu.SMEM)
vmem_spec = pl.BlockSpec(memory_space=pltpu.VMEM)
any_spec = pl.BlockSpec(memory_space=pl.ANY)


def params():
    return pltpu.CompilerParams(vmem_limit_bytes=VMEM)


def cost(us):
    return pl.CostEstimate(flops=int(us * 0.18e9), bytes_accessed=1, transcendentals=0)


def shape(*dims, kind=BF):
    return jax.ShapeDtypeStruct(dims, kind)


def whole(*dims):
    return pl.BlockSpec(dims, lambda *i: (0,) * len(dims))


def attend(t, slopes, q, bias, kv, near, far):
    return pl.pallas_call(
        fwd_kernel,
        grid=(4,),
        in_specs=[
            smem_spec,
            pl.BlockSpec((1, SEG, HD), lambda a: (t, 0, a)),
            pl.BlockSpec((1, HD), lambda a: (0, a)),
            pl.BlockSpec((1, ROWS, 2 * HD), lambda a: (t, 0, a)),
            whole(2 * SEG, SEG),
            whole(SEG, SEG),
        ],
        out_specs=[pl.BlockSpec((SEG, HD), lambda a: (0, a)), pl.BlockSpec((1, 1, SEG), lambda a: (a, 0, 0))],
        out_shape=[shape(SEG, HALF), shape(4, 1, SEG, kind=F32)],
        compiler_params=params(),
        cost_estimate=cost(9),
    )(slopes, q, bias, kv, near, far)


def attend_back(t, slopes, q, bias, kv, near, far, mixed, lse, do):
    column = pl.BlockSpec((SEG, HD), lambda a: (0, a))
    return pl.pallas_call(
        bwd_kernel,
        grid=(4,),
        in_specs=[
            smem_spec,
            pl.BlockSpec((1, SEG, HD), lambda a: (t, 0, a)),
            pl.BlockSpec((1, HD), lambda a: (0, a)),
            pl.BlockSpec((1, ROWS, 2 * HD), lambda a: (t, 0, a)),
            whole(2 * SEG, SEG),
            whole(SEG, SEG),
            column,
            pl.BlockSpec((1, 1, SEG), lambda a: (a, 0, 0)),
            column,
        ],
        out_specs=[column, pl.BlockSpec((ROWS, 2 * HD), lambda a: (0, a)), pl.BlockSpec((1, HD), lambda a: (0, a))],
        out_shape=[shape(SEG, HALF), shape(ROWS, D), shape(1, HALF, kind=F32)],
        compiler_params=params(),
        cost_estimate=cost(12),
    )(slopes, q, bias, kv, near, far, mixed, lse, do)


def pack_kernel(key_ref, value_ref, query_ref, out_ref, *rest):
    smalls, pack_ref = rest[:-1], rest[-1]
    rows = key_ref.shape[0]
    piece = out_ref.shape[0]
    pack_ref[:rows, :HD] = key_ref[:, :HD]
    pack_ref[:rows, HD:2 * HD] = value_ref[:, :HD]
    pack_ref[:rows, 2 * HD:3 * HD] = key_ref[:, HD:]
    pack_ref[:rows, 3 * HD:4 * HD] = value_ref[:, HD:]
    pack_ref[:rows, 4 * HD:6 * HD] = query_ref[...]
    for k in range(4):
        pack_ref[k * piece:(k + 1) * piece, 6 * HD:] = out_ref[:, k * 2 * HD:(k + 1) * 2 * HD]
    line = jnp.concatenate([a[...].astype(F32) for a in smalls], axis=1)
    line = jnp.concatenate([line, jnp.zeros((1, D - line.shape[1]), F32)], axis=1)
    row = lax.broadcasted_iota(jnp.int32, (16, D), 0)
    pack_ref[rows:] = jnp.where(row == 0, jnp.broadcast_to(line, (16, D)), 0.0).astype(BF)


def pack(w_key, w_value, w_query, w_out, smalls):
    return pl.pallas_call(
        pack_kernel,
        in_specs=[vmem_spec] * (4 + len(smalls)),
        out_specs=vmem_spec,
        out_shape=shape(w_key.shape[0] + 16, D),
        compiler_params=params(),
        cost_estimate=cost(1),
    )(w_key, w_value, w_query, w_out, *[a.reshape(1, -1) for a in smalls])


def project_kernel(id_ref, comp_ref, mem_ref, token_ref, w_own_ref, w_par_ref, kv_ref, q_ref, source, own, par, sems):
    n = pl.program_id(0)
    blocks = (comp_ref.at[id_ref[0]], mem_ref.at[id_ref[0]], token_ref)
    moves = [pltpu.make_async_copy(a, source.at[k], sems.at[k]) for k, a in enumerate(blocks)]
    own_move = pltpu.make_async_copy(w_own_ref, own, sems.at[3])
    par_move = pltpu.make_async_copy(w_par_ref, par, sems.at[4])

    @pl.when(n == 0)
    def _():
        own_move.start()
        moves[0].start()
        par_move.start()
        moves[1].start()
        moves[2].start()
        own_move.wait()

    for k in range(3):
        pl.when(n == k)(moves[k].wait)
    a = source[n]
    kv_ref[0, :, :HALF] = nn(a, own[:, :HALF]).astype(BF)
    pl.when(n == 0)(par_move.wait)
    kv_ref[0, :, HALF:] = nn(a, par[:, :HALF]).astype(BF)

    @pl.when(n == 2)
    def _():
        q_ref[0, :, :2 * HD] = nn(a, own[:, HALF:])
        q_ref[0, :, 2 * HD:] = nn(a, par[:, HALF:])


def project(seq, compressed, memory, tokens, w_own, w_par):
    return pl.pallas_call(
        project_kernel,
        grid_spec=pltpu.PrefetchScalarGridSpec(
            num_scalar_prefetch=1,
            grid=(3,),
            in_specs=[any_spec] * 5,
            out_specs=[
                pl.BlockSpec((1, SEG, D), lambda n, seq: (0, n, 0)),
                pl.BlockSpec((1, SEG, HALF), lambda n, seq: (0, 0, 0)),
            ],
            scratch_shapes=[
                pltpu.VMEM((3, SEG, D), BF),
                pltpu.VMEM((D, 6 * HD), BF),
                pltpu.VMEM((D, 6 * HD), BF),
                pltpu.SemaphoreType.DMA((5,)),
            ],
        ),
        out_shape=[shape(1, ROWS, D), shape(1, SEG, HALF, kind=F32)],
        compiler_params=params(),
        cost_estimate=cost(8),
    )(seq.reshape(1), compressed, memory, tokens, w_own, w_par)


def norm_kernel(mixed_ref, sent_ref, w_ref, in_ref, lines_ref, residual_ref, normed_ref):
    out = nn(mixed_ref[...], w_ref[:HALF]) + nn(sent_ref[...], w_ref[HALF:])
    residual = in_ref[...].astype(F32) + out
    residual_ref[...] = residual
    center = residual - jnp.mean(residual, axis=-1, keepdims=True)
    rstd = lax.rsqrt(jnp.mean(center * center, axis=-1, keepdims=True) + LN_EPS)
    normed_ref[...] = (center * rstd * lines_ref[0:1] + lines_ref[1:2]).astype(BF)


def attention_out(mixed, sent, w_o, inputs, lines):
    rows = SEG // 2
    half = pl.BlockSpec((rows, HALF), lambda i: (i, 0))
    full = pl.BlockSpec((rows, D), lambda i: (i, 0))
    return pl.pallas_call(
        norm_kernel,
        grid=(2,),
        in_specs=[half, half, whole(D, D), full, whole(3, D)],
        out_specs=[full, full],
        out_shape=[shape(SEG, D, kind=F32), shape(SEG, D)],
        compiler_params=params(),
        cost_estimate=cost(4),
    )(mixed, sent, w_o, inputs, lines)


def gelu_pair(before):
    c0, c1 = 0.7978845608028654, 0.044715
    sq = before * before
    t = jnp.tanh(c0 * before * (1.0 + c1 * sq))
    half = 0.5 * (1.0 + t)
    return before * half, half + 0.5 * before * (1.0 - t * t) * (c0 * (1.0 + 3.0 * c1 * sq))


def ffn_kernel(n_dp, index_ref, norm_ref, low_ref, high_ref, bias_ref, *refs):
    chunks = refs[:2 * n_dp]
    hid_ref, gb_ref, sum_ref, branch_ref, gn_ref, up_ref, down_ref, branch, gn, sems = refs[2 * n_dp:]
    i, tiles = pl.program_id(0), up_ref.shape[0]
    tile, rows = up_ref.shape[2], D // n_dp

    def moves(step):
        group, column = divmod(step, tiles // 2)
        for k in range(n_dp):
            source = chunks[group * n_dp + k]
            at = pl.ds(pl.multiple_of(index_ref[k] * rows, rows), rows)
            for m, target in enumerate((up_ref, down_ref)):
                yield pltpu.make_async_copy(
                    source.at[pl.ds(m * rows, rows), pl.ds(column * tile, tile)],
                    target.at[step, at],
                    sems.at[(step * n_dp + k) * 2 + m],
                )

    @pl.when(i == 0)
    def _():
        for step in range(tiles):
            for move in moves(step):
                move.start()

    for step in range(tiles):
        @pl.when(i == step)
        def _(step=step):
            for move in moves(step):
                move.wait()

    up, down = up_ref.at[i], down_ref.at[i]
    total = jnp.zeros((1, tile), F32)
    half = SEG // 2
    for c, cot_ref in enumerate((low_ref, high_ref)):
        part = slice(c * half, (c + 1) * half)
        act, slope = gelu_pair(nn(norm_ref[part], up[...]) + bias_ref[...])
        act = act.astype(BF)
        gb = (nn(cot_ref[...], down[...]) * slope).astype(BF)
        hid_ref[part] = act
        gb_ref[part] = gb
        total = total + jnp.sum(gb.astype(F32), axis=0, keepdims=True)
        branch[part] = jnp.where(i > 0, branch[part], 0.0) + nt(act, down[...])
        gn[part] = jnp.where(i > 0, gn[part], 0.0) + nt(gb, up[...])
    sum_ref[...] = total

    @pl.when(i == tiles - 1)
    def _():
        branch_ref[...] = branch[...].astype(branch_ref.dtype)
        gn_ref[...] = gn[...].astype(gn_ref.dtype)


def feed_forward(n_dp, sources, norm, cot, bias, own, par, kind, tile=1024):
    tiles = 2 * D // tile
    part = pl.BlockSpec((SEG, tile), lambda i, index: (0, i))
    line = pl.BlockSpec((1, tile), lambda i, index: (0, i))
    return pl.pallas_call(
        functools.partial(ffn_kernel, n_dp),
        grid_spec=pltpu.PrefetchScalarGridSpec(
            num_scalar_prefetch=1,
            grid=(tiles,),
            in_specs=[whole(SEG, D), whole(SEG // 2, D), whole(SEG // 2, D), line] + [any_spec] * (2 * n_dp),
            out_specs=[part, part, line, whole(SEG, D), whole(SEG, D)],
            scratch_shapes=[pltpu.VMEM((tiles, D, tile), BF)] * 2
            + [pltpu.VMEM((SEG, D), F32)] * 2
            + [pltpu.SemaphoreType.DMA((2 * tiles * n_dp,))],
        ),
        out_shape=[shape(SEG, 2 * D), shape(SEG, 2 * D), shape(1, 2 * D, kind=F32), shape(SEG, D, kind=kind), shape(SEG, D, kind=kind)],
        compiler_params=params(),
        cost_estimate=cost(16),
    )(sources, norm, *cot, bias, *own, *par)


def ffn_grad_kernel(tiles, n0, n1, c0_low, c0_high, c1_low, c1_high, gb0, gb1, hid0, hid1, *rest):
    parts, outs = (rest[:-1], rest[-1:]) if len(rest) > 2 * tiles else ((), rest)
    step = pl.program_id(0) * tiles + pl.program_id(1)
    for m in range(2):
        for i in range(tiles):
            k = m * tiles + i

            @pl.when(step == k)
            def _(m=m, k=k):
                if m == 0:
                    total = tn(n0[...], gb0[...]) + tn(n1[...], gb1[...])
                else:
                    half = SEG // 2
                    total = tn(c0_low[...], hid0[:half]) + tn(c0_high[...], hid0[half:])
                    total = total + tn(c1_low[...], hid1[:half]) + tn(c1_high[...], hid1[half:])
                if parts:
                    out = outs[0]
                    total = total.reshape(out.shape[0], out.shape[2], -1)
                    out[:, 0] = (total + parts[k][...].astype(F32)).astype(BF)
                else:
                    outs[k][...] = total.reshape(outs[k].shape).astype(BF)


def ffn_grads(g, n_dp, norms, cots, gbs, hids, *received, tile=512):
    n = D // tile
    rows = D // n_dp
    tokens = whole(SEG, D)
    early = pl.BlockSpec((SEG, tile), lambda m, i: (0, g * n + jnp.where(m == 0, i, n - 1)))
    late = pl.BlockSpec((SEG, tile), lambda m, i: (0, g * n + jnp.where(m == 0, 0, i)))
    part = whole(n_dp, rows, tile)
    if received:
        out_specs = pl.BlockSpec((n_dp, 1, rows, tile), lambda m, i: (0, m, 0, i))
        out_shape = shape(n_dp, 2, rows, D)
    else:
        out_specs, out_shape = [part] * (2 * n), [shape(n_dp, rows, tile)] * (2 * n)
    return pl.pallas_call(
        functools.partial(ffn_grad_kernel, n),
        grid=(2, n),
        in_specs=[tokens] * 2 + [whole(SEG // 2, D)] * 4 + [early] * 2 + [late] * 2 + [part] * len(received),
        out_specs=out_specs,
        out_shape=out_shape,
        compiler_params=params(),
        cost_estimate=cost(10),
    )(*norms, *cots, *gbs, *hids, *received)


def norm_back_kernel(h_ref, residual_ref, gn_ref, gnx_ref, cot_ref, lines_ref, mixed_ref, sent_ref, w_ref,
                     grad_ref, keep_ref, send_ref, sums_ref, mine_ref, theirs_ref, acc):
    i = pl.program_id(0)
    residual = residual_ref[...]
    center = residual - jnp.mean(residual, axis=-1, keepdims=True)
    rstd = lax.rsqrt(jnp.mean(center * center, axis=-1, keepdims=True) + LN_EPS)
    xhat = center * rstd
    gn = gn_ref[...] + gnx_ref[...].astype(F32)
    g = gn * lines_ref[0:1]
    cot = cot_ref[...].astype(F32)
    grad = cot + rstd * (g - jnp.mean(g, axis=-1, keepdims=True) - xhat * jnp.mean(g * xhat, axis=-1, keepdims=True))
    grad_ref[...] = grad
    low = grad.astype(BF)
    keep_ref[...] = nt(low, w_ref[:HALF]).astype(BF)
    send_ref[...] = nt(low, w_ref[HALF:]).astype(BF)
    total = lambda a: jnp.sum(a, axis=0, keepdims=True)
    sums = jnp.concatenate([total(gn * xhat), total(gn), total(cot)], axis=0)

    @pl.when(i == 0)
    def _():
        sums_ref[...] = sums
        acc[:HALF] = tn(mixed_ref[...], low)
        acc[HALF:] = tn(sent_ref[...], low)

    @pl.when(i > 0)
    def _():
        sums_ref[...] += sums
        acc[:HALF] += tn(mixed_ref[...], low)
        acc[HALF:] += tn(sent_ref[...], low)

    @pl.when(i == pl.num_programs(0) - 1)
    def _():
        per = mine_ref.shape[0] // 4
        first = h_ref[0] % 2 == 0
        for b in range(4):
            block = acc[b * 2 * HD:(b + 1) * 2 * HD].reshape(per, 2, 2, mine_ref.shape[2], D)
            at = pl.ds((h_ref[0] ^ b) * per, per)
            mine_ref[at] = jnp.where(first, block[:, :, 0], block[:, :, 1]).astype(BF)
            theirs_ref[at] = jnp.where(first, block[:, :, 1], block[:, :, 0]).astype(BF)


def out_half_kernel(h_ref, mine_ref, got_ref, keep_ref, send_ref):
    total = mine_ref[...].astype(F32) + got_ref[...].astype(F32)
    first = h_ref[0] // 2 == 0
    keep_ref[...] = jnp.where(first, total[:, 0], total[:, 1]).astype(BF)
    send_ref[...] = jnp.where(first, total[:, 1], total[:, 0]).astype(BF)


def out_half(h, mine, got):
    n_dp, _, rows, _ = mine.shape
    return pl.pallas_call(
        out_half_kernel,
        in_specs=[smem_spec, vmem_spec, vmem_spec],
        out_specs=[vmem_spec, vmem_spec],
        out_shape=[shape(n_dp, rows, D)] * 2,
        compiler_params=pltpu.CompilerParams(vmem_limit_bytes=16 << 20),
        cost_estimate=cost(1),
    )(h, mine, got)


def norm_back(n_dp, h, residual, gn, gnx, cot, gain, mixed, sent, w_o):
    rows = SEG // 2
    half = pl.BlockSpec((rows, HALF), lambda i: (i, 0))
    full = pl.BlockSpec((rows, D), lambda i: (i, 0))
    return pl.pallas_call(
        norm_back_kernel,
        grid=(2,),
        in_specs=[smem_spec, full, full, full, full, whole(3, D), half, half, whole(D, D)],
        out_specs=[full, half, half, whole(3, D)] + [whole(n_dp, 2, D // n_dp // 4, D)] * 2,
        out_shape=[shape(SEG, D, kind=F32), shape(SEG, HALF), shape(SEG, HALF), shape(3, D, kind=F32)] + [shape(n_dp, 2, D // n_dp // 4, D)] * 2,
        scratch_shapes=[pltpu.VMEM((D, D), F32)],
        compiler_params=params(),
        cost_estimate=cost(10),
    )(h, residual, gn, gnx, cot, gain, mixed, sent, w_o)


def term_kernel(dq_ref, dkv_ref, w_own_ref, w_par_ref, *rest):
    out = nt(dkv_ref[:, :HALF], w_own_ref[:, :HALF]) + nt(dkv_ref[:, HALF:], w_par_ref[:, :HALF])
    out = out + nt(dq_ref[:, :2 * HD], w_own_ref[:, HALF:]) + nt(dq_ref[:, 2 * HD:], w_par_ref[:, HALF:])
    if len(rest) > 1:
        out = out + rest[0][...]
    rest[-1][...] = out.astype(rest[-1].dtype)


def token_term(dq, dkv, w_own, w_par, *residual):
    rows = SEG // 2
    full = pl.BlockSpec((rows, D), lambda i: (i, 0))
    weight = whole(D, 3 * 2 * HD)
    return pl.pallas_call(
        term_kernel,
        grid=(2,),
        in_specs=[
            pl.BlockSpec((rows, HALF), lambda i: (i, 0)),
            pl.BlockSpec((rows, D), lambda i: (4 + i, 0)),
            weight,
            weight,
        ] + [full] * len(residual),
        out_specs=full,
        out_shape=shape(SEG, D, kind=F32 if residual else BF),
        compiler_params=params(),
        cost_estimate=cost(4),
    )(dq, dkv, w_own, w_par, *residual)


def weight_grad_kernel(g, ids_ref, comp_ref, mem_ref, own_ref, other_ref, dkv0, dkv1, dq0, dq1, *rest):
    step = pl.program_id(0)
    source, grads, query_grads, acc, sems = rest[-5:]
    parts, outs = (rest[:2], rest[5:6]) if len(rest) > 8 else ((), rest[:2])
    half = rest[0].shape[0]
    rows = D // (2 * half)
    blocks = []
    for t, (tokens, dkv) in enumerate(((own_ref, dkv0), (other_ref, dkv1))):
        for n, a in enumerate((comp_ref.at[ids_ref[t]], mem_ref.at[ids_ref[t]], tokens)):
            blocks.append((a, dkv.at[pl.ds(n * SEG, SEG), pl.ds(g * HALF, HALF)]))
    moves = [
        (pltpu.make_async_copy(a, source.at[k], sems.at[2 * k]), pltpu.make_async_copy(b, grads.at[k], sems.at[2 * k + 1]))
        for k, (a, b) in enumerate(blocks)
    ]
    extra = [
        pltpu.make_async_copy(a.at[:, pl.ds(g * 2 * HD, 2 * HD)], query_grads.at[k], sems.at[12 + k])
        for k, a in enumerate((dq0, dq1))
    ]

    @pl.when(step == 0)
    def _():
        for pair in moves:
            pair[0].start()
            pair[1].start()
        extra[0].start()
        extra[1].start()

    for k in range(6):
        @pl.when(step == k)
        def _(k=k):
            moves[k][0].wait()
            moves[k][1].wait()
            if k == 0:
                acc[:, :HALF] = tn(source[k], grads[k])
            else:
                acc[:, :HALF] += tn(source[k], grads[k])
            if k == 2:
                extra[0].wait()
                acc[:, HALF:] = tn(source[k], query_grads[0])
            if k < 5:
                return
            extra[1].wait()
            acc[:, HALF:] += tn(source[k], query_grads[1])
            total = acc[...].reshape(2 * half, rows, 6 * HD)
            for p in range(2):
                block = slice(p * half, (p + 1) * half)
                if parts:
                    outs[0][block, :rows] = (total[block] + parts[p][...].astype(F32)).astype(BF)
                else:
                    outs[p][...] = total[block].astype(BF)
            if parts:
                tiny, mine, got = rest[2:5]
                out_rows = mine.shape[1]
                other = (mine[...].astype(F32) + got[...].astype(F32)).astype(BF)
                low = rows + (outs[0].shape[1] - rows) // 2
                outs[0][:, rows:] = jnp.zeros((2 * half, outs[0].shape[1] - rows, 6 * HD), BF)
                outs[0][:, rows:rows + out_rows] = other[:, :, :6 * HD]
                outs[0][:, low:low + out_rows, :2 * HD] = other[:, :, 6 * HD:]
                outs[0][:, low:low + 16, 2 * HD:4 * HD] = tiny[...]


def weight_grads(g, n_dp, ids, compressed, memory, own, other, dkvs, dqs, *received):
    rows = D // n_dp
    if received:
        extra = 2 * max(16, received[-1].shape[1])
        out_specs, out_shape = whole(n_dp, rows + extra, 6 * HD), shape(n_dp, rows + extra, 6 * HD)
    else:
        out_specs, out_shape = [whole(n_dp // 2, rows, 6 * HD)] * 2, [shape(n_dp // 2, rows, 6 * HD)] * 2
    return pl.pallas_call(
        functools.partial(weight_grad_kernel, g),
        grid_spec=pltpu.PrefetchScalarGridSpec(
            num_scalar_prefetch=1,
            grid=(6,),
            in_specs=[any_spec] * 8 + [whole(*a.shape) for a in received],
            out_specs=out_specs,
            scratch_shapes=[
                pltpu.VMEM((6, SEG, D), BF),
                pltpu.VMEM((6, SEG, HALF), BF),
                pltpu.VMEM((2, SEG, 2 * HD), BF),
                pltpu.VMEM((D, 6 * HD), F32),
                pltpu.SemaphoreType.DMA((14,)),
            ],
        ),
        out_shape=out_shape,
        compiler_params=params(),
        cost_estimate=cost(10),
    )(ids, compressed, memory, own, other, *dkvs, *dqs, *received)


def copies(moves, out_shapes, index, *arrays):
    count = len(arrays)

    def kernel(index_ref, *refs):
        ins, outs, sems = refs[:count], refs[count:-1], refs[-1]
        started = []
        for n, (source, target) in enumerate(moves(index_ref, ins, outs)):
            copy = pltpu.make_async_copy(source, target, sems.at[n])
            copy.start()
            started.append(copy)
        for copy in started:
            copy.wait()

    return pl.pallas_call(
        kernel,
        in_specs=[smem_spec] + [any_spec] * count,
        out_specs=[vmem_spec] * len(out_shapes),
        out_shape=[shape(*dims) for dims in out_shapes],
        scratch_shapes=[pltpu.SemaphoreType.DMA((192,))],
        compiler_params=pltpu.CompilerParams(vmem_limit_bytes=16 << 20),
        cost_estimate=cost(0),
    )(index, *arrays)


def assemble(chunks, sources, parts):
    n, cols = len(chunks), chunks[0].shape[1]

    def moves(index, ins, outs):
        for k in range(n):
            row = 0
            for out, rows in zip(outs, parts):
                yield ins[k].at[pl.ds(row, rows)], out.at[pl.ds(pl.multiple_of(index[k] * rows, rows), rows)]
                row += rows

    return copies(moves, [(n * rows, cols) for rows in parts], sources, *chunks)


def pick_kernel(index_ref, ahead_ref, back_ref, f_ref, b_ref):
    f_ref[...] = ahead_ref[0]
    b_ref[...] = back_ref[0]


def add_kernel(index_ref, f_in, b_in, ahead_ref, back_ref, f_ref, b_ref):
    f_ref[...] = (f_in[...].astype(F32) + ahead_ref[0].astype(F32)).astype(BF)
    b_ref[...] = (b_in[...].astype(F32) + back_ref[0].astype(F32)).astype(BF)


def add_one_kernel(index_ref, f_in, ahead_ref, back_ref, f_ref):
    f_ref[...] = (f_in[...].astype(F32) + ahead_ref[0].astype(F32)).astype(BF)


def close_kernel(index_ref, f_in, b_in, own_ref, _, out_ref):
    out_ref[...] = f_in[...].astype(F32) + b_in[...].astype(F32) + own_ref[0].astype(F32)


def close_ffn_kernel(index_ref, f_in, b_in, own_ref, _, up_ref, down_ref):
    total = f_in[...].astype(F32) + b_in[...].astype(F32) + own_ref[0].astype(F32)
    rows = up_ref.shape[0]
    up_ref[...] = total[:rows]
    down_ref[...] = total[rows:].T


def close_last_kernel(index_ref, f_in, b_in, own_ref, _, key_ref, value_ref, query_ref, out_ref, small_ref):
    total = f_in[...].astype(F32) + b_in[...].astype(F32) + own_ref[0].astype(F32)
    rows, out_rows = key_ref.shape[0], out_ref.shape[0]
    low = rows + (total.shape[0] - rows) // 2
    key_ref[:, :HD] = total[:rows, :HD]
    value_ref[:, :HD] = total[:rows, HD:2 * HD]
    key_ref[:, HD:] = total[:rows, 2 * HD:3 * HD]
    value_ref[:, HD:] = total[:rows, 3 * HD:4 * HD]
    query_ref[...] = total[:rows, 4 * HD:]
    out_ref[:, :6 * HD] = total[rows:rows + out_rows]
    out_ref[:, 6 * HD:] = total[low:low + out_rows, :2 * HD]
    small_ref[...] = total[low:low + 16, 2 * HD:4 * HD]


def ring_kernel(kernel, array, places, given, outs):
    _, rows, cols = array.shape
    shapes = [shape(rows, cols)] * outs if isinstance(outs, int) else [shape(*dims, kind=F32) for dims in outs]
    flat = pl.BlockSpec((rows, cols), lambda i, index: (0, 0))
    block = lambda k: pl.BlockSpec((1, rows, cols), lambda i, index: (index[k], 0, 0))
    return pl.pallas_call(
        kernel,
        grid_spec=pltpu.PrefetchScalarGridSpec(
            num_scalar_prefetch=1,
            grid=(1,),
            in_specs=[flat] * len(given) + [block(0), block(1)],
            out_specs=[pl.BlockSpec(a.shape, lambda i, index: (0, 0)) for a in shapes],
        ),
        out_shape=shapes,
        compiler_params=pltpu.CompilerParams(vmem_limit_bytes=16 << 20),
        cost_estimate=cost(2),
    )(places, *given, array, array)


class RingScatter:
    def __init__(self, array, d, n):
        self.array, self.n, self.k = array, n, 0
        self.ahead, self.back = ring_perms(n)
        self.place = ring_place(d, n)
        self.up, self.down = n // 2, n - n // 2 - 1
        self.f, self.b = ring_kernel(pick_kernel, array, self.at(self.up, -self.down), (), 2)

    def at(self, p, q):
        return ring_member(self.place + jnp.array([p, q], jnp.int32), self.n).astype(jnp.int32)

    def step(self, first=None):
        self.k += 1
        k = self.k
        if k > self.up:
            return
        if first is not None:
            self.f, self.b = after(first, self.f, self.b)
        self.f = lax.ppermute(self.f, "dp", self.ahead)
        if k <= self.down:
            self.b = lax.ppermute(self.b, "dp", self.back)
        at = self.at(self.up - k, k - self.down)
        if k < self.down:
            self.f, self.b = ring_kernel(add_kernel, self.array, at, (self.f, self.b), 2)
        elif k < self.up:
            (self.f,) = ring_kernel(add_one_kernel, self.array, at, (self.f,), 1)

    def finish(self, kernel=close_kernel, outs=None):
        while self.k < self.up:
            self.step()
        return ring_kernel(kernel, self.array, self.at(0, 0), (self.f, self.b), outs or [self.array.shape[1:]])


def sum_kernel(*refs):
    total = refs[0][...].astype(F32)
    for ref in refs[1:-1]:
        total = total + ref[...].astype(F32)
    refs[-1][...] = total.astype(refs[-1].dtype)


def add_up(kind, *arrays):
    rows, cols = arrays[0].shape
    specs = [
        pl.BlockSpec((rows // 2, cols), lambda i: (i, 0)) if a.shape[0] == rows else whole(*a.shape) for a in arrays
    ]
    return pl.pallas_call(
        sum_kernel,
        grid=(2,),
        in_specs=specs,
        out_specs=specs[0],
        out_shape=shape(rows, cols, kind=kind),
        compiler_params=params(),
        cost_estimate=cost(3),
    )(*arrays)


def compress_kernel(h_ref, memory_ref, compressed_ref, w_ref, bias_ref, out_ref, weight):
    n_dp, _, rows, width = w_ref.shape

    @pl.when(pl.program_id(0) == 0)
    def _():
        for r in range(RATE):
            for k in range(n_dp):
                weight[r, k * rows:(k + 1) * rows] = w_ref[k, r]

    row = lax.broadcasted_iota(jnp.int32, (176, SEG), 0)
    col = lax.broadcasted_iota(jnp.int32, (176, SEG), 1)
    total = jnp.zeros((176, width), F32)
    for r in range(RATE):
        pick = jnp.where((col == RATE * row + r) & (row < CC), 1.0, 0.0).astype(BF)
        taken = nn(pick, memory_ref[0]).astype(BF)
        total = total + nn(taken, weight[r])
    made = (total + bias_ref[...].astype(F32)).astype(BF)
    to = lax.broadcasted_iota(jnp.int32, (SEG, SEG), 0)
    of = lax.broadcasted_iota(jnp.int32, (SEG, SEG), 1)
    keep = jnp.where(of == to + CC, 1.0, 0.0).astype(BF)
    to = lax.broadcasted_iota(jnp.int32, (SEG, 176), 0)
    of = lax.broadcasted_iota(jnp.int32, (SEG, 176), 1)
    put = jnp.where((of == to - (CM - CC)) & (of < CC), 1.0, 0.0).astype(BF)
    out_ref[0] = (nn(keep, compressed_ref[0]) + nn(put, made)).astype(BF)


def compress(h, memory, compressed, w, bias):
    seqs, width = memory.shape[0], w.shape[3]
    return pl.pallas_call(
        compress_kernel,
        grid_spec=pltpu.PrefetchScalarGridSpec(
            num_scalar_prefetch=1,
            grid=(seqs,),
            in_specs=[
                pl.BlockSpec((1, SEG, D), lambda s, h: (s, 0, 0)),
                pl.BlockSpec((1, CM, width), lambda s, h: (s, 0, h[0])),
                whole(*w.shape),
                whole(1, width),
            ],
            out_specs=pl.BlockSpec((1, CM, width), lambda s, h: (s, 0, 0)),
            scratch_shapes=[pltpu.VMEM((RATE, D, width), BF)],
        ),
        out_shape=shape(seqs, CM, width),
        compiler_params=params(),
        cost_estimate=cost(8),
    )(h, memory, compressed, w, bias.reshape(1, -1))


def per_device(
    inputs,
    memory,
    compressed,
    slot_valid,
    slot_age,
    w_query,
    w_key,
    w_value,
    content_bias,
    w_out,
    ln_gain,
    ln_bias,
    w_up,
    up_bias,
    w_down,
    down_bias,
    w_comp,
    comp_bias,
    cotangent,
):
    n_dp = lax.axis_size("dp")
    d = lax.axis_index("dp")
    h = lax.axis_index("head")
    h1 = h.reshape(1)
    ids = jnp.stack([h, h ^ 2]).astype(jnp.int32)
    seqs = memory.shape[0]
    rows = w_key.shape[0]
    out_rows = w_out.shape[0]
    share, up_share = content_bias.shape[0], up_bias.shape[0]
    values = 4 * share + up_share
    sources = ring_sources(d, n_dp)
    pick = lambda a, n, axis: lax.dynamic_index_in_dim(a, n, axis, keepdims=False)

    ring = RingGather(
        pack(w_key, w_value, w_query, w_out, (content_bias, ln_gain, ln_bias, down_bias, up_bias)), n_dp)
    i = jnp.arange(SEG, dtype=jnp.int32)[None, :]
    j = jnp.arange(2 * SEG, dtype=jnp.int32)[:, None]
    gap = i + SEG - j
    near = jnp.where(gap >= 0, jnp.log1p(jnp.maximum(gap, 0).astype(F32)), FAR)

    def far_of(s):
        age, valid = pick(slot_age, s, 0)[:, None], pick(slot_valid, s, 0)[:, None]
        return jnp.where(valid > 0, jnp.log1p(jnp.maximum(i + age, 0).astype(F32)), FAR)

    far = [far_of(h), far_of(h ^ 2)]
    heads = jnp.concatenate([2 * h + jnp.arange(2), 2 * (h ^ 1) + jnp.arange(2)])
    slopes = 0.6 * jnp.power(0.7, heads.astype(F32))
    ffn_chunk = jnp.concatenate([w_up, w_down.T])

    inputs_x = x_swap(inputs)
    ring.step()
    ring.step(near)
    ring.step((far, slopes, ffn_chunk, sources))
    ring.step(inputs_x)
    cot_low = x_swap(after(inputs_x, cotangent[:SEG // 2]))
    chunks = ring.finish()
    pairs = [(chunk, c_swap(chunk)) for chunk in chunks]
    ffn = RingGather(ffn_chunk, n_dp)
    ffn.step((chunks[-1], chunks[-2]))

    def first_moves(index, ins, outs):
        for k in range(n_dp):
            at = pl.multiple_of(index[k] * rows, rows)
            for p in range(2):
                chunk = ins[2 * k + p]
                yield chunk.at[pl.ds(0, rows), pl.ds(0, 6 * HD)], outs[p].at[pl.ds(at, rows)]
                yield chunk.at[pl.ds(rows, 16), pl.ds(0, 2 * HD)], outs[2].at[p, index[k]]
            yield ins[2 * k].at[pl.ds(0, rows), pl.ds(6 * HD, 2 * HD)], outs[3].at[index[k]]

    w_own, w_par, small, wo = copies(
        first_moves, [(D, 6 * HD), (D, 6 * HD), (2, n_dp, 16, 2 * HD), (n_dp, rows, 2 * HD)], sources,
        *[chunk for pair in pairs for chunk in pair])
    small_x = x_swap(small)
    cot_high = x_swap(after(small_x, cotangent[SEG // 2:]))
    small = jnp.stack([small[0, :, 0, :values], small[1, :, 0, :values], small_x[0, :, 0, :values], small_x[1, :, 0, :values]])
    rank = jnp.arange(4) ^ h
    small = sum(jnp.where((rank == e)[None, :, None], small[e][:, None], 0) for e in range(4))
    small = small.reshape(4 * n_dp, values).astype(F32)
    wo = wo.reshape(n_dp, 4, out_rows, 2 * HD)
    wo_x = x_swap(wo)
    wo4 = (wo, c_swap(wo), wo_x, c_swap(wo_x))

    bias_all = small[:, :share].reshape(4, 2 * HD)
    lines = small[:, share:4 * share].reshape(4 * n_dp, 3, share).transpose(1, 0, 2).reshape(3, D)
    up_shift = small[:, 4 * share:].reshape(4, D)
    two = lambda a: jnp.concatenate([pick(a, h, 0), pick(a, h ^ 1, 0)]).reshape(1, -1)
    bias, up_shift = two(bias_all), two(up_shift)

    kv, q = project(h, compressed, memory, after(cot_low, inputs), w_own, w_par)
    ffn.step(kv)
    kv_x, q_x = project(h ^ 2, compressed, memory, after((kv, wo_x), inputs_x), w_own, w_par)
    bias = after((lines, up_shift), bias)
    mixed_x, lse_x = attend(0, slopes, q_x, bias, kv_x, near, far[1])
    ffn.step(mixed_x)
    sent = x_swap(mixed_x)
    mixed, lse = attend(0, slopes, after((mixed_x, cot_high), q), bias, kv, near, far[0])
    ffn.step(mixed)
    chunks = ffn.finish()

    ffn_par = [c_swap(chunk) for chunk in chunks]
    per = n_dp // 4

    def wo_moves(index, ins, outs):
        me = index[0]
        for e in range(4):
            for b in range(4):
                for p in range(4):
                    target = outs[0].at[me ^ b, :, me ^ e, :, pl.ds(p * 2 * HD, 2 * HD)]
                    yield ins[e].at[pl.ds(b * per, per), p], target

    (w_o,) = copies(wo_moves, [(4, per, 4, out_rows, D)], h1, *wo4)
    w_o = w_o.reshape(D, D)

    cot, cot_x = (cotangent[:SEG // 2], cotangent[SEG // 2:]), (cot_low, cot_high)
    residual, normed = attention_out(mixed, sent, w_o, inputs, lines)
    normed_x = x_swap(normed)
    hid, gb, up_cols, branch, gn = feed_forward(n_dp, sources, normed, cot, up_shift, chunks, ffn_par, F32)

    other = (c_swap(inputs), c_swap(inputs_x))

    def memory_moves(index, ins, outs):
        me = index[0]
        yield ins[0], outs[0].at[me]
        yield ins[1], outs[0].at[me ^ 2]
        yield ins[2], outs[0].at[me ^ 1]
        yield ins[3], outs[0].at[me ^ 3]

    (new_memory,) = copies(memory_moves, [(seqs, SEG, D)], h1, inputs, inputs_x, *other)
    comp_w = lax.all_gather(after((chunks[-1], normed), w_comp), "dp", axis=0).reshape(n_dp, RATE, rows, 2 * HD)
    new_compressed = compress(h1, memory, compressed, comp_w, comp_bias)

    hid_x, gb_x, up_cols_x, branch_x, gn_x = feed_forward(n_dp, sources, normed_x, cot_x, up_shift, chunks, ffn_par, BF)
    gn_x = x_swap(gn_x)
    acts = ((normed, normed_x), cot + cot_x, (gb, gb_x), (hid, hid_x))
    from_par = [c_swap(a) for a in ffn_grads(1, n_dp, *acts)]
    from_par = after((new_compressed, new_memory), *from_par)
    ffn_sum = RingScatter(ffn_grads(0, n_dp, *acts, *from_par).reshape(n_dp, 2 * rows, D), d, n_dp)
    gn_x = after(ffn_sum.f, gn_x)
    ffn_sum.step()
    grad_residual, do, do_x, sums, mine, theirs = norm_back(
        n_dp, h1, residual, gn, gn_x, cotangent, lines, mixed, sent, w_o)
    do_x = x_swap(do_x)
    keep, send = out_half(h1, mine, c_swap(theirs))
    do = after((ffn_sum.f, ffn_sum.b), do)
    ffn_sum.step(do)
    got = x_swap(send)
    branch_x = x_swap(after((gn_x, got), branch_x))
    dq, dkv, q_cols = attend_back(0, slopes, q, bias, kv, near, far[0], mixed, lse, do)
    do_x = after((ffn_sum.f, ffn_sum.b), do_x)
    ffn_sum.step(dq)
    branch_x = after(dq, branch_x)
    output = add_up(BF, residual, branch, branch_x, lines[2:])
    term = token_term(dq, dkv, w_own, w_par, grad_residual)
    dq_x, dkv_x, q_cols_x = attend_back(0, slopes, q_x, bias, kv_x, near, far[1], mixed_x, lse_x, do_x)
    ffn_sum.step(dq_x)
    dq_x = after(got, dq_x)
    term_x = token_term(dq_x, dkv_x, w_own, w_par)
    term_sent = x_swap(term_x)
    grad_input = add_up(F32, term, term_sent)

    lane = jnp.arange(4)[:, None]

    def place(a):
        a = a.reshape(2, 1, -1)
        return jnp.where(lane == h, a[0], 0.0) + jnp.where(lane == h ^ 1, a[1], 0.0)

    tiny = jnp.concatenate([
        place(q_cols + q_cols_x).reshape(-1, share),
        sums[0].reshape(-1, share),
        sums[1].reshape(-1, share),
        sums[2].reshape(-1, share),
        place(up_cols + up_cols_x).reshape(-1, up_share),
    ], axis=1)
    tiny = tiny + x_swap(tiny)
    dq, dkv = after((tiny, term_x), dq, dkv)
    tiny = tiny + c_swap(tiny)
    tiny = jnp.pad(tiny.astype(BF).reshape(n_dp, 4, values), ((0, 0), (0, 12), (0, 2 * HD - values)))

    work = (ids, compressed, memory, inputs, inputs_x, (dkv, dkv_x), (dq, dq_x))
    from_par = weight_grads(1, n_dp, *work)
    from_par = after(ffn_sum.f, *from_par)
    from_par = [c_swap(a) for a in from_par]
    grad_up, grad_down = ffn_sum.finish(close_ffn_kernel, [(rows, D), (D, rows)])
    g_sum = RingScatter(weight_grads(0, n_dp, *work, *from_par, tiny, keep, got), d, n_dp)
    g_sum.step()
    g_sum.step((grad_up, grad_down))
    g_sum.step(term)
    g_sum.step(output)
    grad_key, grad_value, grad_query, grad_out, tiny = g_sum.finish(
        close_last_kernel, [(rows, 2 * HD), (rows, 2 * HD), (rows, 2 * HD), (out_rows, D), (16, 2 * HD)])
    tiny = pick(tiny, h, 0)

    return (
        output,
        grad_input,
        grad_query,
        grad_key,
        grad_value,
        tiny[:share],
        grad_out,
        tiny[share:2 * share],
        tiny[2 * share:3 * share],
        grad_up,
        tiny[4 * share:values],
        grad_down,
        tiny[3 * share:4 * share],
        new_memory,
        new_compressed,
    )


def solution(mesh):
    both = ("dp", "head")
    in_specs = (
        P(both, None),
        P("dp", None, None),
        P("dp", None, None),
        P("dp", None),
        P("dp", None),
        P("dp", "head"),
        P("dp", "head"),
        P("dp", "head"),
        P(both),
        P(both, None),
        P(both),
        P(both),
        P("dp", "head"),
        P(both),
        P("head", "dp"),
        P(both),
        P(None, "dp", "head"),
        P("head"),
        P(both, None),
    )
    out_specs = (
        P(both, None),
        P(both, None),
        P("dp", "head"),
        P("dp", "head"),
        P("dp", "head"),
        P(both),
        P(both, None),
        P(both),
        P(both),
        P("dp", "head"),
        P(both),
        P("head", "dp"),
        P(both),
        P("dp", None, None),
        P("dp", None, "head"),
    )
    return jax.shard_map(per_device, mesh=mesh, in_specs=in_specs, out_specs=out_specs, check_vma=False)
```

```python
import functools

import jax
import jax.numpy as jnp
from jax import lax
from jax.experimental import pallas as pl
from jax.experimental.pallas import tpu as pltpu
from jax.sharding import PartitionSpec as P

D = 1024
HD = 128
SEG = 512
CM = 512
RATE = 3
CC = 171
LN_EPS = 1e-05
LOG2E = 1.4426950408889634
SCALE2 = LOG2E * HD ** (-0.5)
FAR = 1e32
VMEM = 56 * 1024 * 1024
BF = jnp.bfloat16
F32 = jnp.float32


def nt(a, b):
    return lax.dot_general(a, b, (((1,), (1,)), ((), ())), preferred_element_type=F32)


def tn(a, b):
    return lax.dot_general(a, b, (((0,), (0,)), ((), ())), preferred_element_type=F32)


def nn(a, b):
    return jnp.dot(a, b, preferred_element_type=F32)


def x_swap(a):
    return lax.ppermute(a, "head", [(i, i ^ 2) for i in range(4)])


def c_swap(a):
    return lax.ppermute(a, "head", [(i, i ^ 1) for i in range(4)])


PIECES = ((0, SEG, 0), (SEG, 2 * SEG, 0), (2 * SEG, 5 * SEG // 2, 0), (5 * SEG // 2, 3 * SEG, SEG // 2))


def decay(near_ref, far_ref, low, high, first):
    return far_ref[low:high, first:] if high <= SEG else near_ref[low - SEG:high - SEG, first:]


def from_column(first, old, new, join):
    return join(old, new) if not first else jnp.concatenate([old[:, :first], join(old[:, first:], new)], axis=1)


def fwd_kernel(slope_ref, q_ref, bias_ref, kv_ref, near_ref, far_ref, mixed_ref, lse_ref):
    slope2 = slope_ref[pl.program_id(0)] * LOG2E
    q = (q_ref[0] + bias_ref[...]).astype(BF)
    parts = []
    top = None
    for low, high, first in PIECES:
        part = nt(kv_ref[0, low:high, :HD], q[first:]) * SCALE2 - slope2 * decay(near_ref, far_ref, low, high, first)
        peak = jnp.max(part, axis=0, keepdims=True)
        top = peak if top is None else from_column(first, top, peak, jnp.maximum)
        parts.append(part)
    total = jnp.zeros((1, SEG), F32)
    acc = jnp.zeros((HD, SEG), F32)
    for (low, high, first), part in zip(PIECES, parts):
        p = jnp.exp2(part - top[:, first:])
        total = from_column(first, total, jnp.sum(p, axis=0, keepdims=True), jnp.add)
        acc = from_column(first, acc, tn(kv_ref[0, low:high, HD:], p.astype(BF)), jnp.add)
    mixed_ref[...] = (acc / total).T.astype(BF)
    lse_ref[...] = (top + jnp.log2(total)).reshape(1, 1, SEG)


def bwd_kernel(slope_ref, q_ref, bias_ref, kv_ref, near_ref, far_ref, mixed_ref, lse_ref, do_ref, dq_ref, dkv_ref, sum_ref):
    slope2 = slope_ref[pl.program_id(0)] * LOG2E
    q = (q_ref[0] + bias_ref[...]).astype(BF)
    do = do_ref[...]
    lse = lse_ref[...].reshape(1, SEG)
    row_dot = jnp.sum((do.astype(F32) * mixed_ref[...].astype(F32)).T, axis=0, keepdims=True)
    inv_root = HD ** (-0.5)
    dq = jnp.zeros((HD, SEG), F32)
    for low, high, first in PIECES:
        k = kv_ref[0, low:high, :HD]
        v = kv_ref[0, low:high, HD:]
        table = decay(near_ref, far_ref, low, high, first)
        p = jnp.exp2(nt(k, q[first:]) * SCALE2 - slope2 * table - lse[:, first:])
        ds = (p * (nt(v, do[first:]) - row_dot[:, first:])).astype(BF)
        dkv_ref[low:high, HD:] = nn(p.astype(BF), do[first:]).astype(BF)
        dkv_ref[low:high, :HD] = (nn(ds, q[first:]) * inv_root).astype(BF)
        dq = from_column(first, dq, tn(k, ds), jnp.add)
    dq = (dq.T * inv_root).astype(BF)
    dq_ref[...] = dq
    sum_ref[...] = jnp.sum(dq.astype(F32), axis=0, keepdims=True)


def ring_order(n):
    up = list(range(0, n, 2))
    return up + [p + 1 for p in reversed(up)]


def ring_perms(n):
    order = ring_order(n)
    ahead = [(order[p], order[(p + 1) % n]) for p in range(n)]
    return ahead, [(b, a) for a, b in ahead]


def ring_place(d, n):
    return jnp.where(d % 2 == 0, d // 2, n - 1 - d // 2)


def ring_member(p, n):
    p = p % n
    return jnp.where(p < n // 2, 2 * p, 2 * (n - 1 - p) + 1)


def after(first, *then):
    out = lax.optimization_barrier((first,) + then)[1:]
    return out if len(then) > 1 else out[0]


class RingGather:
    def __init__(self, chunk, n):
        self.n, self.k = n, 0
        self.ahead, self.back = ring_perms(n)
        self.f = self.b = chunk
        self.chunks = [chunk]

    def step(self, first=None):
        self.k += 1
        if self.k > self.n // 2:
            return
        if first is not None:
            self.f, self.b = after(first, self.f, self.b)
        self.f = lax.ppermute(self.f, "dp", self.ahead)
        self.chunks.append(self.f)
        if self.k < self.n - self.n // 2:
            self.b = lax.ppermute(self.b, "dp", self.back)
            self.chunks.append(self.b)

    def finish(self):
        while self.k < self.n // 2:
            self.step()
        return self.chunks


def ring_sources(d, n):
    place = ring_place(d, n)
    steps = [0]
    for k in range(1, n // 2 + 1):
        steps.append(-k)
        if k < n - n // 2:
            steps.append(k)
    return ring_member(place + jnp.array(steps, jnp.int32), n).astype(jnp.int32)


ROWS = 3 * SEG
HALF = D // 2
smem_spec = pl.BlockSpec(memory_space=pltpu.SMEM)
vmem_spec = pl.BlockSpec(memory_space=pltpu.VMEM)
any_spec = pl.BlockSpec(memory_space=pl.ANY)


def params():
    return pltpu.CompilerParams(vmem_limit_bytes=VMEM)


def cost(us):
    return pl.CostEstimate(flops=int(us * 0.18e9), bytes_accessed=1, transcendentals=0)


def shape(*dims, kind=BF):
    return jax.ShapeDtypeStruct(dims, kind)


def whole(*dims):
    return pl.BlockSpec(dims, lambda *i: (0,) * len(dims))


def attend(t, slopes, q, bias, kv, near, far):
    return pl.pallas_call(
        fwd_kernel,
        grid=(4,),
        in_specs=[
            smem_spec,
            pl.BlockSpec((1, SEG, HD), lambda a: (t, 0, a)),
            pl.BlockSpec((1, HD), lambda a: (0, a)),
            pl.BlockSpec((1, ROWS, 2 * HD), lambda a: (t, 0, a)),
            whole(2 * SEG, SEG),
            whole(SEG, SEG),
        ],
        out_specs=[pl.BlockSpec((SEG, HD), lambda a: (0, a)), pl.BlockSpec((1, 1, SEG), lambda a: (a, 0, 0))],
        out_shape=[shape(SEG, HALF), shape(4, 1, SEG, kind=F32)],
        compiler_params=params(),
        cost_estimate=cost(9),
    )(slopes, q, bias, kv, near, far)


def attend_back(t, slopes, q, bias, kv, near, far, mixed, lse, do):
    column = pl.BlockSpec((SEG, HD), lambda a: (0, a))
    return pl.pallas_call(
        bwd_kernel,
        grid=(4,),
        in_specs=[
            smem_spec,
            pl.BlockSpec((1, SEG, HD), lambda a: (t, 0, a)),
            pl.BlockSpec((1, HD), lambda a: (0, a)),
            pl.BlockSpec((1, ROWS, 2 * HD), lambda a: (t, 0, a)),
            whole(2 * SEG, SEG),
            whole(SEG, SEG),
            column,
            pl.BlockSpec((1, 1, SEG), lambda a: (a, 0, 0)),
            column,
        ],
        out_specs=[column, pl.BlockSpec((ROWS, 2 * HD), lambda a: (0, a)), pl.BlockSpec((1, HD), lambda a: (0, a))],
        out_shape=[shape(SEG, HALF), shape(ROWS, D), shape(1, HALF, kind=F32)],
        compiler_params=params(),
        cost_estimate=cost(12),
    )(slopes, q, bias, kv, near, far, mixed, lse, do)


def pack_kernel(key_ref, value_ref, query_ref, out_ref, *rest):
    smalls, pack_ref = rest[:-1], rest[-1]
    rows = key_ref.shape[0]
    piece = out_ref.shape[0]
    pack_ref[:rows, :HD] = key_ref[:, :HD]
    pack_ref[:rows, HD:2 * HD] = value_ref[:, :HD]
    pack_ref[:rows, 2 * HD:3 * HD] = key_ref[:, HD:]
    pack_ref[:rows, 3 * HD:4 * HD] = value_ref[:, HD:]
    pack_ref[:rows, 4 * HD:6 * HD] = query_ref[...]
    for k in range(4):
        pack_ref[k * piece:(k + 1) * piece, 6 * HD:] = out_ref[:, k * 2 * HD:(k + 1) * 2 * HD]
    line = jnp.concatenate([a[...].astype(F32) for a in smalls], axis=1)
    line = jnp.concatenate([line, jnp.zeros((1, D - line.shape[1]), F32)], axis=1)
    row = lax.broadcasted_iota(jnp.int32, (16, D), 0)
    pack_ref[rows:] = jnp.where(row == 0, jnp.broadcast_to(line, (16, D)), 0.0).astype(BF)


def pack(w_key, w_value, w_query, w_out, smalls):
    return pl.pallas_call(
        pack_kernel,
        in_specs=[vmem_spec] * (4 + len(smalls)),
        out_specs=vmem_spec,
        out_shape=shape(w_key.shape[0] + 16, D),
        compiler_params=params(),
        cost_estimate=cost(1),
    )(w_key, w_value, w_query, w_out, *[a.reshape(1, -1) for a in smalls])


def project_kernel(id_ref, comp_ref, mem_ref, token_ref, w_own_ref, w_par_ref, kv_ref, q_ref, source, own, par, sems):
    n = pl.program_id(0)
    blocks = (comp_ref.at[id_ref[0]], mem_ref.at[id_ref[0]], token_ref)
    moves = [pltpu.make_async_copy(a, source.at[k], sems.at[k]) for k, a in enumerate(blocks)]
    own_move = pltpu.make_async_copy(w_own_ref, own, sems.at[3])
    par_move = pltpu.make_async_copy(w_par_ref, par, sems.at[4])

    @pl.when(n == 0)
    def _():
        own_move.start()
        moves[0].start()
        par_move.start()
        moves[1].start()
        moves[2].start()
        own_move.wait()

    for k in range(3):
        pl.when(n == k)(moves[k].wait)
    a = source[n]
    kv_ref[0, :, :HALF] = nn(a, own[:, :HALF]).astype(BF)
    pl.when(n == 0)(par_move.wait)
    kv_ref[0, :, HALF:] = nn(a, par[:, :HALF]).astype(BF)

    @pl.when(n == 2)
    def _():
        q_ref[0, :, :2 * HD] = nn(a, own[:, HALF:])
        q_ref[0, :, 2 * HD:] = nn(a, par[:, HALF:])


def project(seq, compressed, memory, tokens, w_own, w_par):
    return pl.pallas_call(
        project_kernel,
        grid_spec=pltpu.PrefetchScalarGridSpec(
            num_scalar_prefetch=1,
            grid=(3,),
            in_specs=[any_spec] * 5,
            out_specs=[
                pl.BlockSpec((1, SEG, D), lambda n, seq: (0, n, 0)),
                pl.BlockSpec((1, SEG, HALF), lambda n, seq: (0, 0, 0)),
            ],
            scratch_shapes=[
                pltpu.VMEM((3, SEG, D), BF),
                pltpu.VMEM((D, 6 * HD), BF),
                pltpu.VMEM((D, 6 * HD), BF),
                pltpu.SemaphoreType.DMA((5,)),
            ],
        ),
        out_shape=[shape(1, ROWS, D), shape(1, SEG, HALF, kind=F32)],
        compiler_params=params(),
        cost_estimate=cost(8),
    )(seq.reshape(1), compressed, memory, tokens, w_own, w_par)


def norm_kernel(mixed_ref, sent_ref, w_ref, in_ref, lines_ref, residual_ref, normed_ref):
    out = nn(mixed_ref[...], w_ref[:HALF]) + nn(sent_ref[...], w_ref[HALF:])
    residual = in_ref[...].astype(F32) + out
    residual_ref[...] = residual
    center = residual - jnp.mean(residual, axis=-1, keepdims=True)
    rstd = lax.rsqrt(jnp.mean(center * center, axis=-1, keepdims=True) + LN_EPS)
    normed_ref[...] = (center * rstd * lines_ref[0:1] + lines_ref[1:2]).astype(BF)


def attention_out(mixed, sent, w_o, inputs, lines):
    rows = SEG // 2
    half = pl.BlockSpec((rows, HALF), lambda i: (i, 0))
    full = pl.BlockSpec((rows, D), lambda i: (i, 0))
    return pl.pallas_call(
        norm_kernel,
        grid=(2,),
        in_specs=[half, half, whole(D, D), full, whole(3, D)],
        out_specs=[full, full],
        out_shape=[shape(SEG, D, kind=F32), shape(SEG, D)],
        compiler_params=params(),
        cost_estimate=cost(4),
    )(mixed, sent, w_o, inputs, lines)


def gelu_pair(before):
    c0, c1 = 0.7978845608028654, 0.044715
    sq = before * before
    t = jnp.tanh(c0 * before * (1.0 + c1 * sq))
    half = 0.5 * (1.0 + t)
    return before * half, half + 0.5 * before * (1.0 - t * t) * (c0 * (1.0 + 3.0 * c1 * sq))


def ffn_kernel(n_dp, index_ref, norm_ref, low_ref, high_ref, bias_ref, *refs):
    chunks = refs[:2 * n_dp]
    hid_ref, gb_ref, sum_ref, branch_ref, gn_ref, up_ref, down_ref, branch, gn, sems = refs[2 * n_dp:]
    i, tiles = pl.program_id(0), up_ref.shape[0]
    tile, rows = up_ref.shape[2], D // n_dp

    def moves(step):
        group, column = divmod(step, tiles // 2)
        for k in range(n_dp):
            source = chunks[group * n_dp + k]
            at = pl.ds(pl.multiple_of(index_ref[k] * rows, rows), rows)
            for m, target in enumerate((up_ref, down_ref)):
                yield pltpu.make_async_copy(
                    source.at[pl.ds(m * rows, rows), pl.ds(column * tile, tile)],
                    target.at[step, at],
                    sems.at[(step * n_dp + k) * 2 + m],
                )

    @pl.when(i == 0)
    def _():
        for step in range(tiles):
            for move in moves(step):
                move.start()

    for step in range(tiles):
        @pl.when(i == step)
        def _(step=step):
            for move in moves(step):
                move.wait()

    up, down = up_ref.at[i], down_ref.at[i]
    total = jnp.zeros((1, tile), F32)
    half = SEG // 2
    for c, cot_ref in enumerate((low_ref, high_ref)):
        part = slice(c * half, (c + 1) * half)
        act, slope = gelu_pair(nn(norm_ref[part], up[...]) + bias_ref[...])
        act = act.astype(BF)
        gb = (nn(cot_ref[...], down[...]) * slope).astype(BF)
        hid_ref[part] = act
        gb_ref[part] = gb
        total = total + jnp.sum(gb.astype(F32), axis=0, keepdims=True)
        branch[part] = jnp.where(i > 0, branch[part], 0.0) + nt(act, down[...])
        gn[part] = jnp.where(i > 0, gn[part], 0.0) + nt(gb, up[...])
    sum_ref[...] = total

    @pl.when(i == tiles - 1)
    def _():
        branch_ref[...] = branch[...].astype(branch_ref.dtype)
        gn_ref[...] = gn[...].astype(gn_ref.dtype)


def feed_forward(n_dp, sources, norm, cot, bias, own, par, kind, tile=1024):
    tiles = 2 * D // tile
    part = pl.BlockSpec((SEG, tile), lambda i, index: (0, i))
    line = pl.BlockSpec((1, tile), lambda i, index: (0, i))
    return pl.pallas_call(
        functools.partial(ffn_kernel, n_dp),
        grid_spec=pltpu.PrefetchScalarGridSpec(
            num_scalar_prefetch=1,
            grid=(tiles,),
            in_specs=[whole(SEG, D), whole(SEG // 2, D), whole(SEG // 2, D), line] + [any_spec] * (2 * n_dp),
            out_specs=[part, part, line, whole(SEG, D), whole(SEG, D)],
            scratch_shapes=[pltpu.VMEM((tiles, D, tile), BF)] * 2
            + [pltpu.VMEM((SEG, D), F32)] * 2
            + [pltpu.SemaphoreType.DMA((2 * tiles * n_dp,))],
        ),
        out_shape=[shape(SEG, 2 * D), shape(SEG, 2 * D), shape(1, 2 * D, kind=F32), shape(SEG, D, kind=kind), shape(SEG, D, kind=kind)],
        compiler_params=params(),
        cost_estimate=cost(16),
    )(sources, norm, *cot, bias, *own, *par)


def ffn_grad_kernel(tiles, n0, n1, c0_low, c0_high, c1_low, c1_high, gb0, gb1, hid0, hid1, *rest):
    parts, outs = (rest[:-1], rest[-1:]) if len(rest) > 2 * tiles else ((), rest)
    step = pl.program_id(0) * tiles + pl.program_id(1)
    for m in range(2):
        for i in range(tiles):
            k = m * tiles + i

            @pl.when(step == k)
            def _(m=m, k=k):
                if m == 0:
                    total = tn(n0[...], gb0[...]) + tn(n1[...], gb1[...])
                else:
                    half = SEG // 2
                    total = tn(c0_low[...], hid0[:half]) + tn(c0_high[...], hid0[half:])
                    total = total + tn(c1_low[...], hid1[:half]) + tn(c1_high[...], hid1[half:])
                if parts:
                    out = outs[0]
                    total = total.reshape(out.shape[0], out.shape[2], -1)
                    out[:, 0] = (total + parts[k][...].astype(F32)).astype(BF)
                else:
                    outs[k][...] = total.reshape(outs[k].shape).astype(BF)


def ffn_grads(g, n_dp, norms, cots, gbs, hids, *received, tile=512):
    n = D // tile
    rows = D // n_dp
    tokens = whole(SEG, D)
    early = pl.BlockSpec((SEG, tile), lambda m, i: (0, g * n + jnp.where(m == 0, i, n - 1)))
    late = pl.BlockSpec((SEG, tile), lambda m, i: (0, g * n + jnp.where(m == 0, 0, i)))
    part = whole(n_dp, rows, tile)
    if received:
        out_specs = pl.BlockSpec((n_dp, 1, rows, tile), lambda m, i: (0, m, 0, i))
        out_shape = shape(n_dp, 2, rows, D)
    else:
        out_specs, out_shape = [part] * (2 * n), [shape(n_dp, rows, tile)] * (2 * n)
    return pl.pallas_call(
        functools.partial(ffn_grad_kernel, n),
        grid=(2, n),
        in_specs=[tokens] * 2 + [whole(SEG // 2, D)] * 4 + [early] * 2 + [late] * 2 + [part] * len(received),
        out_specs=out_specs,
        out_shape=out_shape,
        compiler_params=params(),
        cost_estimate=cost(10),
    )(*norms, *cots, *gbs, *hids, *received)


def norm_back_kernel(h_ref, residual_ref, gn_ref, gnx_ref, cot_ref, lines_ref, mixed_ref, sent_ref, w_ref,
                     grad_ref, keep_ref, send_ref, sums_ref, mine_ref, theirs_ref, acc):
    i = pl.program_id(0)
    residual = residual_ref[...]
    center = residual - jnp.mean(residual, axis=-1, keepdims=True)
    rstd = lax.rsqrt(jnp.mean(center * center, axis=-1, keepdims=True) + LN_EPS)
    xhat = center * rstd
    gn = gn_ref[...] + gnx_ref[...].astype(F32)
    g = gn * lines_ref[0:1]
    cot = cot_ref[...].astype(F32)
    grad = cot + rstd * (g - jnp.mean(g, axis=-1, keepdims=True) - xhat * jnp.mean(g * xhat, axis=-1, keepdims=True))
    grad_ref[...] = grad
    low = grad.astype(BF)
    keep_ref[...] = nt(low, w_ref[:HALF]).astype(BF)
    send_ref[...] = nt(low, w_ref[HALF:]).astype(BF)
    total = lambda a: jnp.sum(a, axis=0, keepdims=True)
    sums = jnp.concatenate([total(gn * xhat), total(gn), total(cot)], axis=0)

    @pl.when(i == 0)
    def _():
        sums_ref[...] = sums
        acc[:HALF] = tn(mixed_ref[...], low)
        acc[HALF:] = tn(sent_ref[...], low)

    @pl.when(i > 0)
    def _():
        sums_ref[...] += sums
        acc[:HALF] += tn(mixed_ref[...], low)
        acc[HALF:] += tn(sent_ref[...], low)

    @pl.when(i == pl.num_programs(0) - 1)
    def _():
        per = mine_ref.shape[0] // 4
        first = h_ref[0] % 2 == 0
        for b in range(4):
            block = acc[b * 2 * HD:(b + 1) * 2 * HD].reshape(per, 2, 2, mine_ref.shape[2], D)
            at = pl.ds((h_ref[0] ^ b) * per, per)
            mine_ref[at] = jnp.where(first, block[:, :, 0], block[:, :, 1]).astype(BF)
            theirs_ref[at] = jnp.where(first, block[:, :, 1], block[:, :, 0]).astype(BF)


def out_half_kernel(h_ref, mine_ref, got_ref, keep_ref, send_ref):
    total = mine_ref[...].astype(F32) + got_ref[...].astype(F32)
    first = h_ref[0] // 2 == 0
    keep_ref[...] = jnp.where(first, total[:, 0], total[:, 1]).astype(BF)
    send_ref[...] = jnp.where(first, total[:, 1], total[:, 0]).astype(BF)


def out_half(h, mine, got):
    n_dp, _, rows, _ = mine.shape
    return pl.pallas_call(
        out_half_kernel,
        in_specs=[smem_spec, vmem_spec, vmem_spec],
        out_specs=[vmem_spec, vmem_spec],
        out_shape=[shape(n_dp, rows, D)] * 2,
        compiler_params=pltpu.CompilerParams(vmem_limit_bytes=16 << 20),
        cost_estimate=cost(1),
    )(h, mine, got)


def norm_back(n_dp, h, residual, gn, gnx, cot, gain, mixed, sent, w_o):
    rows = SEG // 2
    half = pl.BlockSpec((rows, HALF), lambda i: (i, 0))
    full = pl.BlockSpec((rows, D), lambda i: (i, 0))
    return pl.pallas_call(
        norm_back_kernel,
        grid=(2,),
        in_specs=[smem_spec, full, full, full, full, whole(3, D), half, half, whole(D, D)],
        out_specs=[full, half, half, whole(3, D)] + [whole(n_dp, 2, D // n_dp // 4, D)] * 2,
        out_shape=[shape(SEG, D, kind=F32), shape(SEG, HALF), shape(SEG, HALF), shape(3, D, kind=F32)] + [shape(n_dp, 2, D // n_dp // 4, D)] * 2,
        scratch_shapes=[pltpu.VMEM((D, D), F32)],
        compiler_params=params(),
        cost_estimate=cost(10),
    )(h, residual, gn, gnx, cot, gain, mixed, sent, w_o)


def term_kernel(dq_ref, dkv_ref, w_own_ref, w_par_ref, *rest):
    out = nt(dkv_ref[:, :HALF], w_own_ref[:, :HALF]) + nt(dkv_ref[:, HALF:], w_par_ref[:, :HALF])
    out = out + nt(dq_ref[:, :2 * HD], w_own_ref[:, HALF:]) + nt(dq_ref[:, 2 * HD:], w_par_ref[:, HALF:])
    if len(rest) > 1:
        out = out + rest[0][...]
    rest[-1][...] = out.astype(rest[-1].dtype)


def token_term(dq, dkv, w_own, w_par, *residual):
    rows = SEG // 2
    full = pl.BlockSpec((rows, D), lambda i: (i, 0))
    weight = whole(D, 3 * 2 * HD)
    return pl.pallas_call(
        term_kernel,
        grid=(2,),
        in_specs=[
            pl.BlockSpec((rows, HALF), lambda i: (i, 0)),
            pl.BlockSpec((rows, D), lambda i: (4 + i, 0)),
            weight,
            weight,
        ] + [full] * len(residual),
        out_specs=full,
        out_shape=shape(SEG, D, kind=F32 if residual else BF),
        compiler_params=params(),
        cost_estimate=cost(4),
    )(dq, dkv, w_own, w_par, *residual)


def weight_grad_kernel(g, ids_ref, comp_ref, mem_ref, own_ref, other_ref, dkv0, dkv1, dq0, dq1, *rest):
    step = pl.program_id(0)
    source, grads, query_grads, acc, sems = rest[-5:]
    parts, outs = (rest[:2], rest[5:6]) if len(rest) > 8 else ((), rest[:2])
    half = rest[0].shape[0]
    rows = D // (2 * half)
    blocks = []
    for t, (tokens, dkv) in enumerate(((own_ref, dkv0), (other_ref, dkv1))):
        for n, a in enumerate((comp_ref.at[ids_ref[t]], mem_ref.at[ids_ref[t]], tokens)):
            blocks.append((a, dkv.at[pl.ds(n * SEG, SEG), pl.ds(g * HALF, HALF)]))
    moves = [
        (pltpu.make_async_copy(a, source.at[k], sems.at[2 * k]), pltpu.make_async_copy(b, grads.at[k], sems.at[2 * k + 1]))
        for k, (a, b) in enumerate(blocks)
    ]
    extra = [
        pltpu.make_async_copy(a.at[:, pl.ds(g * 2 * HD, 2 * HD)], query_grads.at[k], sems.at[12 + k])
        for k, a in enumerate((dq0, dq1))
    ]

    @pl.when(step == 0)
    def _():
        for pair in moves:
            pair[0].start()
            pair[1].start()
        extra[0].start()
        extra[1].start()

    for k in range(6):
        @pl.when(step == k)
        def _(k=k):
            moves[k][0].wait()
            moves[k][1].wait()
            if k == 0:
                acc[:, :HALF] = tn(source[k], grads[k])
            else:
                acc[:, :HALF] += tn(source[k], grads[k])
            if k == 2:
                extra[0].wait()
                acc[:, HALF:] = tn(source[k], query_grads[0])
            if k < 5:
                return
            extra[1].wait()
            acc[:, HALF:] += tn(source[k], query_grads[1])
            total = acc[...].reshape(2 * half, rows, 6 * HD)
            for p in range(2):
                block = slice(p * half, (p + 1) * half)
                if parts:
                    outs[0][block, :rows] = (total[block] + parts[p][...].astype(F32)).astype(BF)
                else:
                    outs[p][...] = total[block].astype(BF)
            if parts:
                tiny, mine, got = rest[2:5]
                out_rows = mine.shape[1]
                other = (mine[...].astype(F32) + got[...].astype(F32)).astype(BF)
                low = rows + (outs[0].shape[1] - rows) // 2
                outs[0][:, rows:] = jnp.zeros((2 * half, outs[0].shape[1] - rows, 6 * HD), BF)
                outs[0][:, rows:rows + out_rows] = other[:, :, :6 * HD]
                outs[0][:, low:low + out_rows, :2 * HD] = other[:, :, 6 * HD:]
                outs[0][:, low:low + 16, 2 * HD:4 * HD] = tiny[...]


def weight_grads(g, n_dp, ids, compressed, memory, own, other, dkvs, dqs, *received):
    rows = D // n_dp
    if received:
        extra = 2 * max(16, received[-1].shape[1])
        out_specs, out_shape = whole(n_dp, rows + extra, 6 * HD), shape(n_dp, rows + extra, 6 * HD)
    else:
        out_specs, out_shape = [whole(n_dp // 2, rows, 6 * HD)] * 2, [shape(n_dp // 2, rows, 6 * HD)] * 2
    return pl.pallas_call(
        functools.partial(weight_grad_kernel, g),
        grid_spec=pltpu.PrefetchScalarGridSpec(
            num_scalar_prefetch=1,
            grid=(6,),
            in_specs=[any_spec] * 8 + [whole(*a.shape) for a in received],
            out_specs=out_specs,
            scratch_shapes=[
                pltpu.VMEM((6, SEG, D), BF),
                pltpu.VMEM((6, SEG, HALF), BF),
                pltpu.VMEM((2, SEG, 2 * HD), BF),
                pltpu.VMEM((D, 6 * HD), F32),
                pltpu.SemaphoreType.DMA((14,)),
            ],
        ),
        out_shape=out_shape,
        compiler_params=params(),
        cost_estimate=cost(10),
    )(ids, compressed, memory, own, other, *dkvs, *dqs, *received)


def copies(moves, out_shapes, index, *arrays):
    count = len(arrays)

    def kernel(index_ref, *refs):
        ins, outs, sems = refs[:count], refs[count:-1], refs[-1]
        started = []
        for n, (source, target) in enumerate(moves(index_ref, ins, outs)):
            copy = pltpu.make_async_copy(source, target, sems.at[n])
            copy.start()
            started.append(copy)
        for copy in started:
            copy.wait()

    return pl.pallas_call(
        kernel,
        in_specs=[smem_spec] + [any_spec] * count,
        out_specs=[vmem_spec] * len(out_shapes),
        out_shape=[shape(*dims) for dims in out_shapes],
        scratch_shapes=[pltpu.SemaphoreType.DMA((192,))],
        compiler_params=pltpu.CompilerParams(vmem_limit_bytes=16 << 20),
        cost_estimate=cost(0),
    )(index, *arrays)


def assemble(chunks, sources, parts):
    n, cols = len(chunks), chunks[0].shape[1]

    def moves(index, ins, outs):
        for k in range(n):
            row = 0
            for out, rows in zip(outs, parts):
                yield ins[k].at[pl.ds(row, rows)], out.at[pl.ds(pl.multiple_of(index[k] * rows, rows), rows)]
                row += rows

    return copies(moves, [(n * rows, cols) for rows in parts], sources, *chunks)


def pick_kernel(index_ref, ahead_ref, back_ref, f_ref, b_ref):
    f_ref[...] = ahead_ref[0]
    b_ref[...] = back_ref[0]


def add_kernel(index_ref, f_in, b_in, ahead_ref, back_ref, f_ref, b_ref):
    f_ref[...] = (f_in[...].astype(F32) + ahead_ref[0].astype(F32)).astype(BF)
    b_ref[...] = (b_in[...].astype(F32) + back_ref[0].astype(F32)).astype(BF)


def add_one_kernel(index_ref, f_in, ahead_ref, back_ref, f_ref):
    f_ref[...] = (f_in[...].astype(F32) + ahead_ref[0].astype(F32)).astype(BF)


def close_kernel(index_ref, f_in, b_in, own_ref, _, out_ref):
    out_ref[...] = f_in[...].astype(F32) + b_in[...].astype(F32) + own_ref[0].astype(F32)


def close_ffn_kernel(index_ref, f_in, b_in, own_ref, _, up_ref, down_ref):
    total = f_in[...].astype(F32) + b_in[...].astype(F32) + own_ref[0].astype(F32)
    rows = up_ref.shape[0]
    up_ref[...] = total[:rows]
    down_ref[...] = total[rows:].T


def close_last_kernel(index_ref, f_in, b_in, own_ref, _, key_ref, value_ref, query_ref, out_ref, small_ref):
    total = f_in[...].astype(F32) + b_in[...].astype(F32) + own_ref[0].astype(F32)
    rows, out_rows = key_ref.shape[0], out_ref.shape[0]
    low = rows + (total.shape[0] - rows) // 2
    key_ref[:, :HD] = total[:rows, :HD]
    value_ref[:, :HD] = total[:rows, HD:2 * HD]
    key_ref[:, HD:] = total[:rows, 2 * HD:3 * HD]
    value_ref[:, HD:] = total[:rows, 3 * HD:4 * HD]
    query_ref[...] = total[:rows, 4 * HD:]
    out_ref[:, :6 * HD] = total[rows:rows + out_rows]
    out_ref[:, 6 * HD:] = total[low:low + out_rows, :2 * HD]
    small_ref[...] = total[low:low + 16, 2 * HD:4 * HD]


def ring_kernel(kernel, array, places, given, outs):
    _, rows, cols = array.shape
    shapes = [shape(rows, cols)] * outs if isinstance(outs, int) else [shape(*dims, kind=F32) for dims in outs]
    flat = pl.BlockSpec((rows, cols), lambda i, index: (0, 0))
    block = lambda k: pl.BlockSpec((1, rows, cols), lambda i, index: (index[k], 0, 0))
    return pl.pallas_call(
        kernel,
        grid_spec=pltpu.PrefetchScalarGridSpec(
            num_scalar_prefetch=1,
            grid=(1,),
            in_specs=[flat] * len(given) + [block(0), block(1)],
            out_specs=[pl.BlockSpec(a.shape, lambda i, index: (0, 0)) for a in shapes],
        ),
        out_shape=shapes,
        compiler_params=pltpu.CompilerParams(vmem_limit_bytes=16 << 20),
        cost_estimate=cost(2),
    )(places, *given, array, array)


class RingScatter:
    def __init__(self, array, d, n):
        self.array, self.n, self.k = array, n, 0
        self.ahead, self.back = ring_perms(n)
        self.place = ring_place(d, n)
        self.up, self.down = n // 2, n - n // 2 - 1
        self.f, self.b = ring_kernel(pick_kernel, array, self.at(self.up, -self.down), (), 2)

    def at(self, p, q):
        return ring_member(self.place + jnp.array([p, q], jnp.int32), self.n).astype(jnp.int32)

    def step(self, first=None):
        self.k += 1
        k = self.k
        if k > self.up:
            return
        if first is not None:
            self.f, self.b = after(first, self.f, self.b)
        self.f = lax.ppermute(self.f, "dp", self.ahead)
        if k <= self.down:
            self.b = lax.ppermute(self.b, "dp", self.back)
        at = self.at(self.up - k, k - self.down)
        if k < self.down:
            self.f, self.b = ring_kernel(add_kernel, self.array, at, (self.f, self.b), 2)
        elif k < self.up:
            (self.f,) = ring_kernel(add_one_kernel, self.array, at, (self.f,), 1)

    def finish(self, kernel=close_kernel, outs=None):
        while self.k < self.up:
            self.step()
        return ring_kernel(kernel, self.array, self.at(0, 0), (self.f, self.b), outs or [self.array.shape[1:]])


def sum_kernel(*refs):
    total = refs[0][...].astype(F32)
    for ref in refs[1:-1]:
        total = total + ref[...].astype(F32)
    refs[-1][...] = total.astype(refs[-1].dtype)


def add_up(kind, *arrays):
    rows, cols = arrays[0].shape
    specs = [
        pl.BlockSpec((rows // 2, cols), lambda i: (i, 0)) if a.shape[0] == rows else whole(*a.shape) for a in arrays
    ]
    return pl.pallas_call(
        sum_kernel,
        grid=(2,),
        in_specs=specs,
        out_specs=specs[0],
        out_shape=shape(rows, cols, kind=kind),
        compiler_params=params(),
        cost_estimate=cost(3),
    )(*arrays)


def compress_kernel(h_ref, memory_ref, compressed_ref, w_ref, bias_ref, out_ref, weight):
    n_dp, _, rows, width = w_ref.shape

    @pl.when(pl.program_id(0) == 0)
    def _():
        for r in range(RATE):
            for k in range(n_dp):
                weight[r, k * rows:(k + 1) * rows] = w_ref[k, r]

    row = lax.broadcasted_iota(jnp.int32, (176, SEG), 0)
    col = lax.broadcasted_iota(jnp.int32, (176, SEG), 1)
    total = jnp.zeros((176, width), F32)
    for r in range(RATE):
        pick = jnp.where((col == RATE * row + r) & (row < CC), 1.0, 0.0).astype(BF)
        taken = nn(pick, memory_ref[0]).astype(BF)
        total = total + nn(taken, weight[r])
    made = (total + bias_ref[...].astype(F32)).astype(BF)
    to = lax.broadcasted_iota(jnp.int32, (SEG, SEG), 0)
    of = lax.broadcasted_iota(jnp.int32, (SEG, SEG), 1)
    keep = jnp.where(of == to + CC, 1.0, 0.0).astype(BF)
    to = lax.broadcasted_iota(jnp.int32, (SEG, 176), 0)
    of = lax.broadcasted_iota(jnp.int32, (SEG, 176), 1)
    put = jnp.where((of == to - (CM - CC)) & (of < CC), 1.0, 0.0).astype(BF)
    out_ref[0] = (nn(keep, compressed_ref[0]) + nn(put, made)).astype(BF)


def compress(h, memory, compressed, w, bias):
    seqs, width = memory.shape[0], w.shape[3]
    return pl.pallas_call(
        compress_kernel,
        grid_spec=pltpu.PrefetchScalarGridSpec(
            num_scalar_prefetch=1,
            grid=(seqs,),
            in_specs=[
                pl.BlockSpec((1, SEG, D), lambda s, h: (s, 0, 0)),
                pl.BlockSpec((1, CM, width), lambda s, h: (s, 0, h[0])),
                whole(*w.shape),
                whole(1, width),
            ],
            out_specs=pl.BlockSpec((1, CM, width), lambda s, h: (s, 0, 0)),
            scratch_shapes=[pltpu.VMEM((RATE, D, width), BF)],
        ),
        out_shape=shape(seqs, CM, width),
        compiler_params=params(),
        cost_estimate=cost(8),
    )(h, memory, compressed, w, bias.reshape(1, -1))


def per_device(
    inputs,
    memory,
    compressed,
    slot_valid,
    slot_age,
    w_query,
    w_key,
    w_value,
    content_bias,
    w_out,
    ln_gain,
    ln_bias,
    w_up,
    up_bias,
    w_down,
    down_bias,
    w_comp,
    comp_bias,
    cotangent,
):
    n_dp = lax.axis_size("dp")
    d = lax.axis_index("dp")
    h = lax.axis_index("head")
    h1 = h.reshape(1)
    ids = jnp.stack([h, h ^ 2]).astype(jnp.int32)
    seqs = memory.shape[0]
    rows = w_key.shape[0]
    out_rows = w_out.shape[0]
    share, up_share = content_bias.shape[0], up_bias.shape[0]
    values = 4 * share + up_share
    sources = ring_sources(d, n_dp)
    pick = lambda a, n, axis: lax.dynamic_index_in_dim(a, n, axis, keepdims=False)

    ring = RingGather(
        pack(w_key, w_value, w_query, w_out, (content_bias, ln_gain, ln_bias, down_bias, up_bias)), n_dp)
    i = jnp.arange(SEG, dtype=jnp.int32)[None, :]
    j = jnp.arange(2 * SEG, dtype=jnp.int32)[:, None]
    gap = i + SEG - j
    near = jnp.where(gap >= 0, jnp.log1p(jnp.maximum(gap, 0).astype(F32)), FAR)

    def far_of(s):
        age, valid = pick(slot_age, s, 0)[:, None], pick(slot_valid, s, 0)[:, None]
        return jnp.where(valid > 0, jnp.log1p(jnp.maximum(i + age, 0).astype(F32)), FAR)

    far = [far_of(h), far_of(h ^ 2)]
    heads = jnp.concatenate([2 * h + jnp.arange(2), 2 * (h ^ 1) + jnp.arange(2)])
    slopes = 0.6 * jnp.power(0.7, heads.astype(F32))
    ffn_chunk = jnp.concatenate([w_up, w_down.T])

    inputs_x = x_swap(inputs)
    ring.step()
    ring.step(near)
    ring.step((far, slopes, ffn_chunk, sources))
    ring.step(inputs_x)
    cot_low = x_swap(after(inputs_x, cotangent[:SEG // 2]))
    chunks = ring.finish()
    pairs = [(chunk, c_swap(chunk)) for chunk in chunks]
    ffn = RingGather(ffn_chunk, n_dp)
    ffn.step((chunks[-1], chunks[-2]))

    def first_moves(index, ins, outs):
        for k in range(n_dp):
            at = pl.multiple_of(index[k] * rows, rows)
            for p in range(2):
                chunk = ins[2 * k + p]
                yield chunk.at[pl.ds(0, rows), pl.ds(0, 6 * HD)], outs[p].at[pl.ds(at, rows)]
                yield chunk.at[pl.ds(rows, 16), pl.ds(0, 2 * HD)], outs[2].at[p, index[k]]
            yield ins[2 * k].at[pl.ds(0, rows), pl.ds(6 * HD, 2 * HD)], outs[3].at[index[k]]

    w_own, w_par, small, wo = copies(
        first_moves, [(D, 6 * HD), (D, 6 * HD), (2, n_dp, 16, 2 * HD), (n_dp, rows, 2 * HD)], sources,
        *[chunk for pair in pairs for chunk in pair])
    small_x = x_swap(small)
    cot_high = x_swap(after(small_x, cotangent[SEG // 2:]))
    small = jnp.stack([small[0, :, 0, :values], small[1, :, 0, :values], small_x[0, :, 0, :values], small_x[1, :, 0, :values]])
    rank = jnp.arange(4) ^ h
    small = sum(jnp.where((rank == e)[None, :, None], small[e][:, None], 0) for e in range(4))
    small = small.reshape(4 * n_dp, values).astype(F32)
    wo = wo.reshape(n_dp, 4, out_rows, 2 * HD)
    wo_x = x_swap(wo)
    wo4 = (wo, c_swap(wo), wo_x, c_swap(wo_x))

    bias_all = small[:, :share].reshape(4, 2 * HD)
    lines = small[:, share:4 * share].reshape(4 * n_dp, 3, share).transpose(1, 0, 2).reshape(3, D)
    up_shift = small[:, 4 * share:].reshape(4, D)
    two = lambda a: jnp.concatenate([pick(a, h, 0), pick(a, h ^ 1, 0)]).reshape(1, -1)
    bias, up_shift = two(bias_all), two(up_shift)

    kv, q = project(h, compressed, memory, after(cot_low, inputs), w_own, w_par)
    ffn.step(kv)
    kv_x, q_x = project(h ^ 2, compressed, memory, after((kv, wo_x), inputs_x), w_own, w_par)
    bias = after((lines, up_shift), bias)
    mixed_x, lse_x = attend(0, slopes, q_x, bias, kv_x, near, far[1])
    ffn.step(mixed_x)
    sent = x_swap(mixed_x)
    mixed, lse = attend(0, slopes, after((mixed_x, cot_high), q), bias, kv, near, far[0])
    ffn.step(mixed)
    chunks = ffn.finish()

    ffn_par = [c_swap(chunk) for chunk in chunks]
    per = n_dp // 4

    def wo_moves(index, ins, outs):
        me = index[0]
        for e in range(4):
            for b in range(4):
                for p in range(4):
                    target = outs[0].at[me ^ b, :, me ^ e, :, pl.ds(p * 2 * HD, 2 * HD)]
                    yield ins[e].at[pl.ds(b * per, per), p], target

    (w_o,) = copies(wo_moves, [(4, per, 4, out_rows, D)], h1, *wo4)
    w_o = w_o.reshape(D, D)

    cot, cot_x = (cotangent[:SEG // 2], cotangent[SEG // 2:]), (cot_low, cot_high)
    residual, normed = attention_out(mixed, sent, w_o, inputs, lines)
    normed_x = x_swap(normed)
    hid, gb, up_cols, branch, gn = feed_forward(n_dp, sources, normed, cot, up_shift, chunks, ffn_par, F32)

    other = (c_swap(inputs), c_swap(inputs_x))

    def memory_moves(index, ins, outs):
        me = index[0]
        yield ins[0], outs[0].at[me]
        yield ins[1], outs[0].at[me ^ 2]
        yield ins[2], outs[0].at[me ^ 1]
        yield ins[3], outs[0].at[me ^ 3]

    (new_memory,) = copies(memory_moves, [(seqs, SEG, D)], h1, inputs, inputs_x, *other)
    comp_w = lax.all_gather(after((chunks[-1], normed), w_comp), "dp", axis=0).reshape(n_dp, RATE, rows, 2 * HD)
    new_compressed = compress(h1, memory, compressed, comp_w, comp_bias)

    hid_x, gb_x, up_cols_x, branch_x, gn_x = feed_forward(n_dp, sources, normed_x, cot_x, up_shift, chunks, ffn_par, BF)
    gn_x = x_swap(gn_x)
    acts = ((normed, normed_x), cot + cot_x, (gb, gb_x), (hid, hid_x))
    from_par = [c_swap(a) for a in ffn_grads(1, n_dp, *acts)]
    from_par = after((new_compressed, new_memory), *from_par)
    ffn_sum = RingScatter(ffn_grads(0, n_dp, *acts, *from_par).reshape(n_dp, 2 * rows, D), d, n_dp)
    gn_x = after(ffn_sum.f, gn_x)
    ffn_sum.step()
    grad_residual, do, do_x, sums, mine, theirs = norm_back(
        n_dp, h1, residual, gn, gn_x, cotangent, lines, mixed, sent, w_o)
    do_x = x_swap(do_x)
    keep, send = out_half(h1, mine, c_swap(theirs))
    do = after((ffn_sum.f, ffn_sum.b), do)
    ffn_sum.step(do)
    got = x_swap(send)
    branch_x = x_swap(after((gn_x, got), branch_x))
    dq, dkv, q_cols = attend_back(0, slopes, q, bias, kv, near, far[0], mixed, lse, do)
    do_x = after((ffn_sum.f, ffn_sum.b), do_x)
    ffn_sum.step(dq)
    branch_x = after(dq, branch_x)
    output = add_up(BF, residual, branch, branch_x, lines[2:])
    term = token_term(dq, dkv, w_own, w_par, grad_residual)
    dq_x, dkv_x, q_cols_x = attend_back(0, slopes, q_x, bias, kv_x, near, far[1], mixed_x, lse_x, do_x)
    ffn_sum.step(dq_x)
    dq_x = after(got, dq_x)
    term_x = token_term(dq_x, dkv_x, w_own, w_par)
    term_sent = x_swap(term_x)
    grad_input = add_up(F32, term, term_sent)

    lane = jnp.arange(4)[:, None]

    def place(a):
        a = a.reshape(2, 1, -1)
        return jnp.where(lane == h, a[0], 0.0) + jnp.where(lane == h ^ 1, a[1], 0.0)

    tiny = jnp.concatenate([
        place(q_cols + q_cols_x).reshape(-1, share),
        sums[0].reshape(-1, share),
        sums[1].reshape(-1, share),
        sums[2].reshape(-1, share),
        place(up_cols + up_cols_x).reshape(-1, up_share),
    ], axis=1)
    tiny = tiny + x_swap(tiny)
    dq, dkv = after((tiny, term_x), dq, dkv)
    tiny = tiny + c_swap(tiny)
    tiny = jnp.pad(tiny.astype(BF).reshape(n_dp, 4, values), ((0, 0), (0, 12), (0, 2 * HD - values)))

    work = (ids, compressed, memory, inputs, inputs_x, (dkv, dkv_x), (dq, dq_x))
    from_par = weight_grads(1, n_dp, *work)
    from_par = after(ffn_sum.f, *from_par)
    from_par = [c_swap(a) for a in from_par]
    grad_up, grad_down = ffn_sum.finish(close_ffn_kernel, [(rows, D), (D, rows)])
    g_sum = RingScatter(weight_grads(0, n_dp, *work, *from_par, tiny, keep, got), d, n_dp)
    g_sum.step()
    g_sum.step((grad_up, grad_down))
    g_sum.step(term)
    g_sum.step(output)
    grad_key, grad_value, grad_query, grad_out, tiny = g_sum.finish(
        close_last_kernel, [(rows, 2 * HD), (rows, 2 * HD), (rows, 2 * HD), (out_rows, D), (16, 2 * HD)])
    tiny = pick(tiny, h, 0)

    return (
        output,
        grad_input,
        grad_query,
        grad_key,
        grad_value,
        tiny[:share],
        grad_out,
        tiny[share:2 * share],
        tiny[2 * share:3 * share],
        grad_up,
        tiny[4 * share:values],
        grad_down,
        tiny[3 * share:4 * share],
        new_memory,
        new_compressed,
    )


def solution(mesh):
    both = ("dp", "head")
    in_specs = (
        P(both, None),
        P("dp", None, None),
        P("dp", None, None),
        P("dp", None),
        P("dp", None),
        P("dp", "head"),
        P("dp", "head"),
        P("dp", "head"),
        P(both),
        P(both, None),
        P(both),
        P(both),
        P("dp", "head"),
        P(both),
        P("head", "dp"),
        P(both),
        P(None, "dp", "head"),
        P("head"),
        P(both, None),
    )
    out_specs = (
        P(both, None),
        P(both, None),
        P("dp", "head"),
        P("dp", "head"),
        P("dp", "head"),
        P(both),
        P(both, None),
        P(both),
        P(both),
        P("dp", "head"),
        P(both),
        P("head", "dp"),
        P(both),
        P("dp", None, None),
        P("dp", None, "head"),
    )
    return jax.shard_map(per_device, mesh=mesh, in_specs=in_specs, out_specs=out_specs, check_vma=False)
```

```python
import functools

import jax
import jax.numpy as jnp
from jax import lax
from jax.experimental import pallas as pl
from jax.experimental.pallas import tpu as pltpu
from jax.sharding import PartitionSpec as P

D = 1024
HD = 128
SEG = 512
CM = 512
RATE = 3
CC = 171
LN_EPS = 1e-05
LOG2E = 1.4426950408889634
SCALE2 = LOG2E * HD ** (-0.5)
FAR = 1e32
VMEM = 56 * 1024 * 1024
BF = jnp.bfloat16
F32 = jnp.float32


def nt(a, b):
    return lax.dot_general(a, b, (((1,), (1,)), ((), ())), preferred_element_type=F32)


def tn(a, b):
    return lax.dot_general(a, b, (((0,), (0,)), ((), ())), preferred_element_type=F32)


def nn(a, b):
    return jnp.dot(a, b, preferred_element_type=F32)


def x_swap(a):
    return lax.ppermute(a, "head", [(i, i ^ 2) for i in range(4)])


def c_swap(a):
    return lax.ppermute(a, "head", [(i, i ^ 1) for i in range(4)])


PIECES = ((0, SEG, 0), (SEG, 2 * SEG, 0), (2 * SEG, 5 * SEG // 2, 0), (5 * SEG // 2, 3 * SEG, SEG // 2))


def decay(near_ref, far_ref, low, high, first):
    return far_ref[low:high, first:] if high <= SEG else near_ref[low - SEG:high - SEG, first:]


def from_column(first, old, new, join):
    return join(old, new) if not first else jnp.concatenate([old[:, :first], join(old[:, first:], new)], axis=1)


def fwd_kernel(slope_ref, q_ref, bias_ref, kv_ref, near_ref, far_ref, mixed_ref, lse_ref):
    slope2 = slope_ref[pl.program_id(0)] * LOG2E
    q = (q_ref[0] + bias_ref[...]).astype(BF)
    parts = []
    top = None
    for low, high, first in PIECES:
        part = nt(kv_ref[0, low:high, :HD], q[first:]) * SCALE2 - slope2 * decay(near_ref, far_ref, low, high, first)
        peak = jnp.max(part, axis=0, keepdims=True)
        top = peak if top is None else from_column(first, top, peak, jnp.maximum)
        parts.append(part)
    total = jnp.zeros((1, SEG), F32)
    acc = jnp.zeros((HD, SEG), F32)
    for (low, high, first), part in zip(PIECES, parts):
        p = jnp.exp2(part - top[:, first:])
        total = from_column(first, total, jnp.sum(p, axis=0, keepdims=True), jnp.add)
        acc = from_column(first, acc, tn(kv_ref[0, low:high, HD:], p.astype(BF)), jnp.add)
    mixed_ref[...] = (acc / total).T.astype(BF)
    lse_ref[...] = (top + jnp.log2(total)).reshape(1, 1, SEG)


def bwd_kernel(slope_ref, q_ref, bias_ref, kv_ref, near_ref, far_ref, mixed_ref, lse_ref, do_ref, dq_ref, dkv_ref, sum_ref):
    slope2 = slope_ref[pl.program_id(0)] * LOG2E
    q = (q_ref[0] + bias_ref[...]).astype(BF)
    do = do_ref[...]
    lse = lse_ref[...].reshape(1, SEG)
    row_dot = jnp.sum((do.astype(F32) * mixed_ref[...].astype(F32)).T, axis=0, keepdims=True)
    inv_root = HD ** (-0.5)
    dq = jnp.zeros((HD, SEG), F32)
    for low, high, first in PIECES:
        k = kv_ref[0, low:high, :HD]
        v = kv_ref[0, low:high, HD:]
        table = decay(near_ref, far_ref, low, high, first)
        p = jnp.exp2(nt(k, q[first:]) * SCALE2 - slope2 * table - lse[:, first:])
        ds = (p * (nt(v, do[first:]) - row_dot[:, first:])).astype(BF)
        dkv_ref[low:high, HD:] = nn(p.astype(BF), do[first:]).astype(BF)
        dkv_ref[low:high, :HD] = (nn(ds, q[first:]) * inv_root).astype(BF)
        dq = from_column(first, dq, tn(k, ds), jnp.add)
    dq = (dq.T * inv_root).astype(BF)
    dq_ref[...] = dq
    sum_ref[...] = jnp.sum(dq.astype(F32), axis=0, keepdims=True)


def ring_order(n):
    up = list(range(0, n, 2))
    return up + [p + 1 for p in reversed(up)]


def ring_perms(n):
    order = ring_order(n)
    ahead = [(order[p], order[(p + 1) % n]) for p in range(n)]
    return ahead, [(b, a) for a, b in ahead]


def ring_place(d, n):
    return jnp.where(d % 2 == 0, d // 2, n - 1 - d // 2)


def ring_member(p, n):
    p = p % n
    return jnp.where(p < n // 2, 2 * p, 2 * (n - 1 - p) + 1)


def after(first, *then):
    out = lax.optimization_barrier((first,) + then)[1:]
    return out if len(then) > 1 else out[0]


class RingGather:
    def __init__(self, chunk, n):
        self.n, self.k = n, 0
        self.ahead, self.back = ring_perms(n)
        self.f = self.b = chunk
        self.chunks = [chunk]

    def step(self, first=None):
        self.k += 1
        if self.k > self.n // 2:
            return
        if first is not None:
            self.f, self.b = after(first, self.f, self.b)
        self.f = lax.ppermute(self.f, "dp", self.ahead)
        self.chunks.append(self.f)
        if self.k < self.n - self.n // 2:
            self.b = lax.ppermute(self.b, "dp", self.back)
            self.chunks.append(self.b)

    def finish(self):
        while self.k < self.n // 2:
            self.step()
        return self.chunks


def ring_sources(d, n):
    place = ring_place(d, n)
    steps = [0]
    for k in range(1, n // 2 + 1):
        steps.append(-k)
        if k < n - n // 2:
            steps.append(k)
    return ring_member(place + jnp.array(steps, jnp.int32), n).astype(jnp.int32)


ROWS = 3 * SEG
HALF = D // 2
smem_spec = pl.BlockSpec(memory_space=pltpu.SMEM)
vmem_spec = pl.BlockSpec(memory_space=pltpu.VMEM)
any_spec = pl.BlockSpec(memory_space=pl.ANY)


def params():
    return pltpu.CompilerParams(vmem_limit_bytes=VMEM)


def cost(us):
    return pl.CostEstimate(flops=int(us * 0.18e9), bytes_accessed=1, transcendentals=0)


def shape(*dims, kind=BF):
    return jax.ShapeDtypeStruct(dims, kind)


def whole(*dims):
    return pl.BlockSpec(dims, lambda *i: (0,) * len(dims))


def attend(t, slopes, q, bias, kv, near, far):
    return pl.pallas_call(
        fwd_kernel,
        grid=(4,),
        in_specs=[
            smem_spec,
            pl.BlockSpec((1, SEG, HD), lambda a: (t, 0, a)),
            pl.BlockSpec((1, HD), lambda a: (0, a)),
            pl.BlockSpec((1, ROWS, 2 * HD), lambda a: (t, 0, a)),
            whole(2 * SEG, SEG),
            whole(SEG, SEG),
        ],
        out_specs=[pl.BlockSpec((SEG, HD), lambda a: (0, a)), pl.BlockSpec((1, 1, SEG), lambda a: (a, 0, 0))],
        out_shape=[shape(SEG, HALF), shape(4, 1, SEG, kind=F32)],
        compiler_params=params(),
        cost_estimate=cost(9),
    )(slopes, q, bias, kv, near, far)


def attend_back(t, slopes, q, bias, kv, near, far, mixed, lse, do):
    column = pl.BlockSpec((SEG, HD), lambda a: (0, a))
    return pl.pallas_call(
        bwd_kernel,
        grid=(4,),
        in_specs=[
            smem_spec,
            pl.BlockSpec((1, SEG, HD), lambda a: (t, 0, a)),
            pl.BlockSpec((1, HD), lambda a: (0, a)),
            pl.BlockSpec((1, ROWS, 2 * HD), lambda a: (t, 0, a)),
            whole(2 * SEG, SEG),
            whole(SEG, SEG),
            column,
            pl.BlockSpec((1, 1, SEG), lambda a: (a, 0, 0)),
            column,
        ],
        out_specs=[column, pl.BlockSpec((ROWS, 2 * HD), lambda a: (0, a)), pl.BlockSpec((1, HD), lambda a: (0, a))],
        out_shape=[shape(SEG, HALF), shape(ROWS, D), shape(1, HALF, kind=F32)],
        compiler_params=params(),
        cost_estimate=cost(12),
    )(slopes, q, bias, kv, near, far, mixed, lse, do)


def pack_kernel(key_ref, value_ref, query_ref, out_ref, *rest):
    smalls, pack_ref = rest[:-1], rest[-1]
    rows = key_ref.shape[0]
    piece = out_ref.shape[0]
    pack_ref[:rows, :HD] = key_ref[:, :HD]
    pack_ref[:rows, HD:2 * HD] = value_ref[:, :HD]
    pack_ref[:rows, 2 * HD:3 * HD] = key_ref[:, HD:]
    pack_ref[:rows, 3 * HD:4 * HD] = value_ref[:, HD:]
    pack_ref[:rows, 4 * HD:6 * HD] = query_ref[...]
    for k in range(4):
        pack_ref[k * piece:(k + 1) * piece, 6 * HD:] = out_ref[:, k * 2 * HD:(k + 1) * 2 * HD]
    line = jnp.concatenate([a[...].astype(F32) for a in smalls], axis=1)
    line = jnp.concatenate([line, jnp.zeros((1, D - line.shape[1]), F32)], axis=1)
    row = lax.broadcasted_iota(jnp.int32, (16, D), 0)
    pack_ref[rows:] = jnp.where(row == 0, jnp.broadcast_to(line, (16, D)), 0.0).astype(BF)


def pack(w_key, w_value, w_query, w_out, smalls):
    return pl.pallas_call(
        pack_kernel,
        in_specs=[vmem_spec] * (4 + len(smalls)),
        out_specs=vmem_spec,
        out_shape=shape(w_key.shape[0] + 16, D),
        compiler_params=params(),
        cost_estimate=cost(1),
    )(w_key, w_value, w_query, w_out, *[a.reshape(1, -1) for a in smalls])


def project_kernel(id_ref, comp_ref, mem_ref, token_ref, w_own_ref, w_par_ref, kv_ref, q_ref, source, own, par, sems):
    n = pl.program_id(0)
    blocks = (comp_ref.at[id_ref[0]], mem_ref.at[id_ref[0]], token_ref)
    moves = [pltpu.make_async_copy(a, source.at[k], sems.at[k]) for k, a in enumerate(blocks)]
    own_move = pltpu.make_async_copy(w_own_ref, own, sems.at[3])
    par_move = pltpu.make_async_copy(w_par_ref, par, sems.at[4])

    @pl.when(n == 0)
    def _():
        own_move.start()
        moves[0].start()
        par_move.start()
        moves[1].start()
        moves[2].start()
        own_move.wait()

    for k in range(3):
        pl.when(n == k)(moves[k].wait)
    a = source[n]
    kv_ref[0, :, :HALF] = nn(a, own[:, :HALF]).astype(BF)
    pl.when(n == 0)(par_move.wait)
    kv_ref[0, :, HALF:] = nn(a, par[:, :HALF]).astype(BF)

    @pl.when(n == 2)
    def _():
        q_ref[0, :, :2 * HD] = nn(a, own[:, HALF:])
        q_ref[0, :, 2 * HD:] = nn(a, par[:, HALF:])


def project(seq, compressed, memory, tokens, w_own, w_par):
    return pl.pallas_call(
        project_kernel,
        grid_spec=pltpu.PrefetchScalarGridSpec(
            num_scalar_prefetch=1,
            grid=(3,),
            in_specs=[any_spec] * 5,
            out_specs=[
                pl.BlockSpec((1, SEG, D), lambda n, seq: (0, n, 0)),
                pl.BlockSpec((1, SEG, HALF), lambda n, seq: (0, 0, 0)),
            ],
            scratch_shapes=[
                pltpu.VMEM((3, SEG, D), BF),
                pltpu.VMEM((D, 6 * HD), BF),
                pltpu.VMEM((D, 6 * HD), BF),
                pltpu.SemaphoreType.DMA((5,)),
            ],
        ),
        out_shape=[shape(1, ROWS, D), shape(1, SEG, HALF, kind=F32)],
        compiler_params=params(),
        cost_estimate=cost(8),
    )(seq.reshape(1), compressed, memory, tokens, w_own, w_par)


def norm_kernel(mixed_ref, sent_ref, w_ref, in_ref, lines_ref, residual_ref, normed_ref):
    out = nn(mixed_ref[...], w_ref[:HALF]) + nn(sent_ref[...], w_ref[HALF:])
    residual = in_ref[...].astype(F32) + out
    residual_ref[...] = residual
    center = residual - jnp.mean(residual, axis=-1, keepdims=True)
    rstd = lax.rsqrt(jnp.mean(center * center, axis=-1, keepdims=True) + LN_EPS)
    normed_ref[...] = (center * rstd * lines_ref[0:1] + lines_ref[1:2]).astype(BF)


def attention_out(mixed, sent, w_o, inputs, lines):
    rows = SEG // 2
    half = pl.BlockSpec((rows, HALF), lambda i: (i, 0))
    full = pl.BlockSpec((rows, D), lambda i: (i, 0))
    return pl.pallas_call(
        norm_kernel,
        grid=(2,),
        in_specs=[half, half, whole(D, D), full, whole(3, D)],
        out_specs=[full, full],
        out_shape=[shape(SEG, D, kind=F32), shape(SEG, D)],
        compiler_params=params(),
        cost_estimate=cost(4),
    )(mixed, sent, w_o, inputs, lines)


def gelu_pair(before):
    c0, c1 = 0.7978845608028654, 0.044715
    sq = before * before
    t = jnp.tanh(c0 * before * (1.0 + c1 * sq))
    half = 0.5 * (1.0 + t)
    return before * half, half + 0.5 * before * (1.0 - t * t) * (c0 * (1.0 + 3.0 * c1 * sq))


def ffn_kernel(n_dp, index_ref, norm_ref, low_ref, high_ref, bias_ref, *refs):
    chunks = refs[:2 * n_dp]
    hid_ref, gb_ref, sum_ref, branch_ref, gn_ref, up_ref, down_ref, branch, gn, sems = refs[2 * n_dp:]
    i, tiles = pl.program_id(0), up_ref.shape[0]
    tile, rows = up_ref.shape[2], D // n_dp

    def moves(step):
        group, column = divmod(step, tiles // 2)
        for k in range(n_dp):
            source = chunks[group * n_dp + k]
            at = pl.ds(pl.multiple_of(index_ref[k] * rows, rows), rows)
            for m, target in enumerate((up_ref, down_ref)):
                yield pltpu.make_async_copy(
                    source.at[pl.ds(m * rows, rows), pl.ds(column * tile, tile)],
                    target.at[step, at],
                    sems.at[(step * n_dp + k) * 2 + m],
                )

    @pl.when(i == 0)
    def _():
        for step in range(tiles):
            for move in moves(step):
                move.start()

    for step in range(tiles):
        @pl.when(i == step)
        def _(step=step):
            for move in moves(step):
                move.wait()

    up, down = up_ref.at[i], down_ref.at[i]
    total = jnp.zeros((1, tile), F32)
    half = SEG // 2
    for c, cot_ref in enumerate((low_ref, high_ref)):
        part = slice(c * half, (c + 1) * half)
        act, slope = gelu_pair(nn(norm_ref[part], up[...]) + bias_ref[...])
        act = act.astype(BF)
        gb = (nn(cot_ref[...], down[...]) * slope).astype(BF)
        hid_ref[part] = act
        gb_ref[part] = gb
        total = total + jnp.sum(gb.astype(F32), axis=0, keepdims=True)
        branch[part] = jnp.where(i > 0, branch[part], 0.0) + nt(act, down[...])
        gn[part] = jnp.where(i > 0, gn[part], 0.0) + nt(gb, up[...])
    sum_ref[...] = total

    @pl.when(i == tiles - 1)
    def _():
        branch_ref[...] = branch[...].astype(branch_ref.dtype)
        gn_ref[...] = gn[...].astype(gn_ref.dtype)


def feed_forward(n_dp, sources, norm, cot, bias, own, par, kind, tile=1024):
    tiles = 2 * D // tile
    part = pl.BlockSpec((SEG, tile), lambda i, index: (0, i))
    line = pl.BlockSpec((1, tile), lambda i, index: (0, i))
    return pl.pallas_call(
        functools.partial(ffn_kernel, n_dp),
        grid_spec=pltpu.PrefetchScalarGridSpec(
            num_scalar_prefetch=1,
            grid=(tiles,),
            in_specs=[whole(SEG, D), whole(SEG // 2, D), whole(SEG // 2, D), line] + [any_spec] * (2 * n_dp),
            out_specs=[part, part, line, whole(SEG, D), whole(SEG, D)],
            scratch_shapes=[pltpu.VMEM((tiles, D, tile), BF)] * 2
            + [pltpu.VMEM((SEG, D), F32)] * 2
            + [pltpu.SemaphoreType.DMA((2 * tiles * n_dp,))],
        ),
        out_shape=[shape(SEG, 2 * D), shape(SEG, 2 * D), shape(1, 2 * D, kind=F32), shape(SEG, D, kind=kind), shape(SEG, D, kind=kind)],
        compiler_params=params(),
        cost_estimate=cost(16),
    )(sources, norm, *cot, bias, *own, *par)


def ffn_grad_kernel(tiles, n0, n1, c0_low, c0_high, c1_low, c1_high, gb0, gb1, hid0, hid1, *rest):
    parts, outs = (rest[:-1], rest[-1:]) if len(rest) > 2 * tiles else ((), rest)
    step = pl.program_id(0) * tiles + pl.program_id(1)
    for m in range(2):
        for i in range(tiles):
            k = m * tiles + i

            @pl.when(step == k)
            def _(m=m, k=k):
                if m == 0:
                    total = tn(n0[...], gb0[...]) + tn(n1[...], gb1[...])
                else:
                    half = SEG // 2
                    total = tn(c0_low[...], hid0[:half]) + tn(c0_high[...], hid0[half:])
                    total = total + tn(c1_low[...], hid1[:half]) + tn(c1_high[...], hid1[half:])
                if parts:
                    out = outs[0]
                    total = total.reshape(out.shape[0], out.shape[2], -1)
                    out[:, 0] = (total + parts[k][...].astype(F32)).astype(BF)
                else:
                    outs[k][...] = total.reshape(outs[k].shape).astype(BF)


def ffn_grads(g, n_dp, norms, cots, gbs, hids, *received, tile=512):
    n = D // tile
    rows = D // n_dp
    tokens = whole(SEG, D)
    early = pl.BlockSpec((SEG, tile), lambda m, i: (0, g * n + jnp.where(m == 0, i, n - 1)))
    late = pl.BlockSpec((SEG, tile), lambda m, i: (0, g * n + jnp.where(m == 0, 0, i)))
    part = whole(n_dp, rows, tile)
    if received:
        out_specs = pl.BlockSpec((n_dp, 1, rows, tile), lambda m, i: (0, m, 0, i))
        out_shape = shape(n_dp, 2, rows, D)
    else:
        out_specs, out_shape = [part] * (2 * n), [shape(n_dp, rows, tile)] * (2 * n)
    return pl.pallas_call(
        functools.partial(ffn_grad_kernel, n),
        grid=(2, n),
        in_specs=[tokens] * 2 + [whole(SEG // 2, D)] * 4 + [early] * 2 + [late] * 2 + [part] * len(received),
        out_specs=out_specs,
        out_shape=out_shape,
        compiler_params=params(),
        cost_estimate=cost(10),
    )(*norms, *cots, *gbs, *hids, *received)


def norm_back_kernel(h_ref, residual_ref, gn_ref, gnx_ref, cot_ref, lines_ref, mixed_ref, sent_ref, w_ref,
                     grad_ref, keep_ref, send_ref, sums_ref, mine_ref, theirs_ref, acc):
    i = pl.program_id(0)
    residual = residual_ref[...]
    center = residual - jnp.mean(residual, axis=-1, keepdims=True)
    rstd = lax.rsqrt(jnp.mean(center * center, axis=-1, keepdims=True) + LN_EPS)
    xhat = center * rstd
    gn = gn_ref[...] + gnx_ref[...].astype(F32)
    g = gn * lines_ref[0:1]
    cot = cot_ref[...].astype(F32)
    grad = cot + rstd * (g - jnp.mean(g, axis=-1, keepdims=True) - xhat * jnp.mean(g * xhat, axis=-1, keepdims=True))
    grad_ref[...] = grad
    low = grad.astype(BF)
    keep_ref[...] = nt(low, w_ref[:HALF]).astype(BF)
    send_ref[...] = nt(low, w_ref[HALF:]).astype(BF)
    total = lambda a: jnp.sum(a, axis=0, keepdims=True)
    sums = jnp.concatenate([total(gn * xhat), total(gn), total(cot)], axis=0)

    @pl.when(i == 0)
    def _():
        sums_ref[...] = sums
        acc[:HALF] = tn(mixed_ref[...], low)
        acc[HALF:] = tn(sent_ref[...], low)

    @pl.when(i > 0)
    def _():
        sums_ref[...] += sums
        acc[:HALF] += tn(mixed_ref[...], low)
        acc[HALF:] += tn(sent_ref[...], low)

    @pl.when(i == pl.num_programs(0) - 1)
    def _():
        per = mine_ref.shape[0] // 4
        first = h_ref[0] % 2 == 0
        for b in range(4):
            block = acc[b * 2 * HD:(b + 1) * 2 * HD].reshape(per, 2, 2, mine_ref.shape[2], D)
            at = pl.ds((h_ref[0] ^ b) * per, per)
            mine_ref[at] = jnp.where(first, block[:, :, 0], block[:, :, 1]).astype(BF)
            theirs_ref[at] = jnp.where(first, block[:, :, 1], block[:, :, 0]).astype(BF)


def out_half_kernel(h_ref, mine_ref, got_ref, keep_ref, send_ref):
    total = mine_ref[...].astype(F32) + got_ref[...].astype(F32)
    first = h_ref[0] // 2 == 0
    keep_ref[...] = jnp.where(first, total[:, 0], total[:, 1]).astype(BF)
    send_ref[...] = jnp.where(first, total[:, 1], total[:, 0]).astype(BF)


def out_half(h, mine, got):
    n_dp, _, rows, _ = mine.shape
    return pl.pallas_call(
        out_half_kernel,
        in_specs=[smem_spec, vmem_spec, vmem_spec],
        out_specs=[vmem_spec, vmem_spec],
        out_shape=[shape(n_dp, rows, D)] * 2,
        compiler_params=pltpu.CompilerParams(vmem_limit_bytes=16 << 20),
        cost_estimate=cost(1),
    )(h, mine, got)


def norm_back(n_dp, h, residual, gn, gnx, cot, gain, mixed, sent, w_o):
    rows = SEG // 2
    half = pl.BlockSpec((rows, HALF), lambda i: (i, 0))
    full = pl.BlockSpec((rows, D), lambda i: (i, 0))
    return pl.pallas_call(
        norm_back_kernel,
        grid=(2,),
        in_specs=[smem_spec, full, full, full, full, whole(3, D), half, half, whole(D, D)],
        out_specs=[full, half, half, whole(3, D)] + [whole(n_dp, 2, D // n_dp // 4, D)] * 2,
        out_shape=[shape(SEG, D, kind=F32), shape(SEG, HALF), shape(SEG, HALF), shape(3, D, kind=F32)] + [shape(n_dp, 2, D // n_dp // 4, D)] * 2,
        scratch_shapes=[pltpu.VMEM((D, D), F32)],
        compiler_params=params(),
        cost_estimate=cost(10),
    )(h, residual, gn, gnx, cot, gain, mixed, sent, w_o)


def term_kernel(dq_ref, dkv_ref, w_own_ref, w_par_ref, *rest):
    out = nt(dkv_ref[:, :HALF], w_own_ref[:, :HALF]) + nt(dkv_ref[:, HALF:], w_par_ref[:, :HALF])
    out = out + nt(dq_ref[:, :2 * HD], w_own_ref[:, HALF:]) + nt(dq_ref[:, 2 * HD:], w_par_ref[:, HALF:])
    if len(rest) > 1:
        out = out + rest[0][...]
    rest[-1][...] = out.astype(rest[-1].dtype)


def token_term(dq, dkv, w_own, w_par, *residual):
    rows = SEG // 2
    full = pl.BlockSpec((rows, D), lambda i: (i, 0))
    weight = whole(D, 3 * 2 * HD)
    return pl.pallas_call(
        term_kernel,
        grid=(2,),
        in_specs=[
            pl.BlockSpec((rows, HALF), lambda i: (i, 0)),
            pl.BlockSpec((rows, D), lambda i: (4 + i, 0)),
            weight,
            weight,
        ] + [full] * len(residual),
        out_specs=full,
        out_shape=shape(SEG, D, kind=F32 if residual else BF),
        compiler_params=params(),
        cost_estimate=cost(4),
    )(dq, dkv, w_own, w_par, *residual)


def weight_grad_kernel(g, ids_ref, comp_ref, mem_ref, own_ref, other_ref, dkv0, dkv1, dq0, dq1, *rest):
    step = pl.program_id(0)
    source, grads, query_grads, acc, sems = rest[-5:]
    parts, outs = (rest[:2], rest[5:6]) if len(rest) > 8 else ((), rest[:2])
    half = rest[0].shape[0]
    rows = D // (2 * half)
    blocks = []
    for t, (tokens, dkv) in enumerate(((own_ref, dkv0), (other_ref, dkv1))):
        for n, a in enumerate((comp_ref.at[ids_ref[t]], mem_ref.at[ids_ref[t]], tokens)):
            blocks.append((a, dkv.at[pl.ds(n * SEG, SEG), pl.ds(g * HALF, HALF)]))
    moves = [
        (pltpu.make_async_copy(a, source.at[pl.ds(k * SEG, SEG)], sems.at[2 * k]),
         pltpu.make_async_copy(b, grads.at[pl.ds(k * SEG, SEG)], sems.at[2 * k + 1]))
        for k, (a, b) in enumerate(blocks)
    ]
    extra = [
        pltpu.make_async_copy(a.at[:, pl.ds(g * 2 * HD, 2 * HD)], query_grads.at[k], sems.at[12 + k])
        for k, a in enumerate((dq0, dq1))
    ]

    @pl.when(step == 0)
    def _():
        for pair in moves:
            pair[0].start()
            pair[1].start()
        extra[0].start()
        extra[1].start()

    spans = ((0, 1), (1, 3), (3, 6))
    for k, (low, high) in enumerate(spans):
        @pl.when(step == k)
        def _(k=k, low=low, high=high):
            for pair in moves[low:high]:
                pair[0].wait()
                pair[1].wait()
            span = slice(low * SEG, high * SEG)
            if k == 0:
                acc[:, :HALF] = tn(source[span], grads[span])
            else:
                acc[:, :HALF] += tn(source[span], grads[span])
            if k == 1:
                extra[0].wait()
                acc[:, HALF:] = tn(source[2 * SEG:3 * SEG], query_grads[0])
            if k < 2:
                return
            extra[1].wait()
            acc[:, HALF:] += tn(source[5 * SEG:], query_grads[1])
            total = acc[...].reshape(2 * half, rows, 6 * HD)
            for p in range(2):
                block = slice(p * half, (p + 1) * half)
                if parts:
                    outs[0][block, :rows] = (total[block] + parts[p][...].astype(F32)).astype(BF)
                else:
                    outs[p][...] = total[block].astype(BF)
            if parts:
                tiny, mine, got = rest[2:5]
                out_rows = mine.shape[1]
                other = (mine[...].astype(F32) + got[...].astype(F32)).astype(BF)
                low = rows + (outs[0].shape[1] - rows) // 2
                outs[0][:, rows:] = jnp.zeros((2 * half, outs[0].shape[1] - rows, 6 * HD), BF)
                outs[0][:, rows:rows + out_rows] = other[:, :, :6 * HD]
                outs[0][:, low:low + out_rows, :2 * HD] = other[:, :, 6 * HD:]
                outs[0][:, low:low + 16, 2 * HD:4 * HD] = tiny[...]


def weight_grads(g, n_dp, ids, compressed, memory, own, other, dkvs, dqs, *received):
    rows = D // n_dp
    if received:
        extra = 2 * max(16, received[-1].shape[1])
        out_specs, out_shape = whole(n_dp, rows + extra, 6 * HD), shape(n_dp, rows + extra, 6 * HD)
    else:
        out_specs, out_shape = [whole(n_dp // 2, rows, 6 * HD)] * 2, [shape(n_dp // 2, rows, 6 * HD)] * 2
    return pl.pallas_call(
        functools.partial(weight_grad_kernel, g),
        grid_spec=pltpu.PrefetchScalarGridSpec(
            num_scalar_prefetch=1,
            grid=(3,),
            in_specs=[any_spec] * 8 + [whole(*a.shape) for a in received],
            out_specs=out_specs,
            scratch_shapes=[
                pltpu.VMEM((6 * SEG, D), BF),
                pltpu.VMEM((6 * SEG, HALF), BF),
                pltpu.VMEM((2, SEG, 2 * HD), BF),
                pltpu.VMEM((D, 6 * HD), F32),
                pltpu.SemaphoreType.DMA((14,)),
            ],
        ),
        out_shape=out_shape,
        compiler_params=params(),
        cost_estimate=cost(10),
    )(ids, compressed, memory, own, other, *dkvs, *dqs, *received)


def copies(moves, out_shapes, index, *arrays):
    count = len(arrays)

    def kernel(index_ref, *refs):
        ins, outs, sems = refs[:count], refs[count:-1], refs[-1]
        started = []
        for n, (source, target) in enumerate(moves(index_ref, ins, outs)):
            copy = pltpu.make_async_copy(source, target, sems.at[n])
            copy.start()
            started.append(copy)
        for copy in started:
            copy.wait()

    return pl.pallas_call(
        kernel,
        in_specs=[smem_spec] + [any_spec] * count,
        out_specs=[vmem_spec] * len(out_shapes),
        out_shape=[shape(*dims) for dims in out_shapes],
        scratch_shapes=[pltpu.SemaphoreType.DMA((192,))],
        compiler_params=pltpu.CompilerParams(vmem_limit_bytes=16 << 20),
        cost_estimate=cost(0),
    )(index, *arrays)


def assemble(chunks, sources, parts):
    n, cols = len(chunks), chunks[0].shape[1]

    def moves(index, ins, outs):
        for k in range(n):
            row = 0
            for out, rows in zip(outs, parts):
                yield ins[k].at[pl.ds(row, rows)], out.at[pl.ds(pl.multiple_of(index[k] * rows, rows), rows)]
                row += rows

    return copies(moves, [(n * rows, cols) for rows in parts], sources, *chunks)


def pick_kernel(index_ref, ahead_ref, back_ref, f_ref, b_ref):
    f_ref[...] = ahead_ref[0]
    b_ref[...] = back_ref[0]


def add_kernel(index_ref, f_in, b_in, ahead_ref, back_ref, f_ref, b_ref):
    f_ref[...] = (f_in[...].astype(F32) + ahead_ref[0].astype(F32)).astype(BF)
    b_ref[...] = (b_in[...].astype(F32) + back_ref[0].astype(F32)).astype(BF)


def add_one_kernel(index_ref, f_in, ahead_ref, back_ref, f_ref):
    f_ref[...] = (f_in[...].astype(F32) + ahead_ref[0].astype(F32)).astype(BF)


def close_kernel(index_ref, f_in, b_in, own_ref, _, out_ref):
    out_ref[...] = f_in[...].astype(F32) + b_in[...].astype(F32) + own_ref[0].astype(F32)


def close_ffn_kernel(index_ref, f_in, b_in, own_ref, _, up_ref, down_ref):
    total = f_in[...].astype(F32) + b_in[...].astype(F32) + own_ref[0].astype(F32)
    rows = up_ref.shape[0]
    up_ref[...] = total[:rows]
    down_ref[...] = total[rows:].T


def close_last_kernel(index_ref, f_in, b_in, own_ref, _, key_ref, value_ref, query_ref, out_ref, small_ref):
    total = f_in[...].astype(F32) + b_in[...].astype(F32) + own_ref[0].astype(F32)
    rows, out_rows = key_ref.shape[0], out_ref.shape[0]
    low = rows + (total.shape[0] - rows) // 2
    key_ref[:, :HD] = total[:rows, :HD]
    value_ref[:, :HD] = total[:rows, HD:2 * HD]
    key_ref[:, HD:] = total[:rows, 2 * HD:3 * HD]
    value_ref[:, HD:] = total[:rows, 3 * HD:4 * HD]
    query_ref[...] = total[:rows, 4 * HD:]
    out_ref[:, :6 * HD] = total[rows:rows + out_rows]
    out_ref[:, 6 * HD:] = total[low:low + out_rows, :2 * HD]
    small_ref[...] = total[low:low + 16, 2 * HD:4 * HD]


def ring_kernel(kernel, array, places, given, outs):
    _, rows, cols = array.shape
    shapes = [shape(rows, cols)] * outs if isinstance(outs, int) else [shape(*dims, kind=F32) for dims in outs]
    flat = pl.BlockSpec((rows, cols), lambda i, index: (0, 0))
    block = lambda k: pl.BlockSpec((1, rows, cols), lambda i, index: (index[k], 0, 0))
    return pl.pallas_call(
        kernel,
        grid_spec=pltpu.PrefetchScalarGridSpec(
            num_scalar_prefetch=1,
            grid=(1,),
            in_specs=[flat] * len(given) + [block(0), block(1)],
            out_specs=[pl.BlockSpec(a.shape, lambda i, index: (0, 0)) for a in shapes],
        ),
        out_shape=shapes,
        compiler_params=pltpu.CompilerParams(vmem_limit_bytes=16 << 20),
        cost_estimate=cost(2),
    )(places, *given, array, array)


class RingScatter:
    def __init__(self, array, d, n):
        self.array, self.n, self.k = array, n, 0
        self.ahead, self.back = ring_perms(n)
        self.place = ring_place(d, n)
        self.up, self.down = n // 2, n - n // 2 - 1
        self.f, self.b = ring_kernel(pick_kernel, array, self.at(self.up, -self.down), (), 2)

    def at(self, p, q):
        return ring_member(self.place + jnp.array([p, q], jnp.int32), self.n).astype(jnp.int32)

    def step(self, first=None):
        self.k += 1
        k = self.k
        if k > self.up:
            return
        if first is not None:
            self.f, self.b = after(first, self.f, self.b)
        self.f = lax.ppermute(self.f, "dp", self.ahead)
        if k <= self.down:
            self.b = lax.ppermute(self.b, "dp", self.back)
        at = self.at(self.up - k, k - self.down)
        if k < self.down:
            self.f, self.b = ring_kernel(add_kernel, self.array, at, (self.f, self.b), 2)
        elif k < self.up:
            (self.f,) = ring_kernel(add_one_kernel, self.array, at, (self.f,), 1)

    def finish(self, kernel=close_kernel, outs=None):
        while self.k < self.up:
            self.step()
        return ring_kernel(kernel, self.array, self.at(0, 0), (self.f, self.b), outs or [self.array.shape[1:]])


def sum_kernel(*refs):
    total = refs[0][...].astype(F32)
    for ref in refs[1:-1]:
        total = total + ref[...].astype(F32)
    refs[-1][...] = total.astype(refs[-1].dtype)


def add_up(kind, *arrays):
    rows, cols = arrays[0].shape
    specs = [
        pl.BlockSpec((rows // 2, cols), lambda i: (i, 0)) if a.shape[0] == rows else whole(*a.shape) for a in arrays
    ]
    return pl.pallas_call(
        sum_kernel,
        grid=(2,),
        in_specs=specs,
        out_specs=specs[0],
        out_shape=shape(rows, cols, kind=kind),
        compiler_params=params(),
        cost_estimate=cost(3),
    )(*arrays)


def compress_kernel(h_ref, memory_ref, compressed_ref, w_ref, bias_ref, out_ref, weight):
    n_dp, _, rows, width = w_ref.shape

    @pl.when(pl.program_id(0) == 0)
    def _():
        for r in range(RATE):
            for k in range(n_dp):
                weight[r, k * rows:(k + 1) * rows] = w_ref[k, r]

    row = lax.broadcasted_iota(jnp.int32, (176, SEG), 0)
    col = lax.broadcasted_iota(jnp.int32, (176, SEG), 1)
    total = jnp.zeros((176, width), F32)
    for r in range(RATE):
        pick = jnp.where((col == RATE * row + r) & (row < CC), 1.0, 0.0).astype(BF)
        taken = nn(pick, memory_ref[0]).astype(BF)
        total = total + nn(taken, weight[r])
    made = (total + bias_ref[...].astype(F32)).astype(BF)
    to = lax.broadcasted_iota(jnp.int32, (SEG, SEG), 0)
    of = lax.broadcasted_iota(jnp.int32, (SEG, SEG), 1)
    keep = jnp.where(of == to + CC, 1.0, 0.0).astype(BF)
    to = lax.broadcasted_iota(jnp.int32, (SEG, 176), 0)
    of = lax.broadcasted_iota(jnp.int32, (SEG, 176), 1)
    put = jnp.where((of == to - (CM - CC)) & (of < CC), 1.0, 0.0).astype(BF)
    out_ref[0] = (nn(keep, compressed_ref[0]) + nn(put, made)).astype(BF)


def compress(h, memory, compressed, w, bias):
    seqs, width = memory.shape[0], w.shape[3]
    return pl.pallas_call(
        compress_kernel,
        grid_spec=pltpu.PrefetchScalarGridSpec(
            num_scalar_prefetch=1,
            grid=(seqs,),
            in_specs=[
                pl.BlockSpec((1, SEG, D), lambda s, h: (s, 0, 0)),
                pl.BlockSpec((1, CM, width), lambda s, h: (s, 0, h[0])),
                whole(*w.shape),
                whole(1, width),
            ],
            out_specs=pl.BlockSpec((1, CM, width), lambda s, h: (s, 0, 0)),
            scratch_shapes=[pltpu.VMEM((RATE, D, width), BF)],
        ),
        out_shape=shape(seqs, CM, width),
        compiler_params=params(),
        cost_estimate=cost(8),
    )(h, memory, compressed, w, bias.reshape(1, -1))


def per_device(
    inputs,
    memory,
    compressed,
    slot_valid,
    slot_age,
    w_query,
    w_key,
    w_value,
    content_bias,
    w_out,
    ln_gain,
    ln_bias,
    w_up,
    up_bias,
    w_down,
    down_bias,
    w_comp,
    comp_bias,
    cotangent,
):
    n_dp = lax.axis_size("dp")
    d = lax.axis_index("dp")
    h = lax.axis_index("head")
    h1 = h.reshape(1)
    ids = jnp.stack([h, h ^ 2]).astype(jnp.int32)
    seqs = memory.shape[0]
    rows = w_key.shape[0]
    out_rows = w_out.shape[0]
    share, up_share = content_bias.shape[0], up_bias.shape[0]
    values = 4 * share + up_share
    sources = ring_sources(d, n_dp)
    pick = lambda a, n, axis: lax.dynamic_index_in_dim(a, n, axis, keepdims=False)

    ring = RingGather(
        pack(w_key, w_value, w_query, w_out, (content_bias, ln_gain, ln_bias, down_bias, up_bias)), n_dp)
    i = jnp.arange(SEG, dtype=jnp.int32)[None, :]
    j = jnp.arange(2 * SEG, dtype=jnp.int32)[:, None]
    gap = i + SEG - j
    near = jnp.where(gap >= 0, jnp.log1p(jnp.maximum(gap, 0).astype(F32)), FAR)

    def far_of(s):
        age, valid = pick(slot_age, s, 0)[:, None], pick(slot_valid, s, 0)[:, None]
        return jnp.where(valid > 0, jnp.log1p(jnp.maximum(i + age, 0).astype(F32)), FAR)

    far = [far_of(h), far_of(h ^ 2)]
    heads = jnp.concatenate([2 * h + jnp.arange(2), 2 * (h ^ 1) + jnp.arange(2)])
    slopes = 0.6 * jnp.power(0.7, heads.astype(F32))
    ffn_chunk = jnp.concatenate([w_up, w_down.T])

    inputs_x = x_swap(inputs)
    ring.step()
    ring.step(near)
    ring.step((far, slopes, ffn_chunk, sources))
    ring.step(inputs_x)
    cot_low = x_swap(after(inputs_x, cotangent[:SEG // 2]))
    chunks = ring.finish()
    pairs = [(chunk, c_swap(chunk)) for chunk in chunks]
    ffn = RingGather(ffn_chunk, n_dp)
    ffn.step((chunks[-1], chunks[-2]))

    def first_moves(index, ins, outs):
        for k in range(n_dp):
            at = pl.multiple_of(index[k] * rows, rows)
            for p in range(2):
                chunk = ins[2 * k + p]
                yield chunk.at[pl.ds(0, rows), pl.ds(0, 6 * HD)], outs[p].at[pl.ds(at, rows)]
                yield chunk.at[pl.ds(rows, 16), pl.ds(0, 2 * HD)], outs[2].at[p, index[k]]
            yield ins[2 * k].at[pl.ds(0, rows), pl.ds(6 * HD, 2 * HD)], outs[3].at[index[k]]

    w_own, w_par, small, wo = copies(
        first_moves, [(D, 6 * HD), (D, 6 * HD), (2, n_dp, 16, 2 * HD), (n_dp, rows, 2 * HD)], sources,
        *[chunk for pair in pairs for chunk in pair])
    small_x = x_swap(small)
    cot_high = x_swap(after(small_x, cotangent[SEG // 2:]))
    small = jnp.stack([small[0, :, 0, :values], small[1, :, 0, :values], small_x[0, :, 0, :values], small_x[1, :, 0, :values]])
    rank = jnp.arange(4) ^ h
    small = sum(jnp.where((rank == e)[None, :, None], small[e][:, None], 0) for e in range(4))
    small = small.reshape(4 * n_dp, values).astype(F32)
    wo = wo.reshape(n_dp, 4, out_rows, 2 * HD)
    wo_x = x_swap(wo)
    wo4 = (wo, c_swap(wo), wo_x, c_swap(wo_x))

    bias_all = small[:, :share].reshape(4, 2 * HD)
    lines = small[:, share:4 * share].reshape(4 * n_dp, 3, share).transpose(1, 0, 2).reshape(3, D)
    up_shift = small[:, 4 * share:].reshape(4, D)
    two = lambda a: jnp.concatenate([pick(a, h, 0), pick(a, h ^ 1, 0)]).reshape(1, -1)
    bias, up_shift = two(bias_all), two(up_shift)

    kv, q = project(h, compressed, memory, after(cot_low, inputs), w_own, w_par)
    ffn.step(kv)
    kv_x, q_x = project(h ^ 2, compressed, memory, after((kv, wo_x), inputs_x), w_own, w_par)
    bias = after((lines, up_shift), bias)
    mixed_x, lse_x = attend(0, slopes, q_x, bias, kv_x, near, far[1])
    ffn.step(mixed_x)
    sent = x_swap(mixed_x)
    mixed, lse = attend(0, slopes, after((mixed_x, cot_high), q), bias, kv, near, far[0])
    ffn.step(mixed)
    chunks = ffn.finish()

    ffn_par = [c_swap(chunk) for chunk in chunks]
    per = n_dp // 4

    def wo_moves(index, ins, outs):
        me = index[0]
        for e in range(4):
            for b in range(4):
                for p in range(4):
                    target = outs[0].at[me ^ b, :, me ^ e, :, pl.ds(p * 2 * HD, 2 * HD)]
                    yield ins[e].at[pl.ds(b * per, per), p], target

    (w_o,) = copies(wo_moves, [(4, per, 4, out_rows, D)], h1, *wo4)
    w_o = w_o.reshape(D, D)

    cot, cot_x = (cotangent[:SEG // 2], cotangent[SEG // 2:]), (cot_low, cot_high)
    residual, normed = attention_out(mixed, sent, w_o, inputs, lines)
    normed_x = x_swap(normed)
    hid, gb, up_cols, branch, gn = feed_forward(n_dp, sources, normed, cot, up_shift, chunks, ffn_par, F32)

    other = (c_swap(inputs), c_swap(inputs_x))

    def memory_moves(index, ins, outs):
        me = index[0]
        yield ins[0], outs[0].at[me]
        yield ins[1], outs[0].at[me ^ 2]
        yield ins[2], outs[0].at[me ^ 1]
        yield ins[3], outs[0].at[me ^ 3]

    (new_memory,) = copies(memory_moves, [(seqs, SEG, D)], h1, inputs, inputs_x, *other)
    comp_w = lax.all_gather(after((chunks[-1], normed), w_comp), "dp", axis=0).reshape(n_dp, RATE, rows, 2 * HD)
    new_compressed = compress(h1, memory, compressed, comp_w, comp_bias)

    hid_x, gb_x, up_cols_x, branch_x, gn_x = feed_forward(n_dp, sources, normed_x, cot_x, up_shift, chunks, ffn_par, BF)
    gn_x = x_swap(gn_x)
    acts = ((normed, normed_x), cot + cot_x, (gb, gb_x), (hid, hid_x))
    from_par = [c_swap(a) for a in ffn_grads(1, n_dp, *acts)]
    from_par = after((new_compressed, new_memory), *from_par)
    ffn_sum = RingScatter(ffn_grads(0, n_dp, *acts, *from_par).reshape(n_dp, 2 * rows, D), d, n_dp)
    gn_x = after(ffn_sum.f, gn_x)
    ffn_sum.step()
    grad_residual, do, do_x, sums, mine, theirs = norm_back(
        n_dp, h1, residual, gn, gn_x, cotangent, lines, mixed, sent, w_o)
    do_x = x_swap(do_x)
    keep, send = out_half(h1, mine, c_swap(theirs))
    do = after((ffn_sum.f, ffn_sum.b), do)
    ffn_sum.step(do)
    got = x_swap(send)
    branch_x = x_swap(after((gn_x, got), branch_x))
    dq, dkv, q_cols = attend_back(0, slopes, q, bias, kv, near, far[0], mixed, lse, do)
    do_x = after((ffn_sum.f, ffn_sum.b), do_x)
    ffn_sum.step(dq)
    branch_x = after(dq, branch_x)
    output = add_up(BF, residual, branch, branch_x, lines[2:])
    term = token_term(dq, dkv, w_own, w_par, grad_residual)
    dq_x, dkv_x, q_cols_x = attend_back(0, slopes, q_x, bias, kv_x, near, far[1], mixed_x, lse_x, do_x)
    ffn_sum.step(dq_x)
    dq_x = after(got, dq_x)
    term_x = token_term(dq_x, dkv_x, w_own, w_par)
    term_sent = x_swap(term_x)
    grad_input = add_up(F32, term, term_sent)

    lane = jnp.arange(4)[:, None]

    def place(a):
        a = a.reshape(2, 1, -1)
        return jnp.where(lane == h, a[0], 0.0) + jnp.where(lane == h ^ 1, a[1], 0.0)

    tiny = jnp.concatenate([
        place(q_cols + q_cols_x).reshape(-1, share),
        sums[0].reshape(-1, share),
        sums[1].reshape(-1, share),
        sums[2].reshape(-1, share),
        place(up_cols + up_cols_x).reshape(-1, up_share),
    ], axis=1)
    tiny = tiny + x_swap(tiny)
    dq, dkv = after((tiny, term_x), dq, dkv)
    tiny = tiny + c_swap(tiny)
    tiny = jnp.pad(tiny.astype(BF).reshape(n_dp, 4, values), ((0, 0), (0, 12), (0, 2 * HD - values)))

    work = (ids, compressed, memory, inputs, inputs_x, (dkv, dkv_x), (dq, dq_x))
    from_par = weight_grads(1, n_dp, *work)
    from_par = after(ffn_sum.f, *from_par)
    from_par = [c_swap(a) for a in from_par]
    grad_up, grad_down = ffn_sum.finish(close_ffn_kernel, [(rows, D), (D, rows)])
    g_sum = RingScatter(weight_grads(0, n_dp, *work, *from_par, tiny, keep, got), d, n_dp)
    g_sum.step()
    g_sum.step((grad_up, grad_down))
    g_sum.step(term)
    g_sum.step(output)
    grad_key, grad_value, grad_query, grad_out, tiny = g_sum.finish(
        close_last_kernel, [(rows, 2 * HD), (rows, 2 * HD), (rows, 2 * HD), (out_rows, D), (16, 2 * HD)])
    tiny = pick(tiny, h, 0)

    return (
        output,
        grad_input,
        grad_query,
        grad_key,
        grad_value,
        tiny[:share],
        grad_out,
        tiny[share:2 * share],
        tiny[2 * share:3 * share],
        grad_up,
        tiny[4 * share:values],
        grad_down,
        tiny[3 * share:4 * share],
        new_memory,
        new_compressed,
    )


def solution(mesh):
    both = ("dp", "head")
    in_specs = (
        P(both, None),
        P("dp", None, None),
        P("dp", None, None),
        P("dp", None),
        P("dp", None),
        P("dp", "head"),
        P("dp", "head"),
        P("dp", "head"),
        P(both),
        P(both, None),
        P(both),
        P(both),
        P("dp", "head"),
        P(both),
        P("head", "dp"),
        P(both),
        P(None, "dp", "head"),
        P("head"),
        P(both, None),
    )
    out_specs = (
        P(both, None),
        P(both, None),
        P("dp", "head"),
        P("dp", "head"),
        P("dp", "head"),
        P(both),
        P(both, None),
        P(both),
        P(both),
        P("dp", "head"),
        P(both),
        P("head", "dp"),
        P(both),
        P("dp", None, None),
        P("dp", None, "head"),
    )
    return jax.shard_map(per_device, mesh=mesh, in_specs=in_specs, out_specs=out_specs, check_vma=False)
```
